256 devices in a mesh: gx: 8 (over y_lo, x), gy: 8 (over z), gz: 4 (over y_hi, core).
Axes of the slice: x: 4, y: 4 (y_hi: 2, y_lo: 2; y = y_hi * 2 + y_lo), z: 8, core: 2. Of those that a mesh axis runs over, the one named last changes fastest.
Arguments:
- cells: int32 [524288], P(('gx', 'gy', 'gz')), may hold values from 0 to 63
- offsets: float32 [3, 524288], P(None, ('gx', 'gy', 'gz')), may hold values from 0.5 to 1.5
- velocity: float32 [3, 524288], P(None, ('gx', 'gy', 'gz')), may hold values from -6 to 6
- affine: float32 [9, 524288], P(None, ('gx', 'gy', 'gz')), may hold values from -6 to 6
- stress: float32 [9, 524288], P(None, ('gx', 'gy', 'gz')), may hold values from -6 to 6
- mass: float32 [524288], P(('gx', 'gy', 'gz')), may hold values from 0.3 to 3
- block_tile: int32 [4096], P(('gx', 'gy', 'gz')), may hold values from 0 to 127
- live_blocks: int32 [256], P(('gx', 'gy', 'gz')), may hold values from 2 to 16, as said below
- bucket_mask: int32 [16, 128, 1024], P('gz', 'gx', 'gy'), may hold values from 0 to 2
- friction_class: int32 [16, 128, 1024], P('gz', 'gx', 'gy'), may hold values from 0 to 3
- bucket_velocity: float32 [3], replicated, may hold values from -4 to 4
Outputs:
- new_velocity: float32 [3, 524288], P(None, ('gx', 'gy', 'gz'))
- new_affine: float32 [9, 524288], P(None, ('gx', 'gy', 'gz'))
- new_offsets: float32 [3, 524288], P(None, ('gx', 'gy', 'gz'))
The draws below stay inside these ranges and needn't reach their ends.
Inputs may be any that keep to these rules, and one draw needn't show every extreme that they name: `block_tile`: tile numbers count tiles of 4 x 4 x 4 nodes of one device's block, z slowest, y fastest: there are 1, 4 and 32 of them along z, x and y. cells[p] = 16 a + 4 b + c puts particle p's nearest node at (a, b, c) inside the tile of its block. Blocks of a device at positions live_blocks and beyond hold no particles; some device has all 16 blocks live.
All inputs are finite; a program needn't handle non-finite values.
Results may differ from the reference program's by a relative error of at most 0.00028.
Values sent between devices are 32-bit elements; how exact they have to be, the bound alone decides.
A program may use at most 64 MiB of HBM per device.

```python
import math
import jax
import jax.numpy as jnp
from jax import lax

CX = 16
CY = 128
CZ = 4
BLOCKS_DEV = 16
NX = 128
NY = 1024
NZ = 16
TILES_DEV = 128
BLOCKS = 4096
PARTICLES = 524288
N_GY = 8
N_GZ = 4
DEVICES = 256


def draw_live_blocks(key, part):
    key = jax.random.fold_in(key, 5)
    halvings = jax.random.randint(jax.random.fold_in(key, 1), (DEVICES,), 0, 4)
    counts = jnp.right_shift(jnp.full((DEVICES,), BLOCKS_DEV, jnp.int32), halvings.astype(jnp.int32))
    chosen = jax.random.randint(jax.random.fold_in(key, 2), (), 0, DEVICES)
    return jnp.where(jnp.arange(DEVICES, dtype=jnp.int32) == chosen, BLOCKS_DEV, counts).astype(jnp.int32)


def touch_ends(drawn, own_key, smallest, high):
    longest = drawn.shape.index(max(drawn.shape))
    spots = []
    for shift in (0, 1):
        where = [jax.random.randint(jax.random.fold_in(own_key, axis), (), 0, length) for axis, length in enumerate(drawn.shape)]
        where[longest] = (where[longest] + shift) % drawn.shape[longest]
        spots.append(tuple(where))
    return drawn.at[spots[0]].set(smallest).at[spots[1]].set(high)


def steps_of(own_key, extent, shards, smallest, largest):
    level = 1.0
    for position, blocks in shards:
        steps = jax.random.uniform(jax.random.fold_in(jax.random.fold_in(own_key, 6), position), (blocks,), jnp.float32, smallest / len(shards), largest / len(shards))
        level = level * jnp.repeat(jnp.exp(steps), extent[position] // blocks).reshape((-1,) + (1,) * (len(extent) - 1 - position))
    return level


def bell_draw(key, extent, deviation, most, cuts=(), held_as=jnp.bfloat16):
    entries = jax.random.normal(key, extent, jnp.float32) * deviation
    if len(cuts) > 0:
        entries = steps_of(key, extent, cuts, -0.22, 0.18) * entries
    return jnp.clip(entries, min=-most, max=most).astype(held_as)


def setup_inputs(seed: int = 0) -> dict:
    streams_of = jax.random.split(jax.random.key(seed), 12)
    cells = touch_ends(jax.random.randint(streams_of[0], (PARTICLES,), 0, 64), jax.random.fold_in(streams_of[0], 1), 0, 63).astype(jnp.int32)
    offsets = jnp.clip(0.5 + 1.0 * jax.random.uniform(streams_of[1], (3, PARTICLES), jnp.float32) ** steps_of(streams_of[1], (3, PARTICLES), ((1, 256),), -0.2, 0.2), 0.5, 1.5)
    velocity = bell_draw(streams_of[2], (3, PARTICLES), 1.0, 6.0, ((1, 256),), jnp.float32)
    affine = bell_draw(streams_of[3], (9, PARTICLES), 1.0, 6.0, ((1, 256),), jnp.float32)
    stress = bell_draw(streams_of[4], (9, PARTICLES), 1.0, 6.0, ((1, 256),), jnp.float32)
    mass = jnp.clip(jnp.exp(math.log(3.0) - 2.3025851 * jax.random.uniform(streams_of[5], (PARTICLES,), jnp.float32) ** steps_of(streams_of[5], (PARTICLES,), ((0, 256),), -0.2, 0.2)), 0.3, 3.0)
    block_tile = touch_ends(jax.random.randint(streams_of[6], (BLOCKS,), 0, TILES_DEV), jax.random.fold_in(streams_of[6], 1), 0, TILES_DEV - 1).astype(jnp.int32)
    live_blocks = draw_live_blocks(jax.random.fold_in(streams_of[11], 71), 0)
    bucket_mask = touch_ends(jax.random.randint(streams_of[8], (NZ, NX, NY), 0, 3), jax.random.fold_in(streams_of[8], 1), 0, 2).astype(jnp.int32)
    friction_class = touch_ends(jax.random.randint(streams_of[9], (NZ, NX, NY), 0, 4), jax.random.fold_in(streams_of[9], 1), 0, 3).astype(jnp.int32)
    bucket_velocity = bell_draw(streams_of[10], (3,), 1.0, 4.0, (), jnp.float32)
    return dict(cells=cells, offsets=offsets, velocity=velocity, affine=affine, stress=stress, mass=mass, block_tile=block_tile, live_blocks=live_blocks, bucket_mask=bucket_mask, friction_class=friction_class, bucket_velocity=bucket_velocity)


DT = 0.1
GRAVITY = -9.8
MASS_FLOOR = 0.5
SLIP_FLOOR = 0.1
FRICTION = (0.1, 0.4, 0.8, 1.2)

def spline_weights(frac):
    return (0.5 * (1.5 - frac) * (1.5 - frac), 0.75 - (frac - 1.0) * (frac - 1.0), 0.5 * (frac - 0.5) * (frac - 0.5))

def grid_update(grid_mass, grid_momentum, bucket_mask, friction_class, bucket_velocity):
    speed = grid_momentum / jnp.maximum(grid_mass, MASS_FLOOR)[None]
    speed = jnp.concatenate([speed[0:1] + DT * GRAVITY, speed[1:3]], axis=0)
    coeff = jnp.zeros(friction_class.shape, jnp.float32)
    for level in range(4):
        coeff = coeff + jnp.where(friction_class == level, FRICTION[level], 0.0)
    rel = speed - bucket_velocity.reshape((3,) + (1,) * (speed.ndim - 1))
    normal = jnp.minimum(rel[0], 0.0)
    slide = jnp.sqrt(rel[1] * rel[1] + rel[2] * rel[2])
    multiplier = jnp.maximum(0.0, 1.0 + coeff * normal / jnp.maximum(slide, SLIP_FLOOR))
    bvel = bucket_velocity.reshape((3,) + (1,) * (speed.ndim - 1))
    contact = bvel + jnp.stack([rel[0] - normal, multiplier * rel[1], multiplier * rel[2]])
    final_output = jnp.where((bucket_mask == 1)[None], contact, speed)
    return jnp.where((bucket_mask == 2)[None], jnp.broadcast_to(bvel, speed.shape), final_output)

def reference(cells, offsets, velocity, affine, stress, mass, block_tile, live_blocks, bucket_mask, friction_class, bucket_velocity):
    per_device = BLOCKS_DEV * 128
    total = cells.shape[0]
    ident = jnp.arange(total, dtype=jnp.int32)
    device = ident // per_device
    block_patch = block_tile[ident // 128]
    tiles_x = CX // 4
    tiles_y = CY // 4
    near_z = block_patch // (tiles_x * tiles_y) * 4 + cells // 16
    near_x = block_patch // tiles_y % tiles_x * 4 + cells // 4 % 4
    near_y = block_patch % tiles_y * 4 + cells % 4
    dev_z = device % N_GZ
    dev_y = device // N_GZ % N_GY
    dev_x = device // (N_GZ * N_GY)
    base_z = dev_z * CZ + near_z - 1
    lower_corner_x = dev_x * CX + near_x - 1
    base_y = dev_y * CY + near_y - 1
    alive = (ident % per_device // 128 < live_blocks[device]).astype(jnp.float32)
    weights = [spline_weights(offsets[d]) for d in range(3)]
    moving = mass * alive
    twist = ((mass[None, :] * affine - 4.0 * DT * stress) * alive[None, :]).reshape(3, 3, total)
    count = NZ * NX * NY
    grid_mass = jnp.zeros((count + 1,), jnp.float32)
    grid_momentum = jnp.zeros((3, count + 1), jnp.float32)
    stencil = [(a, b, c) for a in range(3) for b in range(3) for c in range(3)]

    def locate(a, b, c):
        node_z = base_z + a
        inside = (node_z >= 0) & (node_z < NZ)
        node_x = (lower_corner_x + b) % NX
        node_y = (base_y + c) % NY
        return jnp.where(inside, (node_z * NX + node_x) * NY + node_y, count).astype(jnp.int32)
    for a, b, c in stencil:
        weight = weights[0][a] * weights[1][b] * weights[2][c]
        delta = jnp.stack([a - offsets[0], b - offsets[1], c - offsets[2]])
        push = moving[None] * velocity + lax.optimization_barrier(jnp.sum(twist * delta[None], axis=1))
        index = locate(a, b, c)
        grid_mass = grid_mass.at[index].add(weight * moving)
        grid_momentum = grid_momentum.at[:, index].add(weight[None] * push)
    speed = grid_update(grid_mass[:count], grid_momentum[:, :count], bucket_mask.reshape(count), friction_class.reshape(count), bucket_velocity)
    speed = jnp.concatenate([speed, jnp.zeros((3, 1), jnp.float32)], axis=1)
    new_v = jnp.zeros((3, total), jnp.float32)
    bend = jnp.zeros((3, 3, total), jnp.float32)
    for a, b, c in stencil:
        weight = weights[0][a] * weights[1][b] * weights[2][c]
        delta = jnp.stack([a - offsets[0], b - offsets[1], c - offsets[2]])
        nodal = speed[:, locate(a, b, c)]
        new_v = new_v + weight[None] * nodal
        bend = bend + weight[None, None] * nodal[:, None] * delta[None]
    new_velocity = new_v * alive[None]
    new_affine = 4.0 * bend.reshape(9, total) * alive[None]
    new_offsets = (offsets + DT * new_v) * alive[None]
    return (new_velocity, new_affine, new_offsets)
```

```python
import functools

import jax
import jax.numpy as jnp
from jax import lax
from jax.experimental import pallas as pl
from jax.experimental.pallas import tpu as pltpu
from jax.sharding import PartitionSpec as P

DT = 0.1
GRAVITY = -9.8
MASS_FLOOR = 0.5
SLIP_FLOOR = 0.1
FRICTION = (0.1, 0.4, 0.8, 1.2)

BLOCKS = 16
UNROLL = 2
XP = 20
ROWS = 3 * XP * 8
NODES = 3 * XP
F32 = jnp.float32
BF16 = jnp.bfloat16
MESH = pl.DeviceIdType.MESH

FACES = [(dz, dx) for dz in (-1, 0, 1) for dx in (-1, 0, 1) if (dz, dx) != (0, 0)]
EDGES = [
    (dz, dx, dy)
    for dz in (-1, 0, 1)
    for dx in (-1, 0, 1)
    for dy in (-1, 0, 1)
    if (dz, dx, dy) != (0, 0, 0)
]


def spline(frac):
    weights = (
        0.5 * (1.5 - frac) * (1.5 - frac),
        0.75 - (frac - 1.0) * (frac - 1.0),
        0.5 * (frac - 0.5) * (frac - 0.5),
    )
    moments = tuple(w * (float(k) - frac) for k, w in enumerate(weights))
    return weights, moments


def pick(hits, values):
    out = jnp.where(hits[2], values[2], 0.0)
    out = jnp.where(hits[1], values[1], out)
    return jnp.where(hits[0], values[0], out)


def split(value):
    high = value.astype(BF16)
    return high, (value - high.astype(F32)).astype(BF16)


def along_z(cell, frac):
    low = lax.broadcasted_iota(jnp.int32, (8, 128), 0) & 1
    near = lax.shift_right_logical(cell, 4) - low
    weights, moments = spline(frac)
    plain, moment = [], []
    for pair in range(3):
        hits = [near == 2 * pair - k for k in range(3)]
        plain.append(pick(hits, weights))
        moment.append(pick(hits, moments))
    return plain, moment


def along_x(cell, frac):
    near = lax.shift_right_logical(cell, 2) & 3
    weights, moments = spline(frac)
    hits = [near == v for v in range(4)]
    plain, moment = [], []
    for i in range(6):
        outs = []
        for values in (weights, moments):
            out = jnp.zeros((8, 128), F32)
            for k in range(3):
                if 0 <= i - k < 4:
                    out = jnp.where(hits[i - k], values[k], out)
            outs.append(out)
        plain.append(outs[0])
        moment.append(outs[1])
    return plain, moment


def along_y(cell, frac, first):
    row = lax.broadcasted_iota(jnp.int32, (8, 128), 0)
    base = (cell & 3) + (first - 1)
    weights, moments = spline(frac)
    diff = base - row
    plain, moment = [], []
    for t in range(17):
        shifted, offset = diff, 8 * t
        if t == 0:
            shifted = jnp.where(row == 0, -999, diff)
        elif t == 15:
            shifted = jnp.where(row == 7, -999, diff)
        elif t == 16:
            node = jnp.where(row == 0, -1, jnp.where(row == 1, 0, jnp.where(row == 2, 127, 128)))
            shifted, offset = jnp.where(row < 4, base - node, -999), 0
        hits = [shifted == offset - k for k in range(3)]
        plain.append(pick(hits, weights))
        moment.append(pick(hits, moments))
    zero = jnp.zeros((8, 128), F32)
    plain.append(zero)
    moment.append(zero)
    return jnp.concatenate([jnp.concatenate(plain, 0), jnp.concatenate(moment, 0)], 1)


def by_channel(parts):
    row = lax.broadcasted_iota(jnp.int32, (8, 128), 0)
    out = jnp.where(row < 6, parts[2], parts[3])
    out = jnp.where(row < 4, parts[1], out)
    return jnp.where(row < 2, parts[0], out)


def product(left, right, dims):
    left_high, left_low = split(left)
    right_high, right_low = right
    dot = functools.partial(
        lax.dot_general, dimension_numbers=(dims, ((), ())), preferred_element_type=F32
    )
    return dot(left_high, right_high) + (dot(left_low, right_high) + dot(left_high, right_low))


def contact(mass, momentum, kind, friction, bvel):
    floor = jnp.maximum(mass, MASS_FLOOR)
    speed = [momentum[0] / floor + DT * GRAVITY, momentum[1] / floor, momentum[2] / floor]
    coeff = jnp.where(friction == 3.0, FRICTION[3], 0.0)
    for level in range(3):
        coeff = jnp.where(friction == float(level), FRICTION[level], coeff)
    rel = [speed[i] - bvel[i] for i in range(3)]
    normal = jnp.minimum(rel[0], 0.0)
    slide = jnp.sqrt(rel[1] * rel[1] + rel[2] * rel[2])
    factor = jnp.maximum(0.0, 1.0 + coeff * normal / jnp.maximum(slide, SLIP_FLOOR))
    hit = [bvel[0] + (rel[0] - normal), bvel[1] + factor * rel[1], bvel[2] + factor * rel[2]]
    return [
        jnp.where(kind == 2.0, bvel[i], jnp.where(kind == 1.0, hit[i], speed[i])) for i in range(3)
    ]


def kernel(
    tile_ref,
    live_ref,
    bvel_ref,
    cells_ref,
    offsets_ref,
    velocity_ref,
    affine_ref,
    stress_ref,
    mass_ref,
    mask_ref,
    friction_ref,
    out_velocity,
    out_affine,
    out_offsets,
    wy_high,
    wy_low,
    patch,
    patch_edge,
    grid,
    edge,
    sums,
    classes,
    planes,
    got_z,
    got_x,
    got_zx,
    got_sums,
    class_z,
    class_x,
    class_zx,
    send_sem,
    recv_sem,
):
    ix, iy, iz = lax.axis_index("gx"), lax.axis_index("gy"), lax.axis_index("gz")
    nx, ny, nz = lax.axis_size("gx"), lax.axis_size("gy"), lax.axis_size("gz")

    def device(dz, dx, dy):
        return {
            "gx": lax.rem(ix + dx + nx, nx),
            "gy": lax.rem(iy + dy + ny, ny),
            "gz": lax.rem(iz + dz + nz, nz),
        }

    barrier = pltpu.get_barrier_semaphore()
    for side in EDGES:
        pl.semaphore_signal(barrier, inc=1, device_id=device(*side), device_id_type=MESH)

    counter = iter(range(2 * len(FACES) + len(EDGES)))

    def sender(src, dst, side):
        slot = next(counter)
        return pltpu.make_async_remote_copy(
            src_ref=src,
            dst_ref=dst,
            send_sem=send_sem.at[slot],
            recv_sem=recv_sem.at[slot],
            device_id=device(*side),
            device_id_type=MESH,
        )

    planes[0] = mask_ref[...].astype(F32)
    planes[1] = friction_ref[...].astype(F32)
    classes[...] = jnp.zeros((2, 128, 128), F32)

    def class_row(z):
        return 64 * (z % 2) + XP * (z // 2)

    for kind in range(2):
        for z in range(4):
            classes[kind, pl.ds(class_row(z + 1) + 1, 16), :] = planes[kind, z]

    zero_patch = jnp.zeros((3, 2, 8, 128), F32)
    zero_lead = jnp.zeros((3, 4, 8, 128), F32)
    for ref in (patch, patch_edge):
        ref[BLOCKS, :, pl.ds(0, 4)] = zero_lead

    def particle(b):
        lanes = pl.ds(pl.multiple_of(b * 128, 128), 128)

        def row(ref, r):
            return jnp.broadcast_to(ref[pl.ds(r, 1), lanes], (8, 128))

        cell = jnp.broadcast_to(cells_ref[pl.ds(b, 1), :], (8, 128))
        frac = [row(offsets_ref, r) for r in range(3)]
        alive = jnp.where(b < live_ref[0], 1.0, 0.0)
        return lanes, row, cell, frac, alive

    def scatter(b):
        lanes, row, cell, frac, alive = particle(b)
        tile = tile_ref[b]
        right = split(along_y(cell, frac[2], (tile & 31) * 4))
        wy_high[b] = right[0]
        wy_low[b] = right[1]
        wz, wz_moment = along_z(cell, frac[0])
        wx, wx_moment = along_x(cell, frac[1])
        mass = jnp.broadcast_to(mass_ref[pl.ds(b, 1), :], (8, 128)) * alive
        push = by_channel([mass] + [mass * row(velocity_ref, i) for i in range(3)])
        zero = jnp.zeros((8, 128), F32)
        scale = 4.0 * DT * alive

        def twist(j):
            return mass * by_channel(
                [zero] + [row(affine_ref, 3 * i + j) for i in range(3)]
            ) - scale * by_channel([zero] + [row(stress_ref, 3 * i + j) for i in range(3)])

        twists = [twist(j) for j in range(3)]
        plain, moment = [], []
        for pair in range(3):
            lead = wz[pair] * push + wz_moment[pair] * twists[0]
            second = wz[pair] * twists[1]
            third = wz[pair] * twists[2]
            for i in range(6):
                plain.append(wx[i] * lead + wx_moment[i] * second)
                moment.append(wx[i] * third)
        left = jnp.concatenate(
            [jnp.concatenate(plain, 0), jnp.concatenate(moment, 0)], 1
        )
        pad = jnp.zeros((112, 256), BF16)
        right = [jnp.concatenate([part, pad], 0) for part in right]
        found = product(left, right, ((1,), (1,)))
        patch[b, :, pl.ds(0, 6)] = found[:, :128].reshape(3, 6, 8, 128)
        patch_edge[b, :, pl.ds(0, 6)] = found[:, 128:].reshape(3, 6, 8, 128)
        patch[b, :, pl.ds(6, 2)] = zero_patch
        patch_edge[b, :, pl.ds(6, 2)] = zero_patch

    def scatter_some(step, carry):
        for u in range(UNROLL):
            scatter(step * UNROLL + u)
        return carry

    lax.fori_loop(0, BLOCKS // UNROLL, scatter_some, 0)

    def collect(source, target):
        def one(q, carry):
            total = jnp.zeros((3, 4, 8, 128), F32)
            for b in range(BLOCKS):
                tx = lax.shift_right_logical(tile_ref[b], 5) & 3
                here, before = tx == q, tx == q - 1
                slot = jnp.where(here | before, b, BLOCKS)
                start = jnp.where(before, 4, 0)
                total = total + source[slot, :, pl.ds(start, 4)]
            target[:, pl.ds(4 * q, 4)] = total
            return carry

        lax.fori_loop(0, 5, one, 0)

    collect(patch_edge, edge)
    edge_rows = edge.reshape(ROWS, 128)
    gap = jnp.zeros((4, 128), F32)
    for c in range(4):
        halves = [edge_rows[pl.ds(2 * c + low, NODES, stride=8), :] for low in range(2)]
        flipped = jnp.concatenate([halves[0], gap, halves[1], gap], 0).T
        sums[pl.ds(4 * c, 4), :] = flipped[:4]
    for kind in range(2):
        flipped = classes[kind].T
        zero = jnp.zeros((1, 128), F32)
        sums[pl.ds(16 + 4 * kind, 4), :] = jnp.concatenate(
            [zero, flipped[0:1], flipped[127:128], zero], 0
        )

    pl.semaphore_wait(barrier, len(EDGES))

    edge_sends = {}
    for index, (dz, dx, dy) in enumerate(EDGES):
        edge_sends[-dz, -dx, -dy] = sender(sums, got_sums.at[index], (dz, dx, dy))
        edge_sends[-dz, -dx, -dy].start()
    received = {(-dz, -dx, -dy): index for index, (dz, dx, dy) in enumerate(EDGES)}

    class_sends = {}
    for dz, dx in FACES:
        zs = {-1: pl.ds(0, 1), 0: pl.ds(0, 4), 1: pl.ds(3, 1)}[dz]
        xs = {-1: pl.ds(0, 8), 0: pl.ds(0, 16), 1: pl.ds(8, 8)}[dx]
        if dx == 0:
            target = class_z.at[(dz + 1) // 2]
        elif dz == 0:
            target = class_x.at[(dx + 1) // 2]
        else:
            target = class_zx.at[dz + 1 + (dx + 1) // 2]
        class_sends[-dz, -dx] = sender(planes.at[:, zs, xs], target, (dz, dx, 0))
        class_sends[-dz, -dx].start()

    collect(patch, grid)
    grid_sends = {}
    for dz, dx in FACES:
        zs = {-1: pl.ds(0, 1), 0: pl.ds(0, 3), 1: pl.ds(2, 1)}[dz]
        xs = {-1: pl.ds(0, 2), 0: pl.ds(0, 18), 1: pl.ds(16, 2)}[dx]
        if dx == 0:
            target = got_z.at[(dz + 1) // 2]
        elif dz == 0:
            target = got_x.at[(dx + 1) // 2]
        else:
            target = got_zx.at[dz + 1 + (dx + 1) // 2]
        grid_sends[-dz, -dx] = sender(grid.at[zs, xs], target, (dz, dx, 0))
        grid_sends[-dz, -dx].start()

    inside = {-1: iz > 0, 0: None, 1: iz < nz - 1}
    bvel = [bvel_ref[i] for i in range(3)]

    lane = lax.broadcasted_iota(jnp.int32, (24, 128), 1)
    column = lax.broadcasted_iota(jnp.int32, (24, 128), 0) & 3
    node = lane & 63
    pair = jnp.where(node >= 2 * XP, 2, jnp.where(node >= XP, 1, 0))
    place = node - XP * pair
    total = sums[...]
    for dz in (-1, 0, 1):
        for dx in (-1, 0, 1):
            part = jnp.zeros((24, 128), F32)
            for dy in (-1, 0, 1):
                if (dz, dx, dy) == (0, 0, 0):
                    continue
                edge_sends[dz, dx, dy].wait_recv()
                came = got_sums[received[dz, dx, dy]]
                if dy == -1:
                    came = jnp.where(column < 2, pltpu.roll(came, 22, 0), 0.0)
                elif dy == 1:
                    came = jnp.where(column >= 2, pltpu.roll(came, 2, 0), 0.0)
                part = part + came
            shift = (16 * dx + 2 * XP * dz) % 128
            if shift:
                part = pltpu.roll(part, shift, 1)
            keep = node < NODES
            if dx == -1:
                keep = keep & (place < 2)
            elif dx == 1:
                keep = keep & (place >= 16) & (place < 18)
            if dz == -1:
                keep = keep & (pair == 0) & inside[-1]
            elif dz == 1:
                keep = keep & (pair == 2) & inside[1]
            total = total + jnp.where(keep, part, 0.0)
    new = contact(
        total[0:4],
        [total[4:8], total[8:12], total[12:16]],
        total[16:20],
        total[20:24],
        bvel,
    )
    depth = 2 * pair[:4] + lax.shift_right_logical(lane[:4], 6)
    outside = ((depth == 0) & (iz == 0)) | ((depth == 5) & (iz == nz - 1))
    tail = jnp.zeros((124, 128), F32)
    for i in range(3):
        rows = jnp.concatenate([jnp.where(outside, 0.0, new[i]), tail], 0).T
        for low in range(2):
            edge_rows[pl.ds(2 * i + 2 + low, NODES, stride=8), :] = rows[64 * low : 64 * low + NODES]

    for dz, dx in FACES:
        class_sends[dz, dx].wait_recv()
    for kind in range(2):
        for side, row, x in ((0, 7, 0), (1, 0, 17)):
            for z in range(4):
                classes[kind, pl.ds(class_row(z + 1) + x, 1), :] = class_x[
                    1 - side, kind, z, pl.ds(row, 1), :
                ]
        for side, z in ((0, 0), (1, 5)):
            classes[kind, pl.ds(class_row(z) + 1, 16), :] = class_z[1 - side, kind, 0]
            for other, row, x in ((0, 7, 0), (1, 0, 17)):
                classes[kind, pl.ds(class_row(z) + x, 1), :] = class_zx[
                    2 * (1 - side) + (1 - other), kind, 0, pl.ds(row, 1), :
                ]

    for dz, dx in FACES:
        grid_sends[dz, dx].wait_recv()
        grid_sends[-dz, -dx].wait_send()
    for dz, dx in FACES:
        zs = {-1: pl.ds(0, 1), 0: pl.ds(0, 3), 1: pl.ds(2, 1)}[dz]
        xs = {-1: pl.ds(0, 2), 0: pl.ds(0, 18), 1: pl.ds(16, 2)}[dx]
        if dx == 0:
            came = got_z[(1 - dz) // 2]
        elif dz == 0:
            came = got_x[(1 - dx) // 2]
        else:
            came = got_zx[1 - dz + (1 - dx) // 2]
        if dz:
            came = jnp.where(inside[dz], came, 0.0)
        grid[zs, xs] = grid[zs, xs] + came
    grid_rows = grid.reshape(ROWS, 128)
    number = lax.broadcasted_iota(jnp.int32, (NODES, 128), 0)
    for low in range(2):
        load = [grid_rows[pl.ds(2 * c + low, NODES, stride=8), :] for c in range(4)]
        new = contact(
            load[0],
            load[1:],
            classes[0, pl.ds(64 * low, NODES), :],
            classes[1, pl.ds(64 * low, NODES), :],
            bvel,
        )
        if low == 0:
            outside = (number < XP) & (iz == 0)
        else:
            outside = (number >= 2 * XP) & (iz == nz - 1)
        for i in range(3):
            grid_rows[pl.ds(2 * i + 2 + low, NODES, stride=8), :] = jnp.where(
                outside, 0.0, new[i]
            )

    def gather(b):
        lanes, row, cell, frac, alive = particle(b)
        first = (lax.shift_right_logical(tile_ref[b], 5) & 3) * 4
        left = jnp.concatenate(
            [ref[:, pl.ds(first, 6)].reshape(144, 128) for ref in (grid, edge)], 1
        )
        pad = jnp.zeros((112, 256), BF16)
        right = [jnp.concatenate([ref[b], pad], 0) for ref in (wy_high, wy_low)]
        found = product(left, right, ((1,), (0,)))
        plain = found[:, :128].reshape(3, 6, 8, 128)
        moment = found[:, 128:].reshape(3, 6, 8, 128)
        wz, wz_moment = along_z(cell, frac[0])
        wx, wx_moment = along_x(cell, frac[1])
        totals = [jnp.zeros((8, 128), F32) for _ in range(4)]
        for pair in range(3):
            sum_w = sum(wx[i] * plain[pair, i] for i in range(6))
            sum_x = sum(wx_moment[i] * plain[pair, i] for i in range(6))
            sum_y = sum(wx[i] * moment[pair, i] for i in range(6))
            totals[0] = totals[0] + wz[pair] * sum_w
            totals[1] = totals[1] + wz_moment[pair] * sum_w
            totals[2] = totals[2] + wz[pair] * sum_x
            totals[3] = totals[3] + wz[pair] * sum_y
        totals = [(t + pltpu.roll(t, 7, 0)) * alive for t in totals]
        for i in range(3):
            at = 2 * i + 2
            moved = totals[0][at : at + 1]
            out_velocity[pl.ds(i, 1), lanes] = moved
            out_offsets[pl.ds(i, 1), lanes] = frac[i][:1] * alive + DT * moved
            for j in range(3):
                out_affine[pl.ds(3 * i + j, 1), lanes] = 4.0 * totals[j + 1][at : at + 1]

    def gather_some(step, carry):
        for u in range(UNROLL):
            gather(step * UNROLL + u)
        return carry

    lax.fori_loop(0, BLOCKS // UNROLL, gather_some, 0)
    for send in list(edge_sends.values()) + list(class_sends.values()):
        send.wait_send()


def on_device(
    cells,
    offsets,
    velocity,
    affine,
    stress,
    mass,
    block_tile,
    live_blocks,
    bucket_mask,
    friction_class,
    bucket_velocity,
):
    smem = pl.BlockSpec(memory_space=pltpu.SMEM)
    vmem = pl.BlockSpec(memory_space=pltpu.VMEM)
    count = cells.shape[0]
    copies = 2 * len(FACES) + len(EDGES)
    return pl.pallas_call(
        kernel,
        out_shape=(
            jax.ShapeDtypeStruct((3, count), F32),
            jax.ShapeDtypeStruct((9, count), F32),
            jax.ShapeDtypeStruct((3, count), F32),
        ),
        in_specs=[smem] * 3 + [vmem] * 8,
        out_specs=(vmem,) * 3,
        scratch_shapes=[
            pltpu.VMEM((BLOCKS, 144, 256), BF16),
            pltpu.VMEM((BLOCKS, 144, 256), BF16),
            pltpu.VMEM((BLOCKS + 1, 3, 8, 8, 128), F32),
            pltpu.VMEM((BLOCKS + 1, 3, 8, 8, 128), F32),
            pltpu.VMEM((3, XP, 8, 128), F32),
            pltpu.VMEM((3, XP, 8, 128), F32),
            pltpu.VMEM((24, 128), F32),
            pltpu.VMEM((2, 128, 128), F32),
            pltpu.VMEM((2, 4, 16, 128), F32),
            pltpu.VMEM((2, 1, 18, 8, 128), F32),
            pltpu.VMEM((2, 3, 2, 8, 128), F32),
            pltpu.VMEM((4, 1, 2, 8, 128), F32),
            pltpu.VMEM((len(EDGES), 24, 128), F32),
            pltpu.VMEM((2, 2, 1, 16, 128), F32),
            pltpu.VMEM((2, 2, 4, 8, 128), F32),
            pltpu.VMEM((4, 2, 1, 8, 128), F32),
            pltpu.SemaphoreType.DMA((copies,)),
            pltpu.SemaphoreType.DMA((copies,)),
        ],
        compiler_params=pltpu.CompilerParams(
            collective_id=0, has_side_effects=True, vmem_limit_bytes=40 * 1024 * 1024
        ),
    )(
        block_tile,
        live_blocks,
        bucket_velocity,
        cells.reshape(BLOCKS, 128),
        offsets,
        velocity,
        affine,
        stress,
        mass.reshape(BLOCKS, 128),
        bucket_mask,
        friction_class,
    )


def solution(mesh):
    along = ("gx", "gy", "gz")
    return jax.shard_map(
        on_device,
        mesh=mesh,
        in_specs=(
            P(along),
            P(None, along),
            P(None, along),
            P(None, along),
            P(None, along),
            P(along),
            P(along),
            P(along),
            P("gz", "gx", "gy"),
            P("gz", "gx", "gy"),
            P(),
        ),
        out_specs=(P(None, along), P(None, along), P(None, along)),
        check_vma=False,
    )
```

```python
import functools

import jax
import jax.numpy as jnp
from jax import lax
from jax.experimental import pallas as pl
from jax.experimental.pallas import tpu as pltpu
from jax.sharding import PartitionSpec as P

DT = 0.1
GRAVITY = -9.8
MASS_FLOOR = 0.5
SLIP_FLOOR = 0.1
FRICTION = (0.1, 0.4, 0.8, 1.2)

BLOCKS = 16
UNROLL = 8
VMEM_SPREAD = 52 * 1024 * 1024
VMEM_COLLECT = 16 * 1024 * 1024
XP = 20
ROWS = 3 * XP * 8
NODES = 3 * XP
F32 = jnp.float32
BF16 = jnp.bfloat16
MESH = pl.DeviceIdType.MESH

FACES = [(dz, dx) for dz in (-1, 0, 1) for dx in (-1, 0, 1) if (dz, dx) != (0, 0)]
SLOT = {side: index for index, side in enumerate(FACES)}
SENDS = 3 * len(FACES) + 4
Z_PLANE = {-1: 0, 1: 3}
Z_PAIR = {-1: 0, 1: 2}


def spline(frac):
    weights = (
        0.5 * (1.5 - frac) * (1.5 - frac),
        0.75 - (frac - 1.0) * (frac - 1.0),
        0.5 * (frac - 0.5) * (frac - 0.5),
    )
    moments = tuple(w * (float(k) - frac) for k, w in enumerate(weights))
    return weights, moments


def pick(hits, values):
    out = jnp.where(hits[2], values[2], 0.0)
    out = jnp.where(hits[1], values[1], out)
    return jnp.where(hits[0], values[0], out)


def split(value):
    high = value.astype(BF16)
    return high, (value - high.astype(F32)).astype(BF16)


def along_z(cell, frac):
    low = lax.broadcasted_iota(jnp.int32, (8, 128), 0) & 1
    near = lax.shift_right_logical(cell, 4) - low
    weights, moments = spline(frac)
    plain, moment = [], []
    for pair in range(3):
        hits = [near == 2 * pair - k for k in range(3)]
        plain.append(pick(hits, weights))
        moment.append(pick(hits, moments))
    return plain, moment


def along_x(cell, frac):
    near = lax.shift_right_logical(cell, 2) & 3
    weights, moments = spline(frac)
    hits = [near == v for v in range(4)]
    plain, moment = [], []
    for i in range(6):
        outs = []
        for values in (weights, moments):
            out = jnp.zeros((8, 128), F32)
            for k in range(3):
                if 0 <= i - k < 4:
                    out = jnp.where(hits[i - k], values[k], out)
            outs.append(out)
        plain.append(outs[0])
        moment.append(outs[1])
    return plain, moment


def along_y(cell, frac, first):
    row = lax.broadcasted_iota(jnp.int32, (8, 128), 0)
    base = (cell & 3) + (first - 1)
    weights, moments = spline(frac)
    diff = base - row
    plain, moment = [], []
    for t in range(17):
        shifted, offset = diff, 8 * t
        if t == 0:
            shifted = jnp.where(row == 0, -999, diff)
        elif t == 15:
            shifted = jnp.where(row == 7, -999, diff)
        elif t == 16:
            node = jnp.where(row == 0, -1, jnp.where(row == 1, 0, jnp.where(row == 2, 127, 128)))
            shifted, offset = jnp.where(row < 4, base - node, -999), 0
        hits = [shifted == offset - k for k in range(3)]
        plain.append(pick(hits, weights))
        moment.append(pick(hits, moments))
    zero = jnp.zeros((8, 128), F32)
    plain.append(zero)
    moment.append(zero)
    return jnp.concatenate([jnp.concatenate(plain, 0), jnp.concatenate(moment, 0)], 1)


def by_channel(parts):
    row = lax.broadcasted_iota(jnp.int32, (8, 128), 0)
    out = jnp.where(row < 6, parts[2], parts[3])
    out = jnp.where(row < 4, parts[1], out)
    return jnp.where(row < 2, parts[0], out)


def product(left, right, dims):
    left_high, left_low = split(left)
    right_high, right_low = right
    dot = functools.partial(
        lax.dot_general, dimension_numbers=(dims, ((), ())), preferred_element_type=F32
    )
    return dot(left_high, right_high) + (dot(left_low, right_high) + dot(left_high, right_low))


def contact(mass, momentum, kind, friction, bvel):
    floor = jnp.maximum(mass, MASS_FLOOR)
    speed = [momentum[0] / floor + DT * GRAVITY, momentum[1] / floor, momentum[2] / floor]
    coeff = jnp.where(friction == 3.0, FRICTION[3], 0.0)
    for level in range(3):
        coeff = jnp.where(friction == float(level), FRICTION[level], coeff)
    rel = [speed[i] - bvel[i] for i in range(3)]
    normal = jnp.minimum(rel[0], 0.0)
    slide = jnp.sqrt(rel[1] * rel[1] + rel[2] * rel[2])
    factor = jnp.maximum(0.0, 1.0 + coeff * normal / jnp.maximum(slide, SLIP_FLOOR))
    hit = [bvel[0] + (rel[0] - normal), bvel[1] + factor * rel[1], bvel[2] + factor * rel[2]]
    return [
        jnp.where(kind == 2.0, bvel[i], jnp.where(kind == 1.0, hit[i], speed[i])) for i in range(3)
    ]


def particle(b, tile_ref, live_ref, cells_ref, offsets_ref):
    lanes = pl.ds(pl.multiple_of(b * 128, 128), 128)

    def row(ref, r):
        return jnp.broadcast_to(ref[pl.ds(r, 1), lanes], (8, 128))

    cell = jnp.broadcast_to(cells_ref[pl.ds(b, 1), :], (8, 128))
    frac = [row(offsets_ref, r) for r in range(3)]
    alive = jnp.where(b < live_ref[0], 1.0, 0.0)
    return lanes, row, cell, frac, alive


def spread(
    tile_hbm,
    live_hbm,
    bvel_hbm,
    cells_hbm,
    offsets_hbm,
    velocity_hbm,
    affine_hbm,
    stress_hbm,
    mass_hbm,
    mask_hbm,
    friction_hbm,
    tile_ref,
    live_ref,
    cells_ref,
    offsets_ref,
    wy_high,
    wy_low,
    grid,
    edge,
    bvel_ref,
    velocity_ref,
    affine_ref,
    stress_ref,
    mass_ref,
    mask_ref,
    friction_ref,
    patch,
    patch_edge,
    sums,
    folded,
    classes,
    planes,
    sides,
    ends,
    got_z,
    got_x,
    got_zx,
    got_y,
    got_folded,
    class_z,
    class_x,
    class_y,
    load_sem,
    send_sem,
    recv_sem,
):
    loads = [
        pltpu.make_async_copy(source, target, load_sem.at[index])
        for index, (source, target) in enumerate(
            (
                (cells_hbm, cells_ref),
                (offsets_hbm, offsets_ref),
                (tile_hbm, tile_ref),
                (live_hbm, live_ref),
                (mass_hbm, mass_ref),
                (velocity_hbm, velocity_ref),
                (affine_hbm, affine_ref),
                (stress_hbm, stress_ref),
                (mask_hbm, mask_ref),
                (friction_hbm, friction_ref),
                (bvel_hbm, bvel_ref),
            )
        )
    ]
    for load in loads:
        load.start()

    ix, iy, iz = lax.axis_index("gx"), lax.axis_index("gy"), lax.axis_index("gz")
    nx, ny, nz = lax.axis_size("gx"), lax.axis_size("gy"), lax.axis_size("gz")
    above, below = iz < nz - 1, iz > 0

    def device(dz, dx, dy):
        return {
            "gx": lax.rem(ix + dx + nx, nx),
            "gy": lax.rem(iy + dy + ny, ny),
            "gz": lax.rem(iz + dz + nz, nz),
        }

    def where_z(dz, action):
        if dz == 0:
            action()
        else:
            pl.when(above if dz == 1 else below)(action)

    barrier = pltpu.get_barrier_semaphore()

    def greet(dz, dx, dy):
        where_z(
            dz,
            lambda: pl.semaphore_signal(
                barrier, inc=1, device_id=device(dz, dx, dy), device_id_type=MESH
            ),
        )

    for dz, dx in FACES:
        greet(dz, dx, 0)
    for dy in (-1, 1):
        greet(0, 0, dy)

    counter = iter(range(SENDS))

    def sender(src, dst, dz, dx, dy):
        slot = next(counter)
        return pltpu.make_async_remote_copy(
            src_ref=src,
            dst_ref=dst,
            send_sem=send_sem.at[slot],
            recv_sem=recv_sem.at[slot],
            device_id=device(dz, dx, dy),
            device_id_type=MESH,
        )

    class_sends, grid_sends, edge_sends = {}, {}, {}
    for dz, dx in FACES:
        came = (-dz, -dx)
        if dx == 0:
            class_sends[came] = sender(
                planes.at[:, Z_PLANE[dz]], class_z.at[(1 + dz) // 2], dz, dx, 0
            )
        else:
            class_sends[came] = sender(
                sides.at[(1 + dx) // 2], class_x.at[SLOT[dz, dx]], dz, dx, 0
            )
        if dx == 0:
            grid_sends[came] = sender(
                grid.at[Z_PAIR[dz], pl.ds(0, 18)], got_z.at[(1 + dz) // 2], dz, dx, 0
            )
        elif dz == 0:
            grid_sends[came] = sender(
                grid.at[:, pl.ds(8 + 8 * dx, 2)], got_x.at[(1 + dx) // 2], dz, dx, 0
            )
        else:
            grid_sends[came] = sender(
                grid.at[Z_PAIR[dz], pl.ds(8 + 8 * dx, 2)], got_zx.at[SLOT[dz, dx]], dz, dx, 0
            )
        edge_sends[came] = sender(folded, got_folded.at[SLOT[dz, dx]], dz, dx, 0)
    sum_y = {-dy: sender(sums.at[(1 + dy) // 2], got_y.at[(1 + dy) // 2], 0, 0, dy) for dy in (-1, 1)}
    class_ends = {-dy: sender(ends, class_y.at[(1 + dy) // 2], 0, 0, dy) for dy in (-1, 1)}

    def slot_from(dz, dx):
        return SLOT[-dz, -dx]

    classes[...] = jnp.zeros((2, 128, 128), F32)
    ends[...] = jnp.zeros((8, 128), F32)

    def class_row(z):
        return 64 * (z % 2) + XP * (z // 2)

    zero_patch = jnp.zeros((3, 2, 8, 128), F32)
    zero_lead = jnp.zeros((3, 4, 8, 128), F32)
    for ref in (patch, patch_edge):
        ref[BLOCKS, :, pl.ds(0, 4)] = zero_lead

    def scatter(b):
        lanes, row, cell, frac, alive = particle(b, tile_ref, live_ref, cells_ref, offsets_ref)
        tile = tile_ref[b]
        right = split(along_y(cell, frac[2], (tile & 31) * 4))
        wy_high[b] = right[0]
        wy_low[b] = right[1]
        wz, wz_moment = along_z(cell, frac[0])
        wx, wx_moment = along_x(cell, frac[1])
        mass = jnp.broadcast_to(mass_ref[pl.ds(b, 1), :], (8, 128)) * alive
        push = by_channel([mass] + [mass * row(velocity_ref, i) for i in range(3)])
        zero = jnp.zeros((8, 128), F32)
        scale = 4.0 * DT * alive

        def twist(j):
            return mass * by_channel(
                [zero] + [row(affine_ref, 3 * i + j) for i in range(3)]
            ) - scale * by_channel([zero] + [row(stress_ref, 3 * i + j) for i in range(3)])

        twists = [twist(j) for j in range(3)]
        plain, moment = [], []
        for pair in range(3):
            lead = wz[pair] * push + wz_moment[pair] * twists[0]
            second = wz[pair] * twists[1]
            third = wz[pair] * twists[2]
            for i in range(6):
                plain.append(wx[i] * lead + wx_moment[i] * second)
                moment.append(wx[i] * third)
        left = jnp.concatenate(
            [jnp.concatenate(plain, 0), jnp.concatenate(moment, 0)], 1
        )
        pad = jnp.zeros((112, 256), BF16)
        right = [jnp.concatenate([part, pad], 0) for part in right]
        found = product(left, right, ((1,), (1,)))
        patch[b, :, pl.ds(0, 6)] = found[:, :128].reshape(3, 6, 8, 128)
        patch_edge[b, :, pl.ds(0, 6)] = found[:, 128:].reshape(3, 6, 8, 128)
        patch[b, :, pl.ds(6, 2)] = zero_patch
        patch_edge[b, :, pl.ds(6, 2)] = zero_patch

    def send_classes():
        loads[8].wait()
        loads[9].wait()
        planes[0] = mask_ref[...].astype(F32)
        planes[1] = friction_ref[...].astype(F32)
        flat = planes.reshape(128, 128)
        sides[0] = flat[pl.ds(0, 8, stride=16), :]
        sides[1] = flat[pl.ds(15, 8, stride=16), :]
        for kind in range(2):
            for z in range(4):
                classes[kind, pl.ds(class_row(z + 1) + 1, 16), :] = planes[kind, z]
        partners = len(FACES) + 2
        pl.semaphore_wait(
            barrier, partners - 3 * (1 - above.astype(jnp.int32)) - 3 * (1 - below.astype(jnp.int32))
        )
        for dz, dx in FACES:
            where_z(dz, class_sends[-dz, -dx].start)

    for load in loads[:8]:
        load.wait()

    def scatter_some(step, carry):
        pl.when(step == 1)(send_classes)
        for u in range(UNROLL):
            scatter(step * UNROLL + u)
        return carry

    lax.fori_loop(0, BLOCKS // UNROLL, scatter_some, 0)

    def collect(source, target):
        def one(q, carry):
            total = jnp.zeros((3, 4, 8, 128), F32)
            for b in range(BLOCKS):
                tx = lax.shift_right_logical(tile_ref[b], 5) & 3
                here, before = tx == q, tx == q - 1
                slot = jnp.where(here | before, b, BLOCKS)
                start = jnp.where(before, 4, 0)
                total = total + source[slot, :, pl.ds(start, 4)]
            target[:, pl.ds(4 * q, 4)] = total
            return carry

        lax.fori_loop(0, 5, one, 0)

    collect(patch_edge, edge)
    edge_rows = edge.reshape(ROWS, 128)
    gap = jnp.zeros((4, 128), F32)
    for c in range(4):
        halves = [edge_rows[pl.ds(2 * c + low, NODES, stride=8), :] for low in range(2)]
        flipped = jnp.concatenate([halves[0], gap, halves[1], gap], 0).T
        sums[0, pl.ds(2 * c, 2), :] = flipped[0:2]
        sums[1, pl.ds(2 * c, 2), :] = flipped[2:4]
    for dy in (-1, 1):
        sum_y[-dy].start()

    collect(patch, grid)
    for dz, dx in FACES:
        where_z(dz, grid_sends[-dz, -dx].start)

    for dy in (-1, 1):
        sum_y[dy].wait_recv()
    folded[0] = sums[0] + got_y[1]
    folded[1] = sums[1] + got_y[0]
    for dz, dx in FACES:
        where_z(dz, edge_sends[-dz, -dx].start)

    for dz, dx in FACES:

        def take(dz=dz, dx=dx):
            class_sends[dz, dx].wait_recv()
            if dx == 0:
                z = 0 if dz == -1 else 5
                for kind in range(2):
                    classes[kind, pl.ds(class_row(z) + 1, 16), :] = class_z[(1 - dz) // 2, kind]
            else:
                x = 0 if dx == -1 else 17
                for kind in range(2):
                    for z in range(4) if dz == 0 else (Z_PLANE[-dz],):
                        classes[kind, pl.ds(class_row(z + 1 + 4 * dz) + x, 1), :] = class_x[
                            slot_from(dz, dx), pl.ds(4 * kind + z, 1), :
                        ]

        where_z(dz, take)
    for kind in range(2):
        flipped = classes[kind].T
        ends[pl.ds(2 * kind, 1), :] = flipped[0:1]
        ends[pl.ds(2 * kind + 1, 1), :] = flipped[127:128]
    for dy in (-1, 1):
        class_ends[-dy].start()

    bvel = []
    loads[10].wait()
    for i in range(3):
        bvel.append(bvel_ref[i])

    for dz, dx in FACES:

        def add(dz=dz, dx=dx):
            grid_sends[dz, dx].wait_recv()

        where_z(dz, add)
    for dz, dx in FACES:
        where_z(dz, grid_sends[-dz, -dx].wait_send)
    for dz, dx in FACES:

        def add(dz=dz, dx=dx):
            if dx == 0:
                pair = Z_PAIR[dz]
                grid[pair, pl.ds(0, 18)] = grid[pair, pl.ds(0, 18)] + got_z[(1 - dz) // 2]
            elif dz == 0:
                xs = pl.ds(8 + 8 * dx, 2)
                grid[:, xs] = grid[:, xs] + got_x[(1 - dx) // 2]
            else:
                pair, xs = Z_PAIR[dz], pl.ds(8 + 8 * dx, 2)
                grid[pair, xs] = grid[pair, xs] + got_zx[slot_from(dz, dx)]

        where_z(dz, add)
    grid_rows = grid.reshape(ROWS, 128)
    number = lax.broadcasted_iota(jnp.int32, (NODES, 128), 0)
    for low in range(2):
        load = [grid_rows[pl.ds(2 * c + low, NODES, stride=8), :] for c in range(4)]
        new = contact(
            load[0],
            load[1:],
            classes[0, pl.ds(64 * low, NODES), :],
            classes[1, pl.ds(64 * low, NODES), :],
            bvel,
        )
        if low == 0:
            outside = (number < XP) & (iz == 0)
        else:
            outside = (number >= 2 * XP) & (iz == nz - 1)
        for i in range(3):
            grid_rows[pl.ds(2 * i + 2 + low, NODES, stride=8), :] = jnp.where(
                outside, 0.0, new[i]
            )

    lane = lax.broadcasted_iota(jnp.int32, (8, 128), 1)
    node = lane & 63
    pair = jnp.where(node >= 2 * XP, 2, jnp.where(node >= XP, 1, 0))
    place = node - XP * pair
    totals = [folded[0], folded[1]]
    for dz, dx in FACES:
        where_z(dz, edge_sends[dz, dx].wait_recv)
        keep = node < NODES
        if dx == -1:
            keep = keep & (place < 2)
        elif dx == 1:
            keep = keep & (place >= 16) & (place < 18)
        if dz == -1:
            keep = keep & (pair == 0) & below
        elif dz == 1:
            keep = keep & (pair == 2) & above
        shift = (16 * dx + 2 * XP * dz) % 128
        for side in range(2):
            came = pltpu.roll(got_folded[slot_from(dz, dx), side], shift, 1)
            totals[side] = totals[side] + jnp.where(keep, came, 0.0)
    for dy in (-1, 1):
        class_ends[dy].wait_recv()
    kinds = []
    for kind in range(2):
        low, high = pl.ds(2 * kind, 1), pl.ds(2 * kind + 1, 1)
        kinds.append(
            jnp.concatenate([class_y[1, high, :], ends[low, :], ends[high, :], class_y[0, low, :]], 0)
        )
    parts = [
        jnp.concatenate([totals[0][2 * c : 2 * c + 2], totals[1][2 * c : 2 * c + 2]], 0)
        for c in range(4)
    ]
    new = contact(parts[0], parts[1:], kinds[0], kinds[1], bvel)
    depth = 2 * pair[:4] + lax.shift_right_logical(lane[:4], 6)
    outside = ((depth == 0) & (iz == 0)) | ((depth == 5) & (iz == nz - 1))
    tail = jnp.zeros((124, 128), F32)
    for i in range(3):
        rows = jnp.concatenate([jnp.where(outside, 0.0, new[i]), tail], 0).T
        for low in range(2):
            edge_rows[pl.ds(2 * i + 2 + low, NODES, stride=8), :] = rows[64 * low : 64 * low + NODES]

    for dz, dx in FACES:

        def finish(came=(-dz, -dx)):
            class_sends[came].wait_send()
            edge_sends[came].wait_send()

        where_z(dz, finish)
    for dy in (-1, 1):
        sum_y[dy].wait_send()
        class_ends[dy].wait_send()


def collect_back(
    tile_ref,
    live_ref,
    cells_ref,
    offsets_ref,
    wy_high,
    wy_low,
    grid,
    edge,
    out_velocity,
    out_affine,
    out_offsets,
):
    def gather(b):
        lanes, row, cell, frac, alive = particle(b, tile_ref, live_ref, cells_ref, offsets_ref)
        first = (lax.shift_right_logical(tile_ref[b], 5) & 3) * 4
        left = jnp.concatenate(
            [ref[:, pl.ds(first, 6)].reshape(144, 128) for ref in (grid, edge)], 1
        )
        pad = jnp.zeros((112, 256), BF16)
        right = [jnp.concatenate([ref[b], pad], 0) for ref in (wy_high, wy_low)]
        found = product(left, right, ((1,), (0,)))
        plain = found[:, :128].reshape(3, 6, 8, 128)
        moment = found[:, 128:].reshape(3, 6, 8, 128)
        wz, wz_moment = along_z(cell, frac[0])
        wx, wx_moment = along_x(cell, frac[1])
        totals = [jnp.zeros((8, 128), F32) for _ in range(4)]
        for pair in range(3):
            sum_w = sum(wx[i] * plain[pair, i] for i in range(6))
            sum_x = sum(wx_moment[i] * plain[pair, i] for i in range(6))
            sum_y = sum(wx[i] * moment[pair, i] for i in range(6))
            totals[0] = totals[0] + wz[pair] * sum_w
            totals[1] = totals[1] + wz_moment[pair] * sum_w
            totals[2] = totals[2] + wz[pair] * sum_x
            totals[3] = totals[3] + wz[pair] * sum_y
        totals = [(t + pltpu.roll(t, 7, 0)) * alive for t in totals]
        for i in range(3):
            at = 2 * i + 2
            moved = totals[0][at : at + 1]
            out_velocity[pl.ds(i, 1), lanes] = moved
            out_offsets[pl.ds(i, 1), lanes] = frac[i][:1] * alive + DT * moved
            for j in range(3):
                out_affine[pl.ds(3 * i + j, 1), lanes] = 4.0 * totals[j + 1][at : at + 1]

    def gather_some(step, carry):
        for u in range(UNROLL):
            gather(step * UNROLL + u)
        return carry

    lax.fori_loop(0, BLOCKS // UNROLL, gather_some, 0)


def on_device(
    cells,
    offsets,
    velocity,
    affine,
    stress,
    mass,
    block_tile,
    live_blocks,
    bucket_mask,
    friction_class,
    bucket_velocity,
):
    hbm = pl.BlockSpec(memory_space=pltpu.HBM)
    vmem = pl.BlockSpec(memory_space=pltpu.VMEM)
    smem = pl.BlockSpec(memory_space=pltpu.SMEM)
    count = cells.shape[0]
    args = (
        block_tile,
        live_blocks,
        bucket_velocity,
        cells.reshape(BLOCKS, 128),
        offsets,
        velocity,
        affine,
        stress,
        mass.reshape(BLOCKS, 128),
        bucket_mask,
        friction_class,
    )
    kept = pl.pallas_call(
        spread,
        out_shape=(
            pltpu.SMEM((BLOCKS,), jnp.int32),
            pltpu.SMEM((1,), jnp.int32),
            pltpu.VMEM((BLOCKS, 128), jnp.int32),
            pltpu.VMEM((3, count), F32),
            pltpu.VMEM((BLOCKS, 144, 256), BF16),
            pltpu.VMEM((BLOCKS, 144, 256), BF16),
            pltpu.VMEM((3, XP, 8, 128), F32),
            pltpu.VMEM((3, XP, 8, 128), F32),
        ),
        in_specs=[hbm] * len(args),
        out_specs=(smem,) * 2 + (vmem,) * 6,
        scratch_shapes=[pltpu.SMEM((3,), F32)]
        + [pltpu.VMEM(arg.shape, arg.dtype) for arg in args[5:]]
        + [
            pltpu.VMEM((BLOCKS + 1, 3, 8, 8, 128), F32),
            pltpu.VMEM((BLOCKS + 1, 3, 8, 8, 128), F32),
            pltpu.VMEM((2, 8, 128), F32),
            pltpu.VMEM((2, 8, 128), F32),
            pltpu.VMEM((2, 128, 128), F32),
            pltpu.VMEM((2, 4, 16, 128), F32),
            pltpu.VMEM((2, 8, 128), F32),
            pltpu.VMEM((8, 128), F32),
            pltpu.VMEM((2, 18, 8, 128), F32),
            pltpu.VMEM((2, 3, 2, 8, 128), F32),
            pltpu.VMEM((len(FACES), 2, 8, 128), F32),
            pltpu.VMEM((2, 8, 128), F32),
            pltpu.VMEM((len(FACES), 2, 8, 128), F32),
            pltpu.VMEM((2, 2, 16, 128), F32),
            pltpu.VMEM((len(FACES), 8, 128), F32),
            pltpu.VMEM((2, 8, 128), F32),
            pltpu.SemaphoreType.DMA((len(args),)),
            pltpu.SemaphoreType.DMA((SENDS,)),
            pltpu.SemaphoreType.DMA((SENDS,)),
        ],
        compiler_params=pltpu.CompilerParams(
            collective_id=0, has_side_effects=True, vmem_limit_bytes=VMEM_SPREAD
        ),
    )(*args)
    return pl.pallas_call(
        collect_back,
        out_shape=(
            jax.ShapeDtypeStruct((3, count), F32),
            jax.ShapeDtypeStruct((9, count), F32),
            jax.ShapeDtypeStruct((3, count), F32),
        ),
        in_specs=[smem] * 2 + [vmem] * 6,
        out_specs=(vmem,) * 3,
        compiler_params=pltpu.CompilerParams(vmem_limit_bytes=VMEM_COLLECT),
    )(*kept)


def solution(mesh):
    along = ("gx", "gy", "gz")
    return jax.shard_map(
        on_device,
        mesh=mesh,
        in_specs=(
            P(along),
            P(None, along),
            P(None, along),
            P(None, along),
            P(None, along),
            P(along),
            P(along),
            P(along),
            P("gz", "gx", "gy"),
            P("gz", "gx", "gy"),
            P(),
        ),
        out_specs=(P(None, along), P(None, along), P(None, along)),
        check_vma=False,
    )
```

```python
import jax
import jax.numpy as jnp
from jax import lax
from jax.experimental import pallas as pl
from jax.experimental.pallas import tpu as pltpu
from jax.sharding import PartitionSpec as P

DT = 0.1
GRAVITY = -9.8
MASS_FLOOR = 0.5
SLIP_FLOOR = 0.1
FRICTION = (0.1, 0.4, 0.8, 1.2)

BLOCKS = 16
UNROLL = 8
VMEM_SPREAD = 58 * 1024 * 1024
VMEM_FINISH = 16 * 1024 * 1024
XN = 18
STEP = 20
F32 = jnp.float32
BF16 = jnp.bfloat16
MESH = pl.DeviceIdType.MESH

PLANE, LEFT, EDGE_A, FIRST, EDGE_B, RIGHT, TILES = 0, 4, 5, 7, 25, 27, 28

FACES = [(dz, dx) for dz in (-1, 0, 1) for dx in (-1, 0, 1) if (dz, dx) != (0, 0)]
NINE = [(dz, dx) for dz in (-1, 1, 0) for dx in (-1, 1, 0)]
SLOT = {side: index for index, side in enumerate(NINE)}
Z_PLANE = {-1: 0, 1: 3}
Z_PAIR = {-1: 0, 1: 2}


def spline(frac):
    weights = (
        0.5 * (1.5 - frac) * (1.5 - frac),
        0.75 - (frac - 1.0) * (frac - 1.0),
        0.5 * (frac - 0.5) * (frac - 0.5),
    )
    moments = tuple(w * (float(k) - frac) for k, w in enumerate(weights))
    return weights, moments


def pick(hits, values):
    out = jnp.where(hits[2], values[2], 0.0)
    out = jnp.where(hits[1], values[1], out)
    return jnp.where(hits[0], values[0], out)


def split(value):
    high = value.astype(BF16)
    return high, (value - high.astype(F32)).astype(BF16)


def along_z(cell, frac):
    low = lax.broadcasted_iota(jnp.int32, (8, 128), 0) & 1
    near = lax.shift_right_logical(cell, 4) - low
    weights, moments = spline(frac)
    plain, moment = [], []
    for pair in range(3):
        hits = [near == 2 * pair - k for k in range(3)]
        plain.append(pick(hits, weights))
        moment.append(pick(hits, moments))
    return plain, moment


def six(near, weights, moments):
    hits = [near == v for v in range(4)]
    plain, moment = [], []
    for i in range(6):
        outs = []
        for values in (weights, moments):
            out = jnp.zeros((8, 128), F32)
            for k in range(3):
                if 0 <= i - k < 4:
                    out = jnp.where(hits[i - k], values[k], out)
            outs.append(out)
        plain.append(outs[0])
        moment.append(outs[1])
    return plain, moment


def near_z(cell):
    return lax.shift_right_logical(cell, 4)


def near_x(cell):
    return lax.shift_right_logical(cell, 2) & 3


def along_x_rows(cell, frac):
    row = lax.broadcasted_iota(jnp.int32, (8, 128), 0)
    weights, moments = spline(frac)
    hits = [row - near_x(cell) == k for k in range(3)]
    return jnp.concatenate([pick(hits, weights), pick(hits, moments)], 1)


def along_edge(cell, frac, across):
    row = lax.broadcasted_iota(jnp.int32, (8, 128), 0)
    first = jnp.where(across == 0, 0, jnp.where(across == 31, 4, -999))
    place = (row & 1) - (cell & 3) + first
    weights, moments = spline(frac)
    hits = [place == k for k in range(3)]
    return pick(hits, weights), pick(hits, moments)


def along_y(cell, frac, first):
    row = lax.broadcasted_iota(jnp.int32, (8, 128), 0)
    diff = (cell & 3) + (first - 1) - row
    weights, moments = spline(frac)
    plain, moment = [], []
    for t in range(16):
        shifted = diff
        if t == 0:
            shifted = jnp.where(row == 0, -999, diff)
        elif t == 15:
            shifted = jnp.where(row == 7, -999, diff)
        hits = [shifted == 8 * t - k for k in range(3)]
        plain.append(pick(hits, weights))
        moment.append(pick(hits, moments))
    return jnp.concatenate([jnp.concatenate(plain, 0), jnp.concatenate(moment, 0)], 1)


def by_channel(parts):
    row = lax.broadcasted_iota(jnp.int32, (8, 128), 0)
    out = jnp.where(row < 6, parts[2], parts[3])
    out = jnp.where(row < 4, parts[1], out)
    return jnp.where(row < 2, parts[0], out)


def dot(left, right, dims):
    return lax.dot_general(left, right, (dims, ((), ())), preferred_element_type=F32)


NN = ((1,), (0,))
NT = ((1,), (1,))


def contact(mass, momentum, kind, friction, bvel):
    floor = jnp.maximum(mass, MASS_FLOOR)
    speed = [momentum[0] / floor + DT * GRAVITY, momentum[1] / floor, momentum[2] / floor]
    coeff = jnp.where(friction == 3.0, FRICTION[3], 0.0)
    for level in range(3):
        coeff = jnp.where(friction == float(level), FRICTION[level], coeff)
    rel = [speed[i] - bvel[i] for i in range(3)]
    normal = jnp.minimum(rel[0], 0.0)
    slide = jnp.sqrt(rel[1] * rel[1] + rel[2] * rel[2])
    factor = jnp.maximum(0.0, 1.0 + coeff * normal / jnp.maximum(slide, SLIP_FLOOR))
    hit = [bvel[0] + (rel[0] - normal), bvel[1] + factor * rel[1], bvel[2] + factor * rel[2]]
    return [
        jnp.where(kind == 2.0, bvel[i], jnp.where(kind == 1.0, hit[i], speed[i])) for i in range(3)
    ]


def particle(b, tile_ref, live_ref, cells_ref, offsets_ref):
    lanes = pl.ds(pl.multiple_of(b * 128, 128), 128)

    def row(ref, r):
        return jnp.broadcast_to(ref[pl.ds(r, 1), lanes], (8, 128))

    cell = jnp.broadcast_to(cells_ref[pl.ds(b, 1), :], (8, 128))
    frac = [row(offsets_ref, r) for r in range(3)]
    alive = jnp.where(b < live_ref[0], 1.0, 0.0)
    tile = tile_ref[b]
    return lanes, row, cell, frac, alive, lax.shift_right_logical(tile, 5) & 3, tile & 31


def edge_row(z):
    return 60 * (z % 2) + STEP * (z // 2)


def spread(
    tile_hbm,
    live_hbm,
    bvel_hbm,
    cells_hbm,
    offsets_hbm,
    velocity_hbm,
    affine_hbm,
    stress_hbm,
    mass_hbm,
    mask_hbm,
    friction_hbm,
    tile_ref,
    live_ref,
    cells_ref,
    offsets_ref,
    out_velocity,
    out_affine,
    out_offsets,
    edge_speed,
    bvel_ref,
    velocity_ref,
    affine_ref,
    stress_ref,
    mass_ref,
    mask_ref,
    friction_ref,
    wy,
    patch,
    grid,
    speed,
    ends,
    classes,
    planes,
    got_z,
    got_x,
    got_zx,
    got_ends,
    load_sem,
    send_sem,
    recv_sem,
):
    loads = [
        pltpu.make_async_copy(source, target, load_sem.at[index])
        for index, (source, target) in enumerate(
            (
                (cells_hbm, cells_ref),
                (offsets_hbm, offsets_ref),
                (tile_hbm, tile_ref),
                (live_hbm, live_ref),
                (mass_hbm, mass_ref),
                (velocity_hbm, velocity_ref),
                (affine_hbm, affine_ref),
                (stress_hbm, stress_ref),
                (mask_hbm, mask_ref),
                (friction_hbm, friction_ref),
                (bvel_hbm, bvel_ref),
            )
        )
    ]
    for load in loads:
        load.start()

    ix, iy, iz = lax.axis_index("gx"), lax.axis_index("gy"), lax.axis_index("gz")
    nx, ny, nz = lax.axis_size("gx"), lax.axis_size("gy"), lax.axis_size("gz")
    above, below = iz < nz - 1, iz > 0

    def device(dz, dx, dy):
        return {
            "gx": lax.rem(ix + dx + nx, nx),
            "gy": lax.rem(iy + dy + ny, ny),
            "gz": lax.rem(iz + dz + nz, nz),
        }

    def where_z(dz, action):
        if dz == 0:
            action()
        else:
            pl.when(above if dz == 1 else below)(action)

    barrier = pltpu.get_barrier_semaphore()
    for dz in (-1, 0, 1):

        def greet(dz=dz):
            for dx in (-1, 0, 1):
                for dy in (-1, 0, 1):
                    if (dz, dx, dy) != (0, 0, 0):
                        pl.semaphore_signal(
                            barrier, inc=1, device_id=device(dz, dx, dy), device_id_type=MESH
                        )

        where_z(dz, greet)

    counter = iter(range(26))

    def sender(src, dst, dz, dx, dy):
        slot = next(counter)
        return pltpu.make_async_remote_copy(
            src_ref=src,
            dst_ref=dst,
            send_sem=send_sem.at[slot],
            recv_sem=recv_sem.at[slot],
            device_id=device(dz, dx, dy),
            device_id_type=MESH,
        )

    grid_sends, end_sends = {}, {}
    for dz, dx in FACES:
        if dx == 0:
            src = grid.at[Z_PAIR[dz], pl.ds(PLANE, EDGE_B)]
            dst = got_z.at[(1 + dz) // 2]
        else:
            tiles = pl.ds(LEFT if dx == -1 else EDGE_B - 2, 5)
            if dz == 0:
                src, dst = grid.at[:, tiles], got_x.at[(1 + dx) // 2]
            else:
                src, dst = grid.at[Z_PAIR[dz], tiles], got_zx.at[1 + dz + (1 + dx) // 2]
        grid_sends[-dz, -dx] = sender(src, dst, dz, dx, 0)
    for dz, dx in NINE:
        for dy in (-1, 1):
            side = (1 + dy) // 2
            end_sends[-dz, -dx, -dy] = sender(
                ends.at[side], got_ends.at[side, SLOT[dz, dx]], dz, dx, dy
            )

    speed[...] = jnp.zeros((3, XN, 8, 128), F32)
    classes[...] = jnp.zeros((2, 128, 128), F32)
    patch[pl.ds(0, 12)] = jnp.zeros((12, 3, 8, 128), F32)

    def clear(b, carry):
        patch[pl.ds(STEP * b + 18, 14)] = jnp.zeros((14, 3, 8, 128), F32)
        return carry

    lax.fori_loop(0, BLOCKS, clear, 0)
    for load in loads[:8]:
        load.wait()

    zero = jnp.zeros((8, 128), F32)

    def scatter(b, edges):
        lanes, row, cell, frac, alive, down, across = particle(
            b, tile_ref, live_ref, cells_ref, offsets_ref
        )
        right_high, right_low = split(along_y(cell, frac[2], across * 4))
        right = jnp.concatenate([right_high, right_low], 0)
        wy[b] = right
        wz, wz_moment = along_z(cell, frac[0])
        wx, wx_moment = six(near_x(cell), *spline(frac[1]))
        mass = jnp.broadcast_to(mass_ref[pl.ds(b, 1), :], (8, 128)) * alive
        push = by_channel([mass] + [mass * row(velocity_ref, i) for i in range(3)])
        scale = 4.0 * DT * alive

        def twist(j):
            return mass * by_channel(
                [zero] + [row(affine_ref, 3 * i + j) for i in range(3)]
            ) - scale * by_channel([zero] + [row(stress_ref, 3 * i + j) for i in range(3)])

        twists = [twist(j) for j in range(3)]
        plain, moment = [], []
        for pair in range(3):
            lead = wz[pair] * push + wz_moment[pair] * twists[0]
            second = wz[pair] * twists[1]
            third = wz[pair] * twists[2]
            for i in range(6):
                plain.append(wx[i] * lead + wx_moment[i] * second)
                moment.append(wx[i] * third)
        left = jnp.concatenate([jnp.concatenate(plain, 0), jnp.concatenate(moment, 0)], 1)
        left_high, left_low = split(left)
        found = dot(left_high, right, NT)
        found = found[:, :128] + (found[:, 128:] + dot(left_low, right_high, NT))
        for pair in range(3):
            patch[pl.ds(STEP * b + 12, 6), pair] = found[48 * pair : 48 * pair + 48].reshape(
                6, 8, 128
            )

        we, we_moment = along_edge(cell, frac[2], across)
        lead = we * push + we_moment * twists[2]
        second = we * twists[0]
        third = we * twists[1]
        wz, wz_moment = six(near_z(cell), *spline(frac[0]))
        plain = [wz[z] * lead + wz_moment[z] * second for z in range(6)]
        moment = [wz[z] * third for z in range(6)]
        left = jnp.concatenate([jnp.concatenate(plain, 0), jnp.concatenate(moment, 0)], 1)
        across_x = along_x_rows(cell, frac[1])
        across_high = across_x.astype(BF16).astype(F32)
        pad = jnp.zeros((56, 256), F32)
        right = jnp.concatenate([across_high, pad, across_x - across_high, pad], 0).astype(BF16)
        found = dot(jnp.concatenate(split(left), 0), right, NT)
        found = found[:48] + found[48:]
        low = jnp.where(across == 0, 1.0, 0.0)
        high = jnp.where(across == 31, 1.0, 0.0)
        out = []
        for z in range(6):
            part = pltpu.roll(found[8 * z : 8 * z + 8], 4 * down, 1)
            out.append(edges[2 * z] + low * part)
            out.append(edges[2 * z + 1] + high * part)
        return tuple(out)

    def scatter_some(step, edges):
        for u in range(UNROLL):
            edges = scatter(step * UNROLL + u, edges)
        return edges

    edges = lax.fori_loop(0, BLOCKS // UNROLL, scatter_some, (zero,) * 12)

    lane = lax.broadcasted_iota(jnp.int32, (8, 128), 1)
    for side in range(2):
        total = zero
        for z in range(6):
            part = edges[2 * z + side]
            part = jnp.where(lane < XN, part + pltpu.roll(part, 64, 1), 0.0)
            if edge_row(z):
                part = pltpu.roll(part, edge_row(z), 1)
            total = total + part
        ends[side, 0] = total
        for pair in range(3):
            grid[pair, EDGE_A + side] = total
            grid[pair, EDGE_B + side] = total

    loads[8].wait()
    loads[9].wait()
    planes[0] = mask_ref[...].astype(F32)
    planes[1] = friction_ref[...].astype(F32)
    flat = planes.reshape(128, 128)
    for pair in range(3):
        grid[pair, LEFT] = flat[pl.ds(0, 8, stride=16), :]
        grid[pair, RIGHT] = flat[pl.ds(15, 8, stride=16), :]
    for dz in (-1, 1):
        grid[Z_PAIR[dz], pl.ds(PLANE, 4)] = planes[:, Z_PLANE[dz]].reshape(4, 8, 128)
    grid[1, pl.ds(PLANE, 4)] = jnp.zeros((4, 8, 128), F32)
    for kind in range(2):
        for z in range(4):
            classes[kind, pl.ds(edge_row(z + 1) + 1, 16), :] = planes[kind, z]
    flipped = [classes[kind].T for kind in range(2)]
    tail = jnp.zeros((6, 128), F32)
    for side, y in ((0, 0), (1, 127)):
        ends[side, 1] = jnp.concatenate([flipped[0][y : y + 1], flipped[1][y : y + 1], tail], 0)

    for pair in range(3):
        total = jnp.zeros((XN, 8, 128), F32)
        for b in range(BLOCKS):
            down = lax.shift_right_logical(tile_ref[b], 5) & 3
            total = total + patch[pl.ds(STEP * b + 12 - 4 * down, XN), pair]
        grid[pair, pl.ds(FIRST, XN)] = total

    pl.semaphore_wait(
        barrier, 26 - 9 * (1 - above.astype(jnp.int32)) - 9 * (1 - below.astype(jnp.int32))
    )
    for dz, dx in FACES:
        where_z(dz, grid_sends[-dz, -dx].start)
    for dz in (-1, 1, 0):

        def send_ends(dz=dz):
            for dx in (-1, 1, 0):
                for dy in (-1, 1):
                    end_sends[-dz, -dx, -dy].start()

        where_z(dz, send_ends)

    for pair in range(3):
        speed[pair] = grid[pair, pl.ds(FIRST, XN)]
    for dz, dx in FACES:

        def add(dz=dz, dx=dx):
            grid_sends[dz, dx].wait_recv()
            if dx == 0:
                pair = Z_PAIR[dz]
                came = got_z.at[(1 - dz) // 2]
                speed[pair] = speed[pair] + came[pl.ds(FIRST, XN)]
                z = 0 if dz == -1 else 5
                for kind in range(2):
                    classes[kind, pl.ds(edge_row(z) + 1, 16), :] = came[
                        pl.ds(PLANE + 2 * kind, 2)
                    ].reshape(16, 128)
                return
            x = 0 if dx == -1 else 17
            xs = pl.ds(8 + 8 * dx, 2)
            first, mark = (0, 4) if dx == -1 else (3, 0)
            if dz == 0:
                came = got_x.at[(1 - dx) // 2]
                speed[:, xs] = speed[:, xs] + came[:, pl.ds(first, 2)]
                tile, depths = came[0, mark], range(4)
            else:
                pair = Z_PAIR[dz]
                came = got_zx.at[1 - dz + (1 - dx) // 2]
                speed[pair, xs] = speed[pair, xs] + came[pl.ds(first, 2)]
                tile, depths = came[mark], (Z_PLANE[-dz],)
            for kind in range(2):
                for z in depths:
                    at = edge_row(z + 1 + 4 * dz) + x
                    classes[kind, pl.ds(at, 1), :] = tile[4 * kind + z : 4 * kind + z + 1]

        where_z(dz, add)

    loads[10].wait()
    bvel = [bvel_ref[i] for i in range(3)]
    rows = speed.reshape(3 * XN * 8, 128)
    for z in range(6):
        pair, low = z // 2, z % 2

        def at(c):
            return pl.ds(pair * XN * 8 + 2 * c + low, XN, stride=8)

        load = [rows[at(c), :] for c in range(4)]
        kinds = [classes[kind, pl.ds(edge_row(z), XN), :] for kind in range(2)]
        new = contact(load[0], load[1:], kinds[0], kinds[1], bvel)
        for i in range(3):
            value = new[i]
            if z == 0:
                value = jnp.where(below, value, 0.0)
            elif z == 5:
                value = jnp.where(above, value, 0.0)
            rows[at(i + 1), :] = value

    def gather(b):
        lanes, row, cell, frac, alive, down, across = particle(
            b, tile_ref, live_ref, cells_ref, offsets_ref
        )
        left_high, left_low = split(speed[:, pl.ds(4 * down, 6)].reshape(144, 128))
        right_high, right_low = wy[b, pl.ds(0, 128)], wy[b, pl.ds(128, 128)]
        found = dot(
            jnp.concatenate([left_high, left_low], 1),
            jnp.concatenate([right_high, right_high], 0),
            NN,
        ) + dot(left_high, right_low, NN)
        plain = found[:, :128].reshape(3, 6, 8, 128)
        moment = found[:, 128:].reshape(3, 6, 8, 128)
        wz, wz_moment = along_z(cell, frac[0])
        wx, wx_moment = six(near_x(cell), *spline(frac[1]))
        totals = [zero] * 4
        for pair in range(3):
            sum_w = sum(wx[i] * plain[pair, i] for i in range(6))
            sum_x = sum(wx_moment[i] * plain[pair, i] for i in range(6))
            sum_y = sum(wx[i] * moment[pair, i] for i in range(6))
            totals[0] = totals[0] + wz[pair] * sum_w
            totals[1] = totals[1] + wz_moment[pair] * sum_w
            totals[2] = totals[2] + wz[pair] * sum_x
            totals[3] = totals[3] + wz[pair] * sum_y
        totals = [(t + pltpu.roll(t, 7, 0)) * alive for t in totals]
        for i in range(3):
            here = 2 * i + 2
            moved = totals[0][here : here + 1]
            out_velocity[pl.ds(i, 1), lanes] = moved
            out_offsets[pl.ds(i, 1), lanes] = frac[i][:1] * alive + DT * moved
            for j in range(3):
                out_affine[pl.ds(3 * i + j, 1), lanes] = 4.0 * totals[j + 1][here : here + 1]

    def gather_some(step, carry):
        for u in range(UNROLL):
            gather(step * UNROLL + u)
        return carry

    lax.fori_loop(0, BLOCKS // UNROLL, gather_some, 0)

    flipped = [classes[kind].T for kind in range(2)]
    half = jnp.where(lane >= 60, lane - 60, lane)
    pair = jnp.where(half >= 2 * STEP, 2, jnp.where(half >= STEP, 1, 0))
    place = half - STEP * pair
    inner = lane < 120
    totals = [ends[0, 0], ends[1, 0]]
    marks = [zero, zero]
    for dz, dx in NINE:
        keep = inner
        if dx == -1:
            keep = keep & (place < 2)
        elif dx == 1:
            keep = keep & (place >= 16) & (place < 18)
        if dz == -1:
            keep = keep & (pair == 0) & below
        elif dz == 1:
            keep = keep & (pair == 2) & above
        shift = (16 * dx + 2 * STEP * dz) % 128

        def moved(value):
            return jnp.where(keep, pltpu.roll(value, shift, 1) if shift else value, 0.0)

        if (dz, dx) != (0, 0):
            for side in range(2):
                if dx == 0:
                    came = got_z[(1 - dz) // 2, EDGE_A + side]
                else:
                    tile = (2 if dx == -1 else 1) + side
                    if dz == 0:
                        came = got_x[(1 - dx) // 2, 0, tile]
                    else:
                        came = got_zx[1 - dz + (1 - dx) // 2, tile]
                totals[side] = totals[side] + moved(came)
        for dy in (-1, 1):
            where_z(dz, end_sends[dz, dx, dy].wait_recv)
            side = (1 + dy) // 2
            came = got_ends.at[1 - side, SLOT[-dz, -dx]]
            totals[side] = totals[side] + moved(came[0])
            marks[side] = marks[side] + moved(came[1])
    kinds = [
        jnp.concatenate(
            [
                marks[0][kind : kind + 1],
                flipped[kind][0:1],
                flipped[kind][127:128],
                marks[1][kind : kind + 1],
            ],
            0,
        )
        for kind in range(2)
    ]
    parts = [
        jnp.concatenate([totals[0][2 * c : 2 * c + 2], totals[1][2 * c : 2 * c + 2]], 0)
        for c in range(4)
    ]
    new = contact(parts[0], parts[1:], kinds[0], kinds[1], bvel)
    first_row, last_row = edge_row(0), edge_row(5)
    here = lane[:4]
    outside = ((here < first_row + STEP) & (iz == 0)) | ((here >= last_row) & (iz == nz - 1))
    new = [jnp.where(outside, 0.0, value) for value in new]
    for side in range(2):
        edge_speed[side] = jnp.concatenate(
            [jnp.zeros((2, 128), F32)] + [value[2 * side : 2 * side + 2] for value in new], 0
        )

    for dz in (-1, 0, 1):

        def finish(dz=dz):
            for dx in (-1, 0, 1):
                if (dz, dx) != (0, 0):
                    grid_sends[-dz, -dx].wait_send()
                for dy in (-1, 1):
                    end_sends[-dz, -dx, -dy].wait_send()

        where_z(dz, finish)


def finish(
    tile_ref,
    live_ref,
    cells_ref,
    offsets_ref,
    velocity_ref,
    affine_ref,
    moved_ref,
    edge_speed,
    out_velocity,
    out_affine,
    out_offsets,
):
    out_velocity[...] = velocity_ref[...]
    out_affine[...] = affine_ref[...]
    out_offsets[...] = moved_ref[...]

    def one(b, carry):
        across = tile_ref[b] & 31

        @pl.when((across == 0) | (across == 31))
        def _():
            lanes, row, cell, frac, alive, down, across = particle(
                b, tile_ref, live_ref, cells_ref, offsets_ref
            )
            side = jnp.where(across == 0, 0, 1)
            value = edge_speed[side]
            left = jnp.concatenate(
                [pltpu.roll(value, (128 - edge_row(z) - 4 * down) & 127, 1) for z in range(6)], 0
            )
            left_high, left_low = split(left)
            right = jnp.concatenate(
                [along_x_rows(cell, frac[1]), jnp.zeros((120, 256), F32)], 0
            )
            right_high, right_low = split(right)
            found = dot(left_high, right_high, NN) + (
                dot(left_low, right_high, NN) + dot(left_high, right_low, NN)
            )
            we, we_moment = along_edge(cell, frac[2], across)
            wz, wz_moment = six(near_z(cell), *spline(frac[0]))
            sum_w = sum(wz[z] * found[8 * z : 8 * z + 8, :128] for z in range(6))
            sum_z = sum(wz_moment[z] * found[8 * z : 8 * z + 8, :128] for z in range(6))
            sum_x = sum(wz[z] * found[8 * z : 8 * z + 8, 128:] for z in range(6))
            totals = [we * sum_w, we * sum_z, we * sum_x, we_moment * sum_w]
            totals = [(t + pltpu.roll(t, 7, 0)) * alive for t in totals]
            for i in range(3):
                here = 2 * i + 2
                moved = totals[0][here : here + 1]
                out_velocity[pl.ds(i, 1), lanes] += moved
                out_offsets[pl.ds(i, 1), lanes] += DT * moved
                for j in range(3):
                    out_affine[pl.ds(3 * i + j, 1), lanes] += (
                        4.0 * totals[j + 1][here : here + 1]
                    )

        return carry

    lax.fori_loop(0, BLOCKS, one, 0)


def on_device(
    cells,
    offsets,
    velocity,
    affine,
    stress,
    mass,
    block_tile,
    live_blocks,
    bucket_mask,
    friction_class,
    bucket_velocity,
):
    hbm = pl.BlockSpec(memory_space=pltpu.HBM)
    vmem = pl.BlockSpec(memory_space=pltpu.VMEM)
    smem = pl.BlockSpec(memory_space=pltpu.SMEM)
    count = cells.shape[0]
    args = (
        block_tile,
        live_blocks,
        bucket_velocity,
        cells.reshape(BLOCKS, 128),
        offsets,
        velocity,
        affine,
        stress,
        mass.reshape(BLOCKS, 128),
        bucket_mask,
        friction_class,
    )
    kept = pl.pallas_call(
        spread,
        out_shape=(
            pltpu.SMEM((BLOCKS,), jnp.int32),
            pltpu.SMEM((1,), jnp.int32),
            pltpu.VMEM((BLOCKS, 128), jnp.int32),
            pltpu.VMEM((3, count), F32),
            pltpu.VMEM((3, count), F32),
            pltpu.VMEM((9, count), F32),
            pltpu.VMEM((3, count), F32),
            pltpu.VMEM((2, 8, 128), F32),
        ),
        in_specs=[hbm] * len(args),
        out_specs=(smem,) * 2 + (vmem,) * 6,
        scratch_shapes=[pltpu.SMEM((3,), F32)]
        + [pltpu.VMEM(arg.shape, arg.dtype) for arg in args[5:]]
        + [
            pltpu.VMEM((BLOCKS, 256, 256), BF16),
            pltpu.VMEM((STEP * BLOCKS + 12, 3, 8, 128), F32),
            pltpu.VMEM((3, TILES, 8, 128), F32),
            pltpu.VMEM((3, XN, 8, 128), F32),
            pltpu.VMEM((2, 2, 8, 128), F32),
            pltpu.VMEM((2, 128, 128), F32),
            pltpu.VMEM((2, 4, 16, 128), F32),
            pltpu.VMEM((2, EDGE_B, 8, 128), F32),
            pltpu.VMEM((2, 3, 5, 8, 128), F32),
            pltpu.VMEM((4, 5, 8, 128), F32),
            pltpu.VMEM((2, len(NINE), 2, 8, 128), F32),
            pltpu.SemaphoreType.DMA((len(args),)),
            pltpu.SemaphoreType.DMA((26,)),
            pltpu.SemaphoreType.DMA((26,)),
        ],
        compiler_params=pltpu.CompilerParams(
            collective_id=0, has_side_effects=True, vmem_limit_bytes=VMEM_SPREAD
        ),
    )(*args)
    return pl.pallas_call(
        finish,
        out_shape=(
            jax.ShapeDtypeStruct((3, count), F32),
            jax.ShapeDtypeStruct((9, count), F32),
            jax.ShapeDtypeStruct((3, count), F32),
        ),
        in_specs=[smem] * 2 + [vmem] * 6,
        out_specs=(vmem,) * 3,
        compiler_params=pltpu.CompilerParams(vmem_limit_bytes=VMEM_FINISH),
    )(*kept)


def solution(mesh):
    along = ("gx", "gy", "gz")
    return jax.shard_map(
        on_device,
        mesh=mesh,
        in_specs=(
            P(along),
            P(None, along),
            P(None, along),
            P(None, along),
            P(None, along),
            P(along),
            P(along),
            P(along),
            P("gz", "gx", "gy"),
            P("gz", "gx", "gy"),
            P(),
        ),
        out_specs=(P(None, along), P(None, along), P(None, along)),
        check_vma=False,
    )
```

```python
import jax
import jax.numpy as jnp
from jax import lax
from jax.experimental import pallas as pl
from jax.experimental.pallas import tpu as pltpu
from jax.sharding import PartitionSpec as P

DT = 0.1
GRAVITY = -9.8
MASS_FLOOR = 0.5
SLIP_FLOOR = 0.1
FRICTION = (0.1, 0.4, 0.8, 1.2)

BLOCKS = 16
UNROLL = 8
VMEM_SPREAD = 58 * 1024 * 1024
VMEM_FINISH = 16 * 1024 * 1024
XN = 18
STEP = 20
F32 = jnp.float32
BF16 = jnp.bfloat16
MESH = pl.DeviceIdType.MESH

PLANE, LEFT, EDGE_A, FIRST, EDGE_B, RIGHT, TILES = 0, 4, 5, 6, 24, 25, 26

FACES = [(dz, dx) for dz in (-1, 0, 1) for dx in (-1, 0, 1) if (dz, dx) != (0, 0)]
NINE = [(dz, dx) for dz in (-1, 1, 0) for dx in (-1, 1, 0)]
SLOT = {side: index for index, side in enumerate(NINE)}
Z_PLANE = {-1: 0, 1: 3}
Z_PAIR = {-1: 0, 1: 2}


def spline(frac):
    weights = (
        0.5 * (1.5 - frac) * (1.5 - frac),
        0.75 - (frac - 1.0) * (frac - 1.0),
        0.5 * (frac - 0.5) * (frac - 0.5),
    )
    moments = tuple(w * (float(k) - frac) for k, w in enumerate(weights))
    return weights, moments


def pick(hits, values):
    out = jnp.where(hits[2], values[2], 0.0)
    out = jnp.where(hits[1], values[1], out)
    return jnp.where(hits[0], values[0], out)


def split(value):
    high = value.astype(BF16)
    return high, (value - high.astype(F32)).astype(BF16)


def along_z(cell, frac):
    low = lax.broadcasted_iota(jnp.int32, (8, 128), 0) & 1
    near = lax.shift_right_logical(cell, 4) - low
    weights, moments = spline(frac)
    plain, moment = [], []
    for pair in range(3):
        hits = [near == 2 * pair - k for k in range(3)]
        plain.append(pick(hits, weights))
        moment.append(pick(hits, moments))
    return plain, moment


def six(near, weights, moments):
    hits = [near == v for v in range(4)]
    plain, moment = [], []
    for i in range(6):
        outs = []
        for values in (weights, moments):
            out = jnp.zeros((8, 128), F32)
            for k in range(3):
                if 0 <= i - k < 4:
                    out = jnp.where(hits[i - k], values[k], out)
            outs.append(out)
        plain.append(outs[0])
        moment.append(outs[1])
    return plain, moment


def near_z(cell):
    return lax.shift_right_logical(cell, 4)


def near_x(cell):
    return lax.shift_right_logical(cell, 2) & 3


def along_x_rows(cell, frac):
    row = lax.broadcasted_iota(jnp.int32, (8, 128), 0)
    weights, moments = spline(frac)
    hits = [row - near_x(cell) == k for k in range(3)]
    return jnp.concatenate([pick(hits, weights), pick(hits, moments)], 1)


def along_edge(cell, frac, across):
    row = lax.broadcasted_iota(jnp.int32, (8, 128), 0)
    first = jnp.where(across == 0, 0, jnp.where(across == 31, 4, -999))
    place = (row & 1) - (cell & 3) + first
    weights, moments = spline(frac)
    hits = [place == k for k in range(3)]
    return pick(hits, weights), pick(hits, moments)


def along_y(cell, frac, first):
    row = lax.broadcasted_iota(jnp.int32, (8, 128), 0)
    diff = (cell & 3) + (first - 1) - row
    weights, moments = spline(frac)
    plain, moment = [], []
    for t in range(16):
        shifted = diff
        if t == 0:
            shifted = jnp.where(row == 0, -999, diff)
        elif t == 15:
            shifted = jnp.where(row == 7, -999, diff)
        hits = [shifted == 8 * t - k for k in range(3)]
        plain.append(pick(hits, weights))
        moment.append(pick(hits, moments))
    return jnp.concatenate([jnp.concatenate(plain, 0), jnp.concatenate(moment, 0)], 1)


def by_channel(parts):
    row = lax.broadcasted_iota(jnp.int32, (8, 128), 0)
    out = jnp.where(row < 6, parts[2], parts[3])
    out = jnp.where(row < 4, parts[1], out)
    return jnp.where(row < 2, parts[0], out)


def dot(left, right, dims):
    return lax.dot_general(left, right, (dims, ((), ())), preferred_element_type=F32)


NN = ((1,), (0,))
NT = ((1,), (1,))


def contact(mass, momentum, kind, friction, bvel):
    floor = jnp.maximum(mass, MASS_FLOOR)
    speed = [momentum[0] / floor + DT * GRAVITY, momentum[1] / floor, momentum[2] / floor]
    coeff = jnp.where(friction == 3.0, FRICTION[3], 0.0)
    for level in range(3):
        coeff = jnp.where(friction == float(level), FRICTION[level], coeff)
    rel = [speed[i] - bvel[i] for i in range(3)]
    normal = jnp.minimum(rel[0], 0.0)
    slide = jnp.sqrt(rel[1] * rel[1] + rel[2] * rel[2])
    factor = jnp.maximum(0.0, 1.0 + coeff * normal / jnp.maximum(slide, SLIP_FLOOR))
    hit = [bvel[0] + (rel[0] - normal), bvel[1] + factor * rel[1], bvel[2] + factor * rel[2]]
    return [
        jnp.where(kind == 2.0, bvel[i], jnp.where(kind == 1.0, hit[i], speed[i])) for i in range(3)
    ]


def particle(b, tile_ref, live_ref, cells_ref, offsets_ref):
    lanes = pl.ds(pl.multiple_of(b * 128, 128), 128)

    def row(ref, r):
        return jnp.broadcast_to(ref[pl.ds(r, 1), lanes], (8, 128))

    cell = jnp.broadcast_to(cells_ref[pl.ds(b, 1), :], (8, 128))
    frac = [row(offsets_ref, r) for r in range(3)]
    alive = jnp.where(b < live_ref[0], 1.0, 0.0)
    tile = tile_ref[b]
    return lanes, row, cell, frac, alive, lax.shift_right_logical(tile, 5) & 3, tile & 31


def edge_row(z):
    return 60 * (z % 2) + STEP * (z // 2)


def spread(
    tile_hbm,
    live_hbm,
    bvel_hbm,
    cells_hbm,
    offsets_hbm,
    velocity_hbm,
    affine_hbm,
    stress_hbm,
    mass_hbm,
    mask_hbm,
    friction_hbm,
    tile_ref,
    live_ref,
    cells_ref,
    offsets_ref,
    out_velocity,
    out_affine,
    out_offsets,
    edge_speed,
    bvel_ref,
    velocity_ref,
    affine_ref,
    stress_ref,
    mass_ref,
    mask_ref,
    friction_ref,
    wy,
    patch,
    grid,
    across_x,
    speed,
    ends,
    ends_z,
    classes,
    planes,
    got_z,
    got_x,
    got_zx,
    got_ends,
    load_sem,
    send_sem,
    recv_sem,
):
    loads = [
        pltpu.make_async_copy(source, target, load_sem.at[index])
        for index, (source, target) in enumerate(
            (
                (cells_hbm, cells_ref),
                (offsets_hbm, offsets_ref),
                (tile_hbm, tile_ref),
                (live_hbm, live_ref),
                (mass_hbm, mass_ref),
                (velocity_hbm, velocity_ref),
                (affine_hbm, affine_ref),
                (stress_hbm, stress_ref),
                (mask_hbm, mask_ref),
                (friction_hbm, friction_ref),
                (bvel_hbm, bvel_ref),
            )
        )
    ]
    ix, iy, iz = lax.axis_index("gx"), lax.axis_index("gy"), lax.axis_index("gz")
    nx, ny, nz = lax.axis_size("gx"), lax.axis_size("gy"), lax.axis_size("gz")
    above, below = iz < nz - 1, iz > 0

    def device(dz, dx, dy):
        return {
            "gx": lax.rem(ix + dx + nx, nx),
            "gy": lax.rem(iy + dy + ny, ny),
            "gz": lax.rem(iz + dz + nz, nz),
        }

    def where_z(dz, action):
        if dz == 0:
            action()
        else:
            pl.when(above if dz == 1 else below)(action)

    barrier = pltpu.get_barrier_semaphore()

    def greet(dz, dys):
        for dy in dys:
            for dx in (-1, 1, 0):
                if (dz, dx, dy) != (0, 0, 0):
                    pl.semaphore_signal(
                        barrier, inc=1, device_id=device(dz, dx, dy), device_id_type=MESH
                    )

    for dz in (1, 0, -1):
        where_z(dz, lambda dz=dz: greet(dz, (1,)))
    for load in loads:
        load.start()
    for dz in (1, 0, -1):
        where_z(dz, lambda dz=dz: greet(dz, (-1, 0)))

    counter = iter(range(26))

    def sender(src, dst, dz, dx, dy):
        slot = next(counter)
        return pltpu.make_async_remote_copy(
            src_ref=src,
            dst_ref=dst,
            send_sem=send_sem.at[slot],
            recv_sem=recv_sem.at[slot],
            device_id=device(dz, dx, dy),
            device_id_type=MESH,
        )

    grid_sends, end_sends = {}, {}
    for dz, dx in FACES:
        if dz == 0:
            side = (1 + dx) // 2
            src, dst = across_x.at[side], got_x.at[side]
        elif dx == 0:
            src = grid.at[Z_PAIR[dz], pl.ds(PLANE, EDGE_B)]
            dst = got_z.at[(1 + dz) // 2]
        else:
            src = grid.at[Z_PAIR[dz], pl.ds(LEFT if dx == -1 else EDGE_B - 2, 4)]
            dst = got_zx.at[1 + dz + (1 + dx) // 2]
        grid_sends[-dz, -dx] = sender(src, dst, dz, dx, 0)
    for dz, dx in NINE:
        for dy in (-1, 1):
            side = (1 + dy) // 2
            if dz == 0:
                src, dst = ends.at[side], got_ends.at[side, SLOT[dz, dx]]
            else:
                src = ends_z.at[(1 + dz) // 2, side]
                dst = got_ends.at[side, SLOT[dz, dx], 0]
            end_sends[-dz, -dx, -dy] = sender(src, dst, dz, dx, dy)

    speed[...] = jnp.zeros((3, XN, 8, 128), F32)
    classes[...] = jnp.zeros((2, 128, 128), F32)
    patch[pl.ds(0, 12)] = jnp.zeros((12, 3, 8, 128), F32)

    def clear(b, carry):
        patch[pl.ds(STEP * b + 18, 14)] = jnp.zeros((14, 3, 8, 128), F32)
        return carry

    lax.fori_loop(0, BLOCKS, clear, 0)
    for load in loads[:8]:
        load.wait()

    zero = jnp.zeros((8, 128), F32)

    def scatter(b, edges):
        lanes, row, cell, frac, alive, down, across = particle(
            b, tile_ref, live_ref, cells_ref, offsets_ref
        )
        right_high, right_low = split(along_y(cell, frac[2], across * 4))
        right = jnp.concatenate([right_high, right_low], 0)
        wy[b] = right
        wz, wz_moment = along_z(cell, frac[0])
        wx, wx_moment = six(near_x(cell), *spline(frac[1]))
        mass = jnp.broadcast_to(mass_ref[pl.ds(b, 1), :], (8, 128)) * alive
        push = by_channel([mass] + [mass * row(velocity_ref, i) for i in range(3)])
        scale = 4.0 * DT * alive

        def twist(j):
            return mass * by_channel(
                [zero] + [row(affine_ref, 3 * i + j) for i in range(3)]
            ) - scale * by_channel([zero] + [row(stress_ref, 3 * i + j) for i in range(3)])

        twists = [twist(j) for j in range(3)]
        plain, moment = [], []
        for pair in range(3):
            lead = wz[pair] * push + wz_moment[pair] * twists[0]
            second = wz[pair] * twists[1]
            third = wz[pair] * twists[2]
            for i in range(6):
                plain.append(wx[i] * lead + wx_moment[i] * second)
                moment.append(wx[i] * third)
        left = jnp.concatenate([jnp.concatenate(plain, 0), jnp.concatenate(moment, 0)], 1)
        left_high, left_low = split(left)
        found = dot(left_high, right, NT)
        found = found[:, :128] + (found[:, 128:] + dot(left_low, right_high, NT))
        for pair in range(3):
            patch[pl.ds(STEP * b + 12, 6), pair] = found[48 * pair : 48 * pair + 48].reshape(
                6, 8, 128
            )

        we, we_moment = along_edge(cell, frac[2], across)
        lead = we * push + we_moment * twists[2]
        second = we * twists[0]
        third = we * twists[1]
        wz, wz_moment = six(near_z(cell), *spline(frac[0]))
        plain = [wz[z] * lead + wz_moment[z] * second for z in range(6)]
        moment = [wz[z] * third for z in range(6)]
        left = jnp.concatenate([jnp.concatenate(plain, 0), jnp.concatenate(moment, 0)], 1)
        across_x = along_x_rows(cell, frac[1])
        across_high = across_x.astype(BF16).astype(F32)
        pad = jnp.zeros((56, 256), F32)
        right = jnp.concatenate([across_high, pad, across_x - across_high, pad], 0).astype(BF16)
        found = dot(jnp.concatenate(split(left), 0), right, NT)
        found = found[:48] + found[48:]
        low = jnp.where(across == 0, 1.0, 0.0)
        high = jnp.where(across == 31, 1.0, 0.0)
        out = []
        for z in range(6):
            part = pltpu.roll(found[8 * z : 8 * z + 8], 4 * down, 1)
            out.append(edges[2 * z] + low * part)
            out.append(edges[2 * z + 1] + high * part)
        return tuple(out)

    def scatter_some(step, edges):
        for u in range(UNROLL):
            edges = scatter(step * UNROLL + u, edges)
        return edges

    edges = lax.fori_loop(0, BLOCKS // UNROLL, scatter_some, (zero,) * 12)

    lane = lax.broadcasted_iota(jnp.int32, (8, 128), 1)
    half = jnp.where(lane >= 60, lane - 60, lane)
    pair_of = jnp.where(half >= 2 * STEP, 2, jnp.where(half >= STEP, 1, 0))
    place = half - STEP * pair_of

    for side in range(2):
        total = zero
        for z in range(6):
            part = edges[2 * z + side]
            part = jnp.where(lane < XN, part + pltpu.roll(part, 64, 1), 0.0)
            if edge_row(z):
                part = pltpu.roll(part, edge_row(z), 1)
            total = total + part
        ends[side, 0] = total

    loads[8].wait()
    loads[9].wait()
    planes[0] = mask_ref[...].astype(F32)
    planes[1] = friction_ref[...].astype(F32)
    flat = planes.reshape(128, 128)
    sides = [flat[pl.ds(0, 8, stride=16), :], flat[pl.ds(15, 8, stride=16), :]]
    for kind in range(2):
        for z in range(4):
            classes[kind, pl.ds(edge_row(z + 1) + 1, 16), :] = planes[kind, z]
    flipped = [classes[kind].T for kind in range(2)]
    tail = jnp.zeros((6, 128), F32)
    for side, y in ((0, 0), (1, 127)):
        ends[side, 1] = jnp.concatenate([flipped[0][y : y + 1], flipped[1][y : y + 1], tail], 0)

    for dz in (-1, 1):
        pair = Z_PAIR[dz]
        grid[pair, pl.ds(PLANE, 4)] = planes[:, Z_PLANE[dz]].reshape(4, 8, 128)
        grid[pair, LEFT] = sides[0]
        grid[pair, RIGHT] = sides[1]
        here = pair_of == pair
        shift = (-STEP * dz) % 128

        def beside(first, second):
            moved = pltpu.roll(jnp.where(here, second, 0.0), shift, 1)
            return jnp.where(here, first, 0.0) + moved

        both = beside(ends[0, 0], ends[1, 0])
        grid[pair, EDGE_A] = both
        grid[pair, EDGE_B] = both
        for side in range(2):
            ends_z[(1 + dz) // 2, side] = beside(ends[side, 0], ends[side, 1])
    for side in range(2):
        across_x[side, 6] = ends[0, 0]
        across_x[side, 7] = ends[1, 0]
        across_x[side, 8] = sides[side]

    for pair in range(3):
        total = jnp.zeros((XN, 8, 128), F32)
        for b in range(BLOCKS):
            down = lax.shift_right_logical(tile_ref[b], 5) & 3
            total = total + patch[pl.ds(STEP * b + 12 - 4 * down, XN), pair]
        grid[pair, pl.ds(FIRST, XN)] = total
        speed[pair] = total
        across_x[0, pl.ds(2 * pair, 2)] = total[:2]
        across_x[1, pl.ds(2 * pair, 2)] = total[16:]

    pl.semaphore_wait(
        barrier, 26 - 9 * (1 - above.astype(jnp.int32)) - 9 * (1 - below.astype(jnp.int32))
    )
    def send_ends(dy):
        for dz in (1, -1, 0):

            def start(dz=dz):
                for dx in (1, -1, 0):
                    end_sends[-dz, -dx, -dy].start()

            where_z(dz, start)

    pl.when(iy == ny - 1)(lambda: send_ends(1))
    for dz, dx in FACES:
        where_z(dz, grid_sends[-dz, -dx].start)
    pl.when(iy != ny - 1)(lambda: send_ends(1))
    send_ends(-1)

    for dz, dx in FACES:

        def add(dz=dz, dx=dx):
            grid_sends[dz, dx].wait_recv()
            if dx == 0:
                pair = Z_PAIR[dz]
                came = got_z.at[(1 - dz) // 2]
                speed[pair] = speed[pair] + came[pl.ds(FIRST, XN)]
                z = 0 if dz == -1 else 5
                for kind in range(2):
                    classes[kind, pl.ds(edge_row(z) + 1, 16), :] = came[
                        pl.ds(PLANE + 2 * kind, 2)
                    ].reshape(16, 128)
                return
            x = 0 if dx == -1 else 17
            xs = pl.ds(8 + 8 * dx, 2)
            first, mark = (0, 3) if dx == -1 else (2, 0)
            if dz == 0:
                came = got_x.at[(1 - dx) // 2]
                speed[:, xs] = speed[:, xs] + came[pl.ds(0, 6)].reshape(3, 2, 8, 128)
                tile, depths = came[8], range(4)
            else:
                pair = Z_PAIR[dz]
                came = got_zx.at[1 - dz + (1 - dx) // 2]
                speed[pair, xs] = speed[pair, xs] + came[pl.ds(first, 2)]
                tile, depths = came[mark], (Z_PLANE[-dz],)
            for kind in range(2):
                for z in depths:
                    at = edge_row(z + 1 + 4 * dz) + x
                    classes[kind, pl.ds(at, 1), :] = tile[4 * kind + z : 4 * kind + z + 1]

        where_z(dz, add)

    loads[10].wait()
    bvel = [bvel_ref[i] for i in range(3)]
    rows = speed.reshape(3 * XN * 8, 128)
    for z in range(6):
        pair, low = z // 2, z % 2

        def at(c):
            return pl.ds(pair * XN * 8 + 2 * c + low, XN, stride=8)

        load = [rows[at(c), :] for c in range(4)]
        kinds = [classes[kind, pl.ds(edge_row(z), XN), :] for kind in range(2)]
        new = contact(load[0], load[1:], kinds[0], kinds[1], bvel)
        for i in range(3):
            value = new[i]
            if z == 0:
                value = jnp.where(below, value, 0.0)
            elif z == 5:
                value = jnp.where(above, value, 0.0)
            rows[at(i + 1), :] = value

    def gather(b):
        lanes, row, cell, frac, alive, down, across = particle(
            b, tile_ref, live_ref, cells_ref, offsets_ref
        )
        left_high, left_low = split(speed[:, pl.ds(4 * down, 6)].reshape(144, 128))
        right_high, right_low = wy[b, pl.ds(0, 128)], wy[b, pl.ds(128, 128)]
        found = dot(
            jnp.concatenate([left_high, left_low], 1),
            jnp.concatenate([right_high, right_high], 0),
            NN,
        ) + dot(left_high, right_low, NN)
        plain = found[:, :128].reshape(3, 6, 8, 128)
        moment = found[:, 128:].reshape(3, 6, 8, 128)
        wz, wz_moment = along_z(cell, frac[0])
        wx, wx_moment = six(near_x(cell), *spline(frac[1]))
        totals = [zero] * 4
        for pair in range(3):
            sum_w = sum(wx[i] * plain[pair, i] for i in range(6))
            sum_x = sum(wx_moment[i] * plain[pair, i] for i in range(6))
            sum_y = sum(wx[i] * moment[pair, i] for i in range(6))
            totals[0] = totals[0] + wz[pair] * sum_w
            totals[1] = totals[1] + wz_moment[pair] * sum_w
            totals[2] = totals[2] + wz[pair] * sum_x
            totals[3] = totals[3] + wz[pair] * sum_y
        totals = [(t + pltpu.roll(t, 7, 0)) * alive for t in totals]
        for i in range(3):
            here = 2 * i + 2
            moved = totals[0][here : here + 1]
            out_velocity[pl.ds(i, 1), lanes] = moved
            out_offsets[pl.ds(i, 1), lanes] = frac[i][:1] * alive + DT * moved
            for j in range(3):
                out_affine[pl.ds(3 * i + j, 1), lanes] = 4.0 * totals[j + 1][here : here + 1]

    def gather_some(step, carry):
        for u in range(UNROLL):
            gather(step * UNROLL + u)
        return carry

    lax.fori_loop(0, BLOCKS // UNROLL, gather_some, 0)

    flipped = [classes[kind].T for kind in range(2)]
    inner = lane < 120
    totals = [ends[0, 0], ends[1, 0]]
    marks = [zero, zero]
    for dz, dx in NINE:
        keep = inner
        if dx == -1:
            keep = keep & (place < 2)
        elif dx == 1:
            keep = keep & (place >= 16) & (place < 18)
        if dz == -1:
            keep = keep & (pair_of == 0) & below
        elif dz == 1:
            keep = keep & (pair_of == 2) & above
        shift = 16 * dx + 2 * STEP * dz

        def moved(value, second=False):
            shift_by = (shift - STEP * dz if second else shift) % 128
            return jnp.where(keep, pltpu.roll(value, shift_by, 1) if shift_by else value, 0.0)

        if dz:
            if dx == 0:
                came = got_z[(1 - dz) // 2, EDGE_A]
            else:
                came = got_zx[1 - dz + (1 - dx) // 2, 2 if dx == -1 else 1]
            totals[0] = totals[0] + moved(came)
            totals[1] = totals[1] + moved(came, True)
        elif dx:
            for side in range(2):
                totals[side] = totals[side] + moved(got_x[(1 - dx) // 2, 6 + side])
        for dy in (-1, 1):
            where_z(dz, end_sends[dz, dx, dy].wait_recv)
            side = (1 + dy) // 2
            came = got_ends.at[1 - side, SLOT[-dz, -dx]]
            totals[side] = totals[side] + moved(came[0])
            marks[side] = marks[side] + (moved(came[0], True) if dz else moved(came[1]))
    kinds = [
        jnp.concatenate(
            [
                marks[0][kind : kind + 1],
                flipped[kind][0:1],
                flipped[kind][127:128],
                marks[1][kind : kind + 1],
            ],
            0,
        )
        for kind in range(2)
    ]
    parts = [
        jnp.concatenate([totals[0][2 * c : 2 * c + 2], totals[1][2 * c : 2 * c + 2]], 0)
        for c in range(4)
    ]
    new = contact(parts[0], parts[1:], kinds[0], kinds[1], bvel)
    first_row, last_row = edge_row(0), edge_row(5)
    here = lane[:4]
    outside = ((here < first_row + STEP) & (iz == 0)) | ((here >= last_row) & (iz == nz - 1))
    new = [jnp.where(outside, 0.0, value) for value in new]
    for side in range(2):
        edge_speed[side] = jnp.concatenate(
            [jnp.zeros((2, 128), F32)] + [value[2 * side : 2 * side + 2] for value in new], 0
        )

    for dz in (-1, 0, 1):

        def finish(dz=dz):
            for dx in (-1, 0, 1):
                if (dz, dx) != (0, 0):
                    grid_sends[-dz, -dx].wait_send()
                for dy in (-1, 1):
                    end_sends[-dz, -dx, -dy].wait_send()

        where_z(dz, finish)


def finish(
    tile_ref,
    live_ref,
    cells_ref,
    offsets_ref,
    velocity_ref,
    affine_ref,
    moved_ref,
    edge_speed,
    out_velocity,
    out_affine,
    out_offsets,
):
    out_velocity[...] = velocity_ref[...]
    out_affine[...] = affine_ref[...]
    out_offsets[...] = moved_ref[...]

    def one(b, carry):
        across = tile_ref[b] & 31

        @pl.when((across == 0) | (across == 31))
        def _():
            lanes, row, cell, frac, alive, down, across = particle(
                b, tile_ref, live_ref, cells_ref, offsets_ref
            )
            side = jnp.where(across == 0, 0, 1)
            value = edge_speed[side]
            left = jnp.concatenate(
                [pltpu.roll(value, (128 - edge_row(z) - 4 * down) & 127, 1) for z in range(6)], 0
            )
            left_high, left_low = split(left)
            right = jnp.concatenate(
                [along_x_rows(cell, frac[1]), jnp.zeros((120, 256), F32)], 0
            )
            right_high, right_low = split(right)
            found = dot(left_high, right_high, NN) + (
                dot(left_low, right_high, NN) + dot(left_high, right_low, NN)
            )
            we, we_moment = along_edge(cell, frac[2], across)
            wz, wz_moment = six(near_z(cell), *spline(frac[0]))
            sum_w = sum(wz[z] * found[8 * z : 8 * z + 8, :128] for z in range(6))
            sum_z = sum(wz_moment[z] * found[8 * z : 8 * z + 8, :128] for z in range(6))
            sum_x = sum(wz[z] * found[8 * z : 8 * z + 8, 128:] for z in range(6))
            totals = [we * sum_w, we * sum_z, we * sum_x, we_moment * sum_w]
            totals = [(t + pltpu.roll(t, 7, 0)) * alive for t in totals]
            for i in range(3):
                here = 2 * i + 2
                moved = totals[0][here : here + 1]
                out_velocity[pl.ds(i, 1), lanes] += moved
                out_offsets[pl.ds(i, 1), lanes] += DT * moved
                for j in range(3):
                    out_affine[pl.ds(3 * i + j, 1), lanes] += (
                        4.0 * totals[j + 1][here : here + 1]
                    )

        return carry

    lax.fori_loop(0, BLOCKS, one, 0)


def on_device(
    cells,
    offsets,
    velocity,
    affine,
    stress,
    mass,
    block_tile,
    live_blocks,
    bucket_mask,
    friction_class,
    bucket_velocity,
):
    hbm = pl.BlockSpec(memory_space=pltpu.HBM)
    vmem = pl.BlockSpec(memory_space=pltpu.VMEM)
    smem = pl.BlockSpec(memory_space=pltpu.SMEM)
    count = cells.shape[0]
    args = (
        block_tile,
        live_blocks,
        bucket_velocity,
        cells.reshape(BLOCKS, 128),
        offsets,
        velocity,
        affine,
        stress,
        mass.reshape(BLOCKS, 128),
        bucket_mask,
        friction_class,
    )
    kept = pl.pallas_call(
        spread,
        out_shape=(
            pltpu.SMEM((BLOCKS,), jnp.int32),
            pltpu.SMEM((1,), jnp.int32),
            pltpu.VMEM((BLOCKS, 128), jnp.int32),
            pltpu.VMEM((3, count), F32),
            pltpu.VMEM((3, count), F32),
            pltpu.VMEM((9, count), F32),
            pltpu.VMEM((3, count), F32),
            pltpu.VMEM((2, 8, 128), F32),
        ),
        in_specs=[hbm] * len(args),
        out_specs=(smem,) * 2 + (vmem,) * 6,
        scratch_shapes=[pltpu.SMEM((3,), F32)]
        + [pltpu.VMEM(arg.shape, arg.dtype) for arg in args[5:]]
        + [
            pltpu.VMEM((BLOCKS, 256, 256), BF16),
            pltpu.VMEM((STEP * BLOCKS + 12, 3, 8, 128), F32),
            pltpu.VMEM((3, TILES, 8, 128), F32),
            pltpu.VMEM((2, 9, 8, 128), F32),
            pltpu.VMEM((3, XN, 8, 128), F32),
            pltpu.VMEM((2, 2, 8, 128), F32),
            pltpu.VMEM((2, 2, 8, 128), F32),
            pltpu.VMEM((2, 128, 128), F32),
            pltpu.VMEM((2, 4, 16, 128), F32),
            pltpu.VMEM((2, EDGE_B, 8, 128), F32),
            pltpu.VMEM((2, 9, 8, 128), F32),
            pltpu.VMEM((4, 4, 8, 128), F32),
            pltpu.VMEM((2, len(NINE), 2, 8, 128), F32),
            pltpu.SemaphoreType.DMA((len(args),)),
            pltpu.SemaphoreType.DMA((26,)),
            pltpu.SemaphoreType.DMA((26,)),
        ],
        compiler_params=pltpu.CompilerParams(
            collective_id=0, has_side_effects=True, vmem_limit_bytes=VMEM_SPREAD
        ),
    )(*args)
    return pl.pallas_call(
        finish,
        out_shape=(
            jax.ShapeDtypeStruct((3, count), F32),
            jax.ShapeDtypeStruct((9, count), F32),
            jax.ShapeDtypeStruct((3, count), F32),
        ),
        in_specs=[smem] * 2 + [vmem] * 6,
        out_specs=(vmem,) * 3,
        compiler_params=pltpu.CompilerParams(vmem_limit_bytes=VMEM_FINISH),
    )(*kept)


def solution(mesh):
    along = ("gx", "gy", "gz")
    return jax.shard_map(
        on_device,
        mesh=mesh,
        in_specs=(
            P(along),
            P(None, along),
            P(None, along),
            P(None, along),
            P(None, along),
            P(along),
            P(along),
            P(along),
            P("gz", "gx", "gy"),
            P("gz", "gx", "gy"),
            P(),
        ),
        out_specs=(P(None, along), P(None, along), P(None, along)),
        check_vma=False,
    )
```

```python
import jax
import jax.numpy as jnp
from jax import lax
from jax.experimental import pallas as pl
from jax.experimental.pallas import tpu as pltpu
from jax.sharding import PartitionSpec as P

DT = 0.1
GRAVITY = -9.8
MASS_FLOOR = 0.5
SLIP_FLOOR = 0.1
FRICTION = (0.1, 0.4, 0.8, 1.2)

BLOCKS = 16
UNROLL = 16
VMEM_SPREAD = 58 * 1024 * 1024
VMEM_FINISH = 16 * 1024 * 1024
XN = 18
STEP = 20
F32 = jnp.float32
BF16 = jnp.bfloat16
MESH = pl.DeviceIdType.MESH

PLANE, LEFT, EDGE_A, FIRST, EDGE_B, RIGHT, TILES = 0, 4, 5, 6, 24, 25, 26

FACES = [(dz, dx) for dz in (-1, 0, 1) for dx in (-1, 0, 1) if (dz, dx) != (0, 0)]
NINE = [(dz, dx) for dz in (-1, 1, 0) for dx in (-1, 1, 0)]
SLOT = {side: index for index, side in enumerate(NINE)}
Z_PLANE = {-1: 0, 1: 3}
Z_PAIR = {-1: 0, 1: 2}


def spline(frac):
    weights = (
        0.5 * (1.5 - frac) * (1.5 - frac),
        0.75 - (frac - 1.0) * (frac - 1.0),
        0.5 * (frac - 0.5) * (frac - 0.5),
    )
    moments = tuple(w * (float(k) - frac) for k, w in enumerate(weights))
    return weights, moments


def pick(hits, values):
    out = jnp.where(hits[2], values[2], 0.0)
    out = jnp.where(hits[1], values[1], out)
    return jnp.where(hits[0], values[0], out)


def split(value):
    high = value.astype(BF16)
    return high, (value - high.astype(F32)).astype(BF16)


def along_z(cell, frac):
    low = lax.broadcasted_iota(jnp.int32, (8, 128), 0) & 1
    near = lax.shift_right_logical(cell, 4) - low
    weights, moments = spline(frac)
    plain, moment = [], []
    for pair in range(3):
        hits = [near == 2 * pair - k for k in range(3)]
        plain.append(pick(hits, weights))
        moment.append(pick(hits, moments))
    return plain, moment


def six(near, weights, moments):
    hits = [near == v for v in range(4)]
    plain, moment = [], []
    for i in range(6):
        outs = []
        for values in (weights, moments):
            out = jnp.zeros((8, 128), F32)
            for k in range(3):
                if 0 <= i - k < 4:
                    out = jnp.where(hits[i - k], values[k], out)
            outs.append(out)
        plain.append(outs[0])
        moment.append(outs[1])
    return plain, moment


def near_z(cell):
    return lax.shift_right_logical(cell, 4)


def near_x(cell):
    return lax.shift_right_logical(cell, 2) & 3


def along_x_rows(cell, frac):
    row = lax.broadcasted_iota(jnp.int32, (8, 128), 0)
    weights, moments = spline(frac)
    hits = [row - near_x(cell) == k for k in range(3)]
    return jnp.concatenate([pick(hits, weights), pick(hits, moments)], 1)


def along_edge(cell, frac, across):
    row = lax.broadcasted_iota(jnp.int32, (8, 128), 0)
    first = jnp.where(across == 0, 0, jnp.where(across == 31, 4, -999))
    place = (row & 1) - (cell & 3) + first
    weights, moments = spline(frac)
    hits = [place == k for k in range(3)]
    return pick(hits, weights), pick(hits, moments)


def along_y(cell, frac, across):
    row = lax.broadcasted_iota(jnp.int32, (8, 128), 0)
    first = jnp.where(across == 0, 2, 0)
    last = jnp.where(across == 31, 4, 6)
    place = jnp.where((row >= first) & (row < last), row - (cell & 3), -9)
    weights, moments = spline(frac)
    hits = [place == k for k in range(3)]
    return pick(hits, weights), pick(hits, moments)


def by_channel(parts):
    row = lax.broadcasted_iota(jnp.int32, (8, 128), 0)
    out = jnp.where(row < 6, parts[2], parts[3])
    out = jnp.where(row < 4, parts[1], out)
    return jnp.where(row < 2, parts[0], out)


def dot(left, right, dims):
    return lax.dot_general(left, right, (dims, ((), ())), preferred_element_type=F32)


NN = ((1,), (0,))
NT = ((1,), (1,))


def contact(mass, momentum, kind, friction, bvel):
    floor = jnp.maximum(mass, MASS_FLOOR)
    speed = [momentum[0] / floor + DT * GRAVITY, momentum[1] / floor, momentum[2] / floor]
    coeff = jnp.where(friction == 3.0, FRICTION[3], 0.0)
    for level in range(3):
        coeff = jnp.where(friction == float(level), FRICTION[level], coeff)
    rel = [speed[i] - bvel[i] for i in range(3)]
    normal = jnp.minimum(rel[0], 0.0)
    slide = jnp.sqrt(rel[1] * rel[1] + rel[2] * rel[2])
    factor = jnp.maximum(0.0, 1.0 + coeff * normal / jnp.maximum(slide, SLIP_FLOOR))
    hit = [bvel[0] + (rel[0] - normal), bvel[1] + factor * rel[1], bvel[2] + factor * rel[2]]
    return [
        jnp.where(kind == 2.0, bvel[i], jnp.where(kind == 1.0, hit[i], speed[i])) for i in range(3)
    ]


def particle(b, tile_ref, live_ref, cells_ref, offsets_ref):
    lanes = pl.ds(pl.multiple_of(b * 128, 128), 128)

    def row(ref, r):
        return jnp.broadcast_to(ref[pl.ds(r, 1), lanes], (8, 128))

    cell = jnp.broadcast_to(cells_ref[pl.ds(b, 1), :], (8, 128))
    frac = [row(offsets_ref, r) for r in range(3)]
    alive = jnp.where(b < live_ref[0], 1.0, 0.0)
    tile = tile_ref[b]
    return lanes, row, cell, frac, alive, lax.shift_right_logical(tile, 5) & 3, tile & 31


def place_of(down, across):
    return (32 * down + 4 * across + 127) & 127


def weights_xy(cell, frac, across):
    weights, moments = spline(frac[1])
    wx, wx_moment = six(near_x(cell), weights, moments)
    wy, wy_moment = along_y(cell, frac[2], across)
    value = jnp.concatenate(
        [
            jnp.concatenate([wx[i] * wy for i in range(6)], 0),
            jnp.concatenate([wx_moment[i] * wy for i in range(6)], 0),
            jnp.concatenate([wx[i] * wy_moment for i in range(6)], 0),
        ],
        1,
    )
    high, low = split(value)
    pad = jnp.zeros((16, 384), BF16)
    return jnp.concatenate([high, pad, low, pad], 0)


def edge_row(z):
    return 60 * (z % 2) + STEP * (z // 2)


def spread(
    tile_hbm,
    live_hbm,
    bvel_hbm,
    cells_hbm,
    offsets_hbm,
    velocity_hbm,
    affine_hbm,
    stress_hbm,
    mass_hbm,
    mask_hbm,
    friction_hbm,
    tile_ref,
    live_ref,
    cells_ref,
    offsets_ref,
    out_velocity,
    out_affine,
    out_offsets,
    edge_speed,
    listed,
    bvel_ref,
    velocity_ref,
    affine_ref,
    stress_ref,
    mass_ref,
    mask_ref,
    friction_ref,
    weights,
    patch,
    grid,
    across_x,
    speed,
    ends,
    ends_z,
    classes,
    planes,
    got_z,
    got_x,
    got_zx,
    got_ends,
    load_sem,
    send_sem,
    recv_sem,
):
    loads = [
        pltpu.make_async_copy(source, target, load_sem.at[index])
        for index, (source, target) in enumerate(
            (
                (cells_hbm, cells_ref),
                (offsets_hbm, offsets_ref),
                (tile_hbm, tile_ref),
                (live_hbm, live_ref),
                (mass_hbm, mass_ref),
                (velocity_hbm, velocity_ref),
                (affine_hbm, affine_ref),
                (stress_hbm, stress_ref),
                (mask_hbm, mask_ref),
                (friction_hbm, friction_ref),
                (bvel_hbm, bvel_ref),
            )
        )
    ]
    ix, iy, iz = lax.axis_index("gx"), lax.axis_index("gy"), lax.axis_index("gz")
    nx, ny, nz = lax.axis_size("gx"), lax.axis_size("gy"), lax.axis_size("gz")
    above, below = iz < nz - 1, iz > 0

    def device(dz, dx, dy):
        return {
            "gx": lax.rem(ix + dx + nx, nx),
            "gy": lax.rem(iy + dy + ny, ny),
            "gz": lax.rem(iz + dz + nz, nz),
        }

    def where_z(dz, action):
        if dz == 0:
            action()
        else:
            pl.when(above if dz == 1 else below)(action)

    barrier = pltpu.get_barrier_semaphore()

    def greet(dz, dys):
        for dy in dys:
            for dx in (-1, 1, 0):
                if (dz, dx, dy) != (0, 0, 0):
                    pl.semaphore_signal(
                        barrier, inc=1, device_id=device(dz, dx, dy), device_id_type=MESH
                    )

    for dz in (1, 0, -1):
        where_z(dz, lambda dz=dz: greet(dz, (1,)))
    for load in loads:
        load.start()
    for dz in (1, 0, -1):
        where_z(dz, lambda dz=dz: greet(dz, (-1, 0)))

    counter = iter(range(26))

    def sender(src, dst, dz, dx, dy):
        slot = next(counter)
        return pltpu.make_async_remote_copy(
            src_ref=src,
            dst_ref=dst,
            send_sem=send_sem.at[slot],
            recv_sem=recv_sem.at[slot],
            device_id=device(dz, dx, dy),
            device_id_type=MESH,
        )

    grid_sends, end_sends = {}, {}
    for dz, dx in FACES:
        if dz == 0:
            side = (1 + dx) // 2
            src, dst = across_x.at[side], got_x.at[side]
        elif dx == 0:
            src = grid.at[Z_PAIR[dz], pl.ds(PLANE, EDGE_B)]
            dst = got_z.at[(1 + dz) // 2]
        else:
            src = grid.at[Z_PAIR[dz], pl.ds(LEFT if dx == -1 else EDGE_B - 2, 4)]
            dst = got_zx.at[1 + dz + (1 + dx) // 2]
        grid_sends[-dz, -dx] = sender(src, dst, dz, dx, 0)
    for dz, dx in NINE:
        for dy in (-1, 1):
            side = (1 + dy) // 2
            if dz == 0:
                src, dst = ends.at[side], got_ends.at[side, SLOT[dz, dx]]
            else:
                src = ends_z.at[(1 + dz) // 2, side]
                dst = got_ends.at[side, SLOT[dz, dx], 0]
            end_sends[-dz, -dx, -dy] = sender(src, dst, dz, dx, dy)

    speed[...] = jnp.zeros((3, XN, 8, 128), F32)
    classes[...] = jnp.zeros((2, 128, 128), F32)
    patch[pl.ds(0, 12)] = jnp.zeros((12, 3, 8, 128), F32)

    def clear(b, carry):
        patch[pl.ds(STEP * b + 18, 14)] = jnp.zeros((14, 3, 8, 128), F32)
        return carry

    lax.fori_loop(0, BLOCKS, clear, 0)
    for load in loads[:8]:
        load.wait()

    zero = jnp.zeros((8, 128), F32)
    lane = lax.broadcasted_iota(jnp.int32, (8, 128), 1)

    def scatter(b, edges):
        lanes, row, cell, frac, alive, down, across = particle(
            b, tile_ref, live_ref, cells_ref, offsets_ref
        )
        right = weights_xy(cell, frac, across)
        weights[b] = right
        wz, wz_moment = along_z(cell, frac[0])
        mass = jnp.broadcast_to(mass_ref[pl.ds(b, 1), :], (8, 128)) * alive
        push = by_channel([mass] + [mass * row(velocity_ref, i) for i in range(3)])
        scale = 4.0 * DT * alive

        def twist(j):
            return mass * by_channel(
                [zero] + [row(affine_ref, 3 * i + j) for i in range(3)]
            ) - scale * by_channel([zero] + [row(stress_ref, 3 * i + j) for i in range(3)])

        twists = [twist(j) for j in range(3)]
        left = jnp.concatenate(
            [
                jnp.concatenate([wz[p] * push + wz_moment[p] * twists[0] for p in range(3)], 0),
                jnp.concatenate([wz[p] * twists[1] for p in range(3)], 0),
                jnp.concatenate([wz[p] * twists[2] for p in range(3)], 0),
            ],
            1,
        )
        found = dot(jnp.concatenate(split(left), 0), right, NT)
        found = found[:24] + found[24:]
        start = place_of(down, across)
        group = lax.shift_right_logical((lane - start) & 127, 3)
        for pair in range(3):
            part = found[8 * pair : 8 * pair + 8]
            part = jnp.where(lane < 48, part + pltpu.roll(part, 64, 1), 0.0)
            part = pltpu.roll(part, start, 1)
            for i in range(6):
                patch[STEP * b + 12 + i, pair] = jnp.where(group == i, part, 0.0)

        we, we_moment = along_edge(cell, frac[2], across)
        lead = we * push + we_moment * twists[2]
        second = we * twists[0]
        third = we * twists[1]
        wz, wz_moment = six(near_z(cell), *spline(frac[0]))
        plain = [wz[z] * lead + wz_moment[z] * second for z in range(6)]
        moment = [wz[z] * third for z in range(6)]
        left = jnp.concatenate([jnp.concatenate(plain, 0), jnp.concatenate(moment, 0)], 1)
        across_x = along_x_rows(cell, frac[1])
        across_high = across_x.astype(BF16).astype(F32)
        pad = jnp.zeros((56, 256), F32)
        right = jnp.concatenate([across_high, pad, across_x - across_high, pad], 0).astype(BF16)
        found = dot(jnp.concatenate(split(left), 0), right, NT)
        found = found[:48] + found[48:]
        low = jnp.where(across == 0, 1.0, 0.0)
        high = jnp.where(across == 31, 1.0, 0.0)
        out = []
        for z in range(6):
            part = pltpu.roll(found[8 * z : 8 * z + 8], 4 * down, 1)
            out.append(edges[2 * z] + low * part)
            out.append(edges[2 * z + 1] + high * part)
        return tuple(out)

    def scatter_some(step, edges):
        for u in range(UNROLL):
            edges = scatter(step * UNROLL + u, edges)
        return edges

    edges = lax.fori_loop(0, BLOCKS // UNROLL, scatter_some, (zero,) * 12)

    half = jnp.where(lane >= 60, lane - 60, lane)
    pair_of = jnp.where(half >= 2 * STEP, 2, jnp.where(half >= STEP, 1, 0))
    place = half - STEP * pair_of

    for side in range(2):
        total = zero
        for z in range(6):
            part = edges[2 * z + side]
            part = jnp.where(lane < XN, part + pltpu.roll(part, 64, 1), 0.0)
            if edge_row(z):
                part = pltpu.roll(part, edge_row(z), 1)
            total = total + part
        ends[side, 0] = total

    loads[8].wait()
    loads[9].wait()
    flipped = []
    for kind, source in enumerate((mask_ref, friction_ref)):
        for z in range(4):
            value = source[z].astype(F32)
            classes[kind, pl.ds(edge_row(z + 1) + 1, 16), :] = value
            planes[kind, z] = pltpu.roll(value, 8, 1, stride=8, stride_axis=0)
        flipped.append(classes[kind].T)
        for z in range(4):
            classes[kind, pl.ds(edge_row(z + 1) + 1, 16), :] = planes[kind, z]
    flat = planes.reshape(128, 128)
    sides = [flat[pl.ds(0, 8, stride=16), :], flat[pl.ds(15, 8, stride=16), :]]
    tail = jnp.zeros((6, 128), F32)
    for side, y in ((0, 0), (1, 127)):
        ends[side, 1] = jnp.concatenate([flipped[0][y : y + 1], flipped[1][y : y + 1], tail], 0)

    loads[10].wait()
    count = jnp.int32(0)
    order = []
    for b in range(BLOCKS):
        across = tile_ref[b] & 31
        touches = jnp.where((across == 0) | (across == 31), 1, 0)
        order.append((touches, count))
        count = count + touches
    listed[0] = count
    for k in range(BLOCKS):
        at = jnp.int32(0)
        for b in range(k, BLOCKS):
            touches, before = order[b]
            at = at + jnp.where(before == k, b * touches, 0)
        listed[k + 1] = at

    for dz in (-1, 1):
        pair = Z_PAIR[dz]
        grid[pair, pl.ds(PLANE, 4)] = planes[:, Z_PLANE[dz]].reshape(4, 8, 128)
        grid[pair, LEFT] = sides[0]
        grid[pair, RIGHT] = sides[1]
        here = pair_of == pair
        shift = (-STEP * dz) % 128

        def beside(first, second):
            moved = pltpu.roll(jnp.where(here, second, 0.0), shift, 1)
            return jnp.where(here, first, 0.0) + moved

        both = beside(ends[0, 0], ends[1, 0])
        grid[pair, EDGE_A] = both
        grid[pair, EDGE_B] = both
        for side in range(2):
            ends_z[(1 + dz) // 2, side] = beside(ends[side, 0], ends[side, 1])
    for side in range(2):
        across_x[side, 6] = ends[0, 0]
        across_x[side, 7] = ends[1, 0]
        across_x[side, 8] = sides[side]

    for pair in range(3):
        total = jnp.zeros((XN, 8, 128), F32)
        for b in range(BLOCKS):
            down = lax.shift_right_logical(tile_ref[b], 5) & 3
            total = total + patch[pl.ds(STEP * b + 12 - 4 * down, XN), pair]
        grid[pair, pl.ds(FIRST, XN)] = total
        speed[pair] = total
        across_x[0, pl.ds(2 * pair, 2)] = total[:2]
        across_x[1, pl.ds(2 * pair, 2)] = total[16:]

    pl.semaphore_wait(
        barrier, 26 - 9 * (1 - above.astype(jnp.int32)) - 9 * (1 - below.astype(jnp.int32))
    )
    def send_ends(dy):
        for dz in (1, -1, 0):

            def start(dz=dz):
                for dx in (1, -1, 0):
                    end_sends[-dz, -dx, -dy].start()

            where_z(dz, start)

    pl.when(iy == ny - 1)(lambda: send_ends(1))
    for dz, dx in FACES:
        where_z(dz, grid_sends[-dz, -dx].start)
    pl.when(iy != ny - 1)(lambda: send_ends(1))
    send_ends(-1)

    for dz, dx in FACES:

        def add(dz=dz, dx=dx):
            grid_sends[dz, dx].wait_recv()
            if dx == 0:
                pair = Z_PAIR[dz]
                came = got_z.at[(1 - dz) // 2]
                speed[pair] = speed[pair] + came[pl.ds(FIRST, XN)]
                z = 0 if dz == -1 else 5
                for kind in range(2):
                    classes[kind, pl.ds(edge_row(z) + 1, 16), :] = came[
                        pl.ds(PLANE + 2 * kind, 2)
                    ].reshape(16, 128)
                return
            x = 0 if dx == -1 else 17
            xs = pl.ds(8 + 8 * dx, 2)
            first, mark = (0, 3) if dx == -1 else (2, 0)
            if dz == 0:
                came = got_x.at[(1 - dx) // 2]
                speed[:, xs] = speed[:, xs] + came[pl.ds(0, 6)].reshape(3, 2, 8, 128)
                tile, depths = came[8], range(4)
            else:
                pair = Z_PAIR[dz]
                came = got_zx.at[1 - dz + (1 - dx) // 2]
                speed[pair, xs] = speed[pair, xs] + came[pl.ds(first, 2)]
                tile, depths = came[mark], (Z_PLANE[-dz],)
            for kind in range(2):
                for z in depths:
                    at = edge_row(z + 1 + 4 * dz) + x
                    classes[kind, pl.ds(at, 1), :] = tile[4 * kind + z : 4 * kind + z + 1]

        where_z(dz, add)

    columns = []
    for kind in range(2):
        flipped = classes[kind].T
        for y in (0, 127):
            value = jnp.zeros((1, 128), F32)
            for x in range(16):
                at = (y + 8 * x) & 127
                value = jnp.where((place[:1] & 15) == x, flipped[at : at + 1], value)
            columns.append(value)
    bvel = [bvel_ref[i] for i in range(3)]
    rows = speed.reshape(3 * XN * 8, 128)
    for z in range(6):
        pair, low = z // 2, z % 2

        def at(c):
            return pl.ds(pair * XN * 8 + 2 * c + low, XN, stride=8)

        load = [rows[at(c), :] for c in range(4)]
        kinds = [classes[kind, pl.ds(edge_row(z), XN), :] for kind in range(2)]
        new = contact(load[0], load[1:], kinds[0], kinds[1], bvel)
        for i in range(3):
            value = new[i]
            if z == 0:
                value = jnp.where(below, value, 0.0)
            elif z == 5:
                value = jnp.where(above, value, 0.0)
            rows[at(i + 1), :] = value

    def gather(b):
        lanes, row, cell, frac, alive, down, across = particle(
            b, tile_ref, live_ref, cells_ref, offsets_ref
        )
        start = place_of(down, across)
        group = lax.shift_right_logical((lane - start) & 127, 3)
        back = (128 - start) & 127
        high, low = [], []
        for pair in range(3):
            value = speed[pair, pl.ds(4 * down, 6)]
            part = value[5]
            for i in range(5):
                part = jnp.where(group == i, value[i], part)
            part = jnp.where(lane < 48, pltpu.roll(part, back, 1), 0.0)
            rounded = part.astype(BF16).astype(F32)
            high.append(rounded + pltpu.roll(rounded, 64, 1))
            low.append(part - rounded)
        found = dot(jnp.concatenate(high + low, 0).astype(BF16), weights[b], NN)
        found = found[:24] + found[24:]
        wz, wz_moment = along_z(cell, frac[0])
        totals = [zero] * 4
        for pair in range(3):
            rows_of = slice(8 * pair, 8 * pair + 8)
            plain = found[rows_of, :128]
            totals[0] = totals[0] + wz[pair] * plain
            totals[1] = totals[1] + wz_moment[pair] * plain
            totals[2] = totals[2] + wz[pair] * found[rows_of, 128:256]
            totals[3] = totals[3] + wz[pair] * found[rows_of, 256:]
        totals = [(t + pltpu.roll(t, 7, 0)) * alive for t in totals]
        for i in range(3):
            here = 2 * i + 2
            moved = totals[0][here : here + 1]
            out_velocity[pl.ds(i, 1), lanes] = moved
            out_offsets[pl.ds(i, 1), lanes] = frac[i][:1] * alive + DT * moved
            for j in range(3):
                out_affine[pl.ds(3 * i + j, 1), lanes] = 4.0 * totals[j + 1][here : here + 1]

    def gather_some(step, carry):
        for u in range(UNROLL):
            gather(step * UNROLL + u)
        return carry

    lax.fori_loop(0, BLOCKS // UNROLL, gather_some, 0)

    inner = lane < 120
    totals = [ends[0, 0], ends[1, 0]]
    marks = [zero, zero]
    for dz, dx in NINE:
        keep = inner
        if dx == -1:
            keep = keep & (place < 2)
        elif dx == 1:
            keep = keep & (place >= 16) & (place < 18)
        if dz == -1:
            keep = keep & (pair_of == 0) & below
        elif dz == 1:
            keep = keep & (pair_of == 2) & above
        shift = 16 * dx + 2 * STEP * dz

        def moved(value, second=False):
            shift_by = (shift - STEP * dz if second else shift) % 128
            return jnp.where(keep, pltpu.roll(value, shift_by, 1) if shift_by else value, 0.0)

        if dz:
            if dx == 0:
                came = got_z[(1 - dz) // 2, EDGE_A]
            else:
                came = got_zx[1 - dz + (1 - dx) // 2, 2 if dx == -1 else 1]
            totals[0] = totals[0] + moved(came)
            totals[1] = totals[1] + moved(came, True)
        elif dx:
            for side in range(2):
                totals[side] = totals[side] + moved(got_x[(1 - dx) // 2, 6 + side])
        for dy in (-1, 1):
            where_z(dz, end_sends[dz, dx, dy].wait_recv)
            side = (1 + dy) // 2
            came = got_ends.at[1 - side, SLOT[-dz, -dx]]
            totals[side] = totals[side] + moved(came[0])
            marks[side] = marks[side] + (moved(came[0], True) if dz else moved(came[1]))
    kinds = [
        jnp.concatenate(
            [
                marks[0][kind : kind + 1],
                columns[2 * kind],
                columns[2 * kind + 1],
                marks[1][kind : kind + 1],
            ],
            0,
        )
        for kind in range(2)
    ]
    parts = [
        jnp.concatenate([totals[0][2 * c : 2 * c + 2], totals[1][2 * c : 2 * c + 2]], 0)
        for c in range(4)
    ]
    new = contact(parts[0], parts[1:], kinds[0], kinds[1], bvel)
    first_row, last_row = edge_row(0), edge_row(5)
    here = lane[:4]
    outside = ((here < first_row + STEP) & (iz == 0)) | ((here >= last_row) & (iz == nz - 1))
    new = [jnp.where(outside, 0.0, value) for value in new]
    for side in range(2):
        edge_speed[side] = jnp.concatenate(
            [jnp.zeros((2, 128), F32)] + [value[2 * side : 2 * side + 2] for value in new], 0
        )

    for dz in (-1, 0, 1):

        def finish(dz=dz):
            for dx in (-1, 0, 1):
                if (dz, dx) != (0, 0):
                    grid_sends[-dz, -dx].wait_send()
                for dy in (-1, 1):
                    end_sends[-dz, -dx, -dy].wait_send()

        where_z(dz, finish)


def finish(
    tile_ref,
    live_ref,
    cells_ref,
    offsets_ref,
    velocity_ref,
    affine_ref,
    moved_ref,
    edge_speed,
    listed,
    out_velocity,
    out_affine,
    out_offsets,
):
    out_velocity[...] = velocity_ref[...]
    out_affine[...] = affine_ref[...]
    out_offsets[...] = moved_ref[...]

    def one(k, carry):
        b = listed[k + 1]
        lanes, row, cell, frac, alive, down, across = particle(
            b, tile_ref, live_ref, cells_ref, offsets_ref
        )
        side = jnp.where(across == 0, 0, 1)
        value = edge_speed[side]
        left = jnp.concatenate(
            [pltpu.roll(value, (128 - edge_row(z) - 4 * down) & 127, 1) for z in range(6)], 0
        )
        left_high, left_low = split(left)
        right = jnp.concatenate(
            [along_x_rows(cell, frac[1]), jnp.zeros((120, 256), F32)], 0
        )
        right_high, right_low = split(right)
        found = dot(left_high, right_high, NN) + (
            dot(left_low, right_high, NN) + dot(left_high, right_low, NN)
        )
        we, we_moment = along_edge(cell, frac[2], across)
        wz, wz_moment = six(near_z(cell), *spline(frac[0]))
        sum_w = sum(wz[z] * found[8 * z : 8 * z + 8, :128] for z in range(6))
        sum_z = sum(wz_moment[z] * found[8 * z : 8 * z + 8, :128] for z in range(6))
        sum_x = sum(wz[z] * found[8 * z : 8 * z + 8, 128:] for z in range(6))
        totals = [we * sum_w, we * sum_z, we * sum_x, we_moment * sum_w]
        totals = [(t + pltpu.roll(t, 7, 0)) * alive for t in totals]
        for i in range(3):
            here = 2 * i + 2
            moved = totals[0][here : here + 1]
            out_velocity[pl.ds(i, 1), lanes] += moved
            out_offsets[pl.ds(i, 1), lanes] += DT * moved
            for j in range(3):
                out_affine[pl.ds(3 * i + j, 1), lanes] += (
                    4.0 * totals[j + 1][here : here + 1]
                )
        return carry

    lax.fori_loop(0, listed[0], one, 0)


def on_device(
    cells,
    offsets,
    velocity,
    affine,
    stress,
    mass,
    block_tile,
    live_blocks,
    bucket_mask,
    friction_class,
    bucket_velocity,
):
    hbm = pl.BlockSpec(memory_space=pltpu.HBM)
    vmem = pl.BlockSpec(memory_space=pltpu.VMEM)
    smem = pl.BlockSpec(memory_space=pltpu.SMEM)
    count = cells.shape[0]
    args = (
        block_tile,
        live_blocks,
        bucket_velocity,
        cells.reshape(BLOCKS, 128),
        offsets,
        velocity,
        affine,
        stress,
        mass.reshape(BLOCKS, 128),
        bucket_mask,
        friction_class,
    )
    kept = pl.pallas_call(
        spread,
        out_shape=(
            pltpu.SMEM((BLOCKS,), jnp.int32),
            pltpu.SMEM((1,), jnp.int32),
            pltpu.VMEM((BLOCKS, 128), jnp.int32),
            pltpu.VMEM((3, count), F32),
            pltpu.VMEM((3, count), F32),
            pltpu.VMEM((9, count), F32),
            pltpu.VMEM((3, count), F32),
            pltpu.VMEM((2, 8, 128), F32),
            pltpu.SMEM((BLOCKS + 1,), jnp.int32),
        ),
        in_specs=[hbm] * len(args),
        out_specs=(smem,) * 2 + (vmem,) * 6 + (smem,),
        scratch_shapes=[pltpu.SMEM((3,), F32)]
        + [pltpu.VMEM(arg.shape, arg.dtype) for arg in args[5:]]
        + [
            pltpu.VMEM((BLOCKS, 128, 384), BF16),
            pltpu.VMEM((STEP * BLOCKS + 12, 3, 8, 128), F32),
            pltpu.VMEM((3, TILES, 8, 128), F32),
            pltpu.VMEM((2, 9, 8, 128), F32),
            pltpu.VMEM((3, XN, 8, 128), F32),
            pltpu.VMEM((2, 2, 8, 128), F32),
            pltpu.VMEM((2, 2, 8, 128), F32),
            pltpu.VMEM((2, 128, 128), F32),
            pltpu.VMEM((2, 4, 16, 128), F32),
            pltpu.VMEM((2, EDGE_B, 8, 128), F32),
            pltpu.VMEM((2, 9, 8, 128), F32),
            pltpu.VMEM((4, 4, 8, 128), F32),
            pltpu.VMEM((2, len(NINE), 2, 8, 128), F32),
            pltpu.SemaphoreType.DMA((len(args),)),
            pltpu.SemaphoreType.DMA((26,)),
            pltpu.SemaphoreType.DMA((26,)),
        ],
        compiler_params=pltpu.CompilerParams(
            collective_id=0, has_side_effects=True, vmem_limit_bytes=VMEM_SPREAD
        ),
    )(*args)
    return pl.pallas_call(
        finish,
        out_shape=(
            jax.ShapeDtypeStruct((3, count), F32),
            jax.ShapeDtypeStruct((9, count), F32),
            jax.ShapeDtypeStruct((3, count), F32),
        ),
        in_specs=[smem] * 2 + [vmem] * 6 + [smem],
        out_specs=(vmem,) * 3,
        compiler_params=pltpu.CompilerParams(vmem_limit_bytes=VMEM_FINISH),
    )(*kept)


def solution(mesh):
    along = ("gx", "gy", "gz")
    return jax.shard_map(
        on_device,
        mesh=mesh,
        in_specs=(
            P(along),
            P(None, along),
            P(None, along),
            P(None, along),
            P(None, along),
            P(along),
            P(along),
            P(along),
            P("gz", "gx", "gy"),
            P("gz", "gx", "gy"),
            P(),
        ),
        out_specs=(P(None, along), P(None, along), P(None, along)),
        check_vma=False,
    )
```

```python
import jax
import jax.numpy as jnp
from jax import lax
from jax.experimental import pallas as pl
from jax.experimental.pallas import tpu as pltpu
from jax.sharding import PartitionSpec as P

DT = 0.1
GRAVITY = -9.8
MASS_FLOOR = 0.5
SLIP_FLOOR = 0.1
FRICTION = (0.1, 0.4, 0.8, 1.2)

BLOCKS = 16
UNROLL = 16
VMEM_SPREAD = 58 * 1024 * 1024
VMEM_FINISH = 16 * 1024 * 1024
XN = 18
STEP = 20
F32 = jnp.float32
BF16 = jnp.bfloat16
MESH = pl.DeviceIdType.MESH

PLANE, LEFT, EDGE_A, FIRST, EDGE_B, RIGHT, TILES = 0, 4, 5, 6, 24, 25, 26

FACES = [(dz, dx) for dz in (-1, 0, 1) for dx in (-1, 0, 1) if (dz, dx) != (0, 0)]
NINE = [(dz, dx) for dz in (-1, 1, 0) for dx in (-1, 1, 0)]
SLOT = {side: index for index, side in enumerate(NINE)}
Z_PLANE = {-1: 0, 1: 3}
Z_PAIR = {-1: 0, 1: 2}


def spline(frac):
    weights = (
        0.5 * (1.5 - frac) * (1.5 - frac),
        0.75 - (frac - 1.0) * (frac - 1.0),
        0.5 * (frac - 0.5) * (frac - 0.5),
    )
    moments = tuple(w * (float(k) - frac) for k, w in enumerate(weights))
    return weights, moments


def pick(hits, values):
    out = jnp.where(hits[2], values[2], 0.0)
    out = jnp.where(hits[1], values[1], out)
    return jnp.where(hits[0], values[0], out)


def split(value):
    high = value.astype(BF16)
    return high, (value - high.astype(F32)).astype(BF16)


def along_z(cell, frac):
    low = lax.broadcasted_iota(jnp.int32, (8, 128), 0) & 1
    near = lax.shift_right_logical(cell, 4) - low
    weights, moments = spline(frac)
    plain, moment = [], []
    for pair in range(3):
        hits = [near == 2 * pair - k for k in range(3)]
        plain.append(pick(hits, weights))
        moment.append(pick(hits, moments))
    return plain, moment


def six(near, weights, moments):
    hits = [near == v for v in range(4)]
    plain, moment = [], []
    for i in range(6):
        outs = []
        for values in (weights, moments):
            out = jnp.zeros((8, 128), F32)
            for k in range(3):
                if 0 <= i - k < 4:
                    out = jnp.where(hits[i - k], values[k], out)
            outs.append(out)
        plain.append(outs[0])
        moment.append(outs[1])
    return plain, moment


def near_z(cell):
    return lax.shift_right_logical(cell, 4)


def near_x(cell):
    return lax.shift_right_logical(cell, 2) & 3


def along_x_rows(cell, frac):
    row = lax.broadcasted_iota(jnp.int32, (8, 128), 0)
    weights, moments = spline(frac)
    hits = [row - near_x(cell) == k for k in range(3)]
    return jnp.concatenate([pick(hits, weights), pick(hits, moments)], 1)


def along_edge(cell, frac, across):
    row = lax.broadcasted_iota(jnp.int32, (8, 128), 0)
    first = jnp.where(across == 0, 0, jnp.where(across == 31, 4, -999))
    place = (row & 1) - (cell & 3) + first
    weights, moments = spline(frac)
    hits = [place == k for k in range(3)]
    return pick(hits, weights), pick(hits, moments)


def along_y(cell, frac, across):
    row = lax.broadcasted_iota(jnp.int32, (8, 128), 0)
    first = jnp.where(across == 0, 2, 0)
    last = jnp.where(across == 31, 4, 6)
    place = jnp.where((row >= first) & (row < last), row - (cell & 3), -9)
    weights, moments = spline(frac)
    hits = [place == k for k in range(3)]
    return pick(hits, weights), pick(hits, moments)


def by_channel(parts):
    row = lax.broadcasted_iota(jnp.int32, (8, 128), 0)
    out = jnp.where(row < 6, parts[2], parts[3])
    out = jnp.where(row < 4, parts[1], out)
    return jnp.where(row < 2, parts[0], out)


def dot(left, right, dims):
    return lax.dot_general(left, right, (dims, ((), ())), preferred_element_type=F32)


NN = ((1,), (0,))
NT = ((1,), (1,))


def contact(mass, momentum, kind, friction, bvel):
    floor = jnp.maximum(mass, MASS_FLOOR)
    speed = [momentum[0] / floor + DT * GRAVITY, momentum[1] / floor, momentum[2] / floor]
    coeff = jnp.where(friction == 3.0, FRICTION[3], 0.0)
    for level in range(3):
        coeff = jnp.where(friction == float(level), FRICTION[level], coeff)
    rel = [speed[i] - bvel[i] for i in range(3)]
    normal = jnp.minimum(rel[0], 0.0)
    slide = jnp.sqrt(rel[1] * rel[1] + rel[2] * rel[2])
    factor = jnp.maximum(0.0, 1.0 + coeff * normal / jnp.maximum(slide, SLIP_FLOOR))
    hit = [bvel[0] + (rel[0] - normal), bvel[1] + factor * rel[1], bvel[2] + factor * rel[2]]
    return [
        jnp.where(kind == 2.0, bvel[i], jnp.where(kind == 1.0, hit[i], speed[i])) for i in range(3)
    ]


def particle(b, tile_ref, live_ref, cells_ref, offsets_ref):
    lanes = pl.ds(pl.multiple_of(b * 128, 128), 128)

    def row(ref, r):
        return jnp.broadcast_to(ref[pl.ds(r, 1), lanes], (8, 128))

    cell = jnp.broadcast_to(cells_ref[pl.ds(b, 1), :], (8, 128))
    frac = [row(offsets_ref, r) for r in range(3)]
    alive = jnp.where(b < live_ref[0], 1.0, 0.0)
    tile = tile_ref[b]
    return lanes, row, cell, frac, alive, lax.shift_right_logical(tile, 5) & 3, tile & 31


def place_of(down, across):
    return (32 * down + 4 * across + 127) & 127


def weights_xy(cell, frac, across):
    weights, moments = spline(frac[1])
    wx, wx_moment = six(near_x(cell), weights, moments)
    wy, wy_moment = along_y(cell, frac[2], across)
    value = jnp.concatenate(
        [
            jnp.concatenate([wx[i] * wy for i in range(6)], 0),
            jnp.concatenate([wx_moment[i] * wy for i in range(6)], 0),
            jnp.concatenate([wx[i] * wy_moment for i in range(6)], 0),
        ],
        1,
    )
    high, low = split(value)
    pad = jnp.zeros((16, 384), BF16)
    return jnp.concatenate([high, pad, low, pad], 0)


def edge_row(z):
    return 60 * (z % 2) + STEP * (z // 2)


def spread(
    tile_hbm,
    live_hbm,
    bvel_hbm,
    cells_hbm,
    offsets_hbm,
    velocity_hbm,
    affine_hbm,
    stress_hbm,
    mass_hbm,
    mask_hbm,
    friction_hbm,
    tile_ref,
    live_ref,
    cells_ref,
    offsets_ref,
    out_velocity,
    out_affine,
    out_offsets,
    edge_speed,
    listed,
    bvel_ref,
    velocity_ref,
    affine_ref,
    stress_ref,
    mass_ref,
    mask_ref,
    friction_ref,
    weights,
    patch,
    grid,
    across_x,
    speed,
    ends,
    ends_z,
    classes,
    planes,
    got_z,
    got_x,
    got_zx,
    got_ends,
    load_sem,
    send_sem,
    recv_sem,
):
    loads = [
        pltpu.make_async_copy(source, target, load_sem.at[index])
        for index, (source, target) in enumerate(
            (
                (cells_hbm, cells_ref),
                (offsets_hbm, offsets_ref),
                (tile_hbm, tile_ref),
                (live_hbm, live_ref),
                (mass_hbm, mass_ref),
                (velocity_hbm, velocity_ref),
                (affine_hbm, affine_ref),
                (stress_hbm, stress_ref),
                (mask_hbm, mask_ref),
                (friction_hbm, friction_ref),
                (bvel_hbm, bvel_ref),
            )
        )
    ]
    ix, iy, iz = lax.axis_index("gx"), lax.axis_index("gy"), lax.axis_index("gz")
    nx, ny, nz = lax.axis_size("gx"), lax.axis_size("gy"), lax.axis_size("gz")
    above, below = iz < nz - 1, iz > 0

    def beside_of(i, n):
        return {-1: jnp.where(i == 0, n - 1, i - 1), 0: i, 1: jnp.where(i == n - 1, 0, i + 1)}

    at_x, at_y, at_z = beside_of(ix, nx), beside_of(iy, ny), beside_of(iz, nz)

    def device(dz, dx, dy):
        return {"gx": at_x[dx], "gy": at_y[dy], "gz": at_z[dz]}

    def where_z(dz, action):
        if dz == 0:
            action()
        else:
            pl.when(above if dz == 1 else below)(action)

    barrier = pltpu.get_barrier_semaphore()

    def greet(dz, dys):
        for dy in dys:
            for dx in (-1, 1, 0):
                if (dz, dx, dy) != (0, 0, 0):
                    pl.semaphore_signal(
                        barrier, inc=1, device_id=device(dz, dx, dy), device_id_type=MESH
                    )

    for dz in (1, 0, -1):
        where_z(dz, lambda dz=dz: greet(dz, (1,)))
    for load in loads:
        load.start()
    for dz in (1, 0, -1):
        where_z(dz, lambda dz=dz: greet(dz, (-1, 0)))

    counter = iter(range(26))

    def sender(src, dst, dz, dx, dy):
        slot = next(counter)
        return pltpu.make_async_remote_copy(
            src_ref=src,
            dst_ref=dst,
            send_sem=send_sem.at[slot],
            recv_sem=recv_sem.at[slot],
            device_id=device(dz, dx, dy),
            device_id_type=MESH,
        )

    grid_sends, end_sends = {}, {}
    for dz, dx in FACES:
        if dz == 0:
            side = (1 + dx) // 2
            src, dst = across_x.at[side], got_x.at[side]
        elif dx == 0:
            src = grid.at[Z_PAIR[dz], pl.ds(PLANE, EDGE_B)]
            dst = got_z.at[(1 + dz) // 2]
        else:
            src = grid.at[Z_PAIR[dz], pl.ds(LEFT if dx == -1 else EDGE_B - 2, 4)]
            dst = got_zx.at[1 + dz + (1 + dx) // 2]
        grid_sends[-dz, -dx] = sender(src, dst, dz, dx, 0)
    for dz, dx in NINE:
        for dy in (-1, 1):
            side = (1 + dy) // 2
            if dz == 0:
                src, dst = ends.at[side], got_ends.at[side, SLOT[dz, dx]]
            else:
                src = ends_z.at[(1 + dz) // 2, side]
                dst = got_ends.at[side, SLOT[dz, dx], 0]
            end_sends[-dz, -dx, -dy] = sender(src, dst, dz, dx, dy)

    speed[...] = jnp.zeros((3, XN, 8, 128), F32)
    classes[...] = jnp.zeros((2, 128, 128), F32)
    patch[pl.ds(0, 12)] = jnp.zeros((12, 3, 8, 128), F32)

    def clear(b, carry):
        patch[pl.ds(STEP * b + 18, 14)] = jnp.zeros((14, 3, 8, 128), F32)
        return carry

    lax.fori_loop(0, BLOCKS, clear, 0)
    for load in loads[:8]:
        load.wait()

    zero = jnp.zeros((8, 128), F32)
    lane = lax.broadcasted_iota(jnp.int32, (8, 128), 1)

    def scatter(b, edges):
        lanes, row, cell, frac, alive, down, across = particle(
            b, tile_ref, live_ref, cells_ref, offsets_ref
        )
        right = weights_xy(cell, frac, across)
        weights[b] = right
        wz, wz_moment = along_z(cell, frac[0])
        mass = jnp.broadcast_to(mass_ref[pl.ds(b, 1), :], (8, 128)) * alive
        push = by_channel([mass] + [mass * row(velocity_ref, i) for i in range(3)])
        scale = 4.0 * DT * alive

        def twist(j):
            return mass * by_channel(
                [zero] + [row(affine_ref, 3 * i + j) for i in range(3)]
            ) - scale * by_channel([zero] + [row(stress_ref, 3 * i + j) for i in range(3)])

        twists = [twist(j) for j in range(3)]
        left = jnp.concatenate(
            [
                jnp.concatenate([wz[p] * push + wz_moment[p] * twists[0] for p in range(3)], 0),
                jnp.concatenate([wz[p] * twists[1] for p in range(3)], 0),
                jnp.concatenate([wz[p] * twists[2] for p in range(3)], 0),
            ],
            1,
        )
        found = dot(jnp.concatenate(split(left), 0), right, NT)
        found = found[:24] + found[24:]
        start = place_of(down, across)
        group = lax.shift_right_logical((lane - start) & 127, 3)
        for pair in range(3):
            part = found[8 * pair : 8 * pair + 8]
            part = jnp.where(lane < 48, part + pltpu.roll(part, 64, 1), 0.0)
            part = pltpu.roll(part, start, 1)
            for i in range(6):
                patch[STEP * b + 12 + i, pair] = jnp.where(group == i, part, 0.0)

        we, we_moment = along_edge(cell, frac[2], across)
        lead = we * push + we_moment * twists[2]
        second = we * twists[0]
        third = we * twists[1]
        wz, wz_moment = six(near_z(cell), *spline(frac[0]))
        plain = [wz[z] * lead + wz_moment[z] * second for z in range(6)]
        moment = [wz[z] * third for z in range(6)]
        left = jnp.concatenate([jnp.concatenate(plain, 0), jnp.concatenate(moment, 0)], 1)
        across_x = along_x_rows(cell, frac[1])
        across_high = across_x.astype(BF16).astype(F32)
        pad = jnp.zeros((56, 256), F32)
        right = jnp.concatenate([across_high, pad, across_x - across_high, pad], 0).astype(BF16)
        found = dot(jnp.concatenate(split(left), 0), right, NT)
        found = found[:48] + found[48:]
        low = jnp.where(across == 0, 1.0, 0.0)
        high = jnp.where(across == 31, 1.0, 0.0)
        out = []
        for z in range(6):
            part = pltpu.roll(found[8 * z : 8 * z + 8], 4 * down, 1)
            out.append(edges[2 * z] + low * part)
            out.append(edges[2 * z + 1] + high * part)
        return tuple(out)

    def scatter_some(step, edges):
        for u in range(UNROLL):
            edges = scatter(step * UNROLL + u, edges)
        return edges

    edges = lax.fori_loop(0, BLOCKS // UNROLL, scatter_some, (zero,) * 12)

    half = jnp.where(lane >= 60, lane - 60, lane)
    pair_of = jnp.where(half >= 2 * STEP, 2, jnp.where(half >= STEP, 1, 0))
    place = half - STEP * pair_of

    for side in range(2):
        total = zero
        for z in range(6):
            part = edges[2 * z + side]
            part = jnp.where(lane < XN, part + pltpu.roll(part, 64, 1), 0.0)
            if edge_row(z):
                part = pltpu.roll(part, edge_row(z), 1)
            total = total + part
        ends[side, 0] = total

    loads[8].wait()
    loads[9].wait()
    flipped = []
    for kind, source in enumerate((mask_ref, friction_ref)):
        for z in range(4):
            value = source[z].astype(F32)
            classes[kind, pl.ds(edge_row(z + 1) + 1, 16), :] = value
            planes[kind, z] = pltpu.roll(value, 8, 1, stride=8, stride_axis=0)
        flipped.append(classes[kind].T)
        for z in range(4):
            classes[kind, pl.ds(edge_row(z + 1) + 1, 16), :] = planes[kind, z]
    flat = planes.reshape(128, 128)
    sides = [flat[pl.ds(0, 8, stride=16), :], flat[pl.ds(15, 8, stride=16), :]]
    tail = jnp.zeros((6, 128), F32)
    for side, y in ((0, 0), (1, 127)):
        ends[side, 1] = jnp.concatenate([flipped[0][y : y + 1], flipped[1][y : y + 1], tail], 0)

    loads[10].wait()
    count = jnp.int32(0)
    order = []
    for b in range(BLOCKS):
        across = tile_ref[b] & 31
        touches = jnp.where((across == 0) | (across == 31), 1, 0)
        order.append((touches, count))
        count = count + touches
    listed[0] = count
    for k in range(BLOCKS):
        at = jnp.int32(0)
        for b in range(k, BLOCKS):
            touches, before = order[b]
            at = at + jnp.where(before == k, b * touches, 0)
        listed[k + 1] = at

    for dz in (-1, 1):
        pair = Z_PAIR[dz]
        grid[pair, pl.ds(PLANE, 4)] = planes[:, Z_PLANE[dz]].reshape(4, 8, 128)
        grid[pair, LEFT] = sides[0]
        grid[pair, RIGHT] = sides[1]
        here = pair_of == pair
        shift = (-STEP * dz) % 128

        def beside(first, second):
            moved = pltpu.roll(jnp.where(here, second, 0.0), shift, 1)
            return jnp.where(here, first, 0.0) + moved

        both = beside(ends[0, 0], ends[1, 0])
        grid[pair, EDGE_A] = both
        grid[pair, EDGE_B] = both
        for side in range(2):
            ends_z[(1 + dz) // 2, side] = beside(ends[side, 0], ends[side, 1])
    for side in range(2):
        across_x[side, 6] = ends[0, 0]
        across_x[side, 7] = ends[1, 0]
        across_x[side, 8] = sides[side]

    for pair in range(3):
        total = jnp.zeros((XN, 8, 128), F32)
        for b in range(BLOCKS):
            down = lax.shift_right_logical(tile_ref[b], 5) & 3
            total = total + patch[pl.ds(STEP * b + 12 - 4 * down, XN), pair]
        grid[pair, pl.ds(FIRST, XN)] = total
        speed[pair] = total
        across_x[0, pl.ds(2 * pair, 2)] = total[:2]
        across_x[1, pl.ds(2 * pair, 2)] = total[16:]

    pl.semaphore_wait(
        barrier, 26 - 9 * (1 - above.astype(jnp.int32)) - 9 * (1 - below.astype(jnp.int32))
    )
    def send_ends(dy):
        for dz in (1, -1, 0):

            def start(dz=dz):
                for dx in (1, -1, 0):
                    end_sends[-dz, -dx, -dy].start()

            where_z(dz, start)

    pl.when(iy == ny - 1)(lambda: send_ends(1))
    for dz in (1, -1, 0):

        def start(dz=dz):
            for dx in (1, -1, 0):
                if (dz, dx) != (0, 0):
                    grid_sends[-dz, -dx].start()

        where_z(dz, start)
    pl.when(iy != ny - 1)(lambda: send_ends(1))
    send_ends(-1)

    for dz in (0, 1, -1):

        def wait(dz=dz):
            for dx in (-1, 0, 1):
                if (dz, dx) != (0, 0):
                    grid_sends[dz, dx].wait_recv()

        where_z(dz, wait)
    there = {-1: below, 1: above}
    for dx in (-1, 1):
        came = got_x.at[(1 - dx) // 2]
        xs = pl.ds(8 + 8 * dx, 2)
        speed[:, xs] = speed[:, xs] + came[pl.ds(0, 6)].reshape(3, 2, 8, 128)
    for dz in (-1, 1):
        pair = Z_PAIR[dz]
        came = got_z[(1 - dz) // 2, pl.ds(FIRST, XN)]
        parts = [got_zx[1 - dz + (1 - dx) // 2, pl.ds(0 if dx == -1 else 2, 2)] for dx in (-1, 1)]
        came = jnp.concatenate(
            [came[:2] + parts[0], came[2:16], came[16:] + parts[1]], 0
        )
        speed[pair] = speed[pair] + jnp.where(there[dz], came, 0.0)
    for kind in range(2):
        for dx, x, mark in ((-1, 0, 3), (1, 17, 0)):
            for z in range(4):
                classes[kind, pl.ds(edge_row(z + 1) + x, 1), :] = got_x[
                    (1 - dx) // 2, 8, pl.ds(4 * kind + z, 1), :
                ]
            for dz in (-1, 1):
                classes[kind, pl.ds(edge_row(0 if dz == -1 else 5) + x, 1), :] = got_zx[
                    1 - dz + (1 - dx) // 2, mark, pl.ds(4 * kind + Z_PLANE[-dz], 1), :
                ]
        for dz in (-1, 1):
            classes[kind, pl.ds(edge_row(0 if dz == -1 else 5) + 1, 16), :] = got_z[
                (1 - dz) // 2, pl.ds(PLANE + 2 * kind, 2)
            ].reshape(16, 128)

    columns = []
    for kind in range(2):
        flipped = classes[kind].T
        for y in (0, 127):
            value = jnp.zeros((1, 128), F32)
            for x in range(16):
                at = (y + 8 * x) & 127
                value = jnp.where((place[:1] & 15) == x, flipped[at : at + 1], value)
            columns.append(value)
    bvel = [bvel_ref[i] for i in range(3)]
    rows = speed.reshape(3 * XN * 8, 128)
    for z in range(6):
        pair, low = z // 2, z % 2

        def at(c):
            return pl.ds(pair * XN * 8 + 2 * c + low, XN, stride=8)

        load = [rows[at(c), :] for c in range(4)]
        kinds = [classes[kind, pl.ds(edge_row(z), XN), :] for kind in range(2)]
        new = contact(load[0], load[1:], kinds[0], kinds[1], bvel)
        for i in range(3):
            value = new[i]
            if z == 0:
                value = jnp.where(below, value, 0.0)
            elif z == 5:
                value = jnp.where(above, value, 0.0)
            rows[at(i + 1), :] = value

    def gather(b):
        lanes, row, cell, frac, alive, down, across = particle(
            b, tile_ref, live_ref, cells_ref, offsets_ref
        )
        start = place_of(down, across)
        group = lax.shift_right_logical((lane - start) & 127, 3)
        back = (128 - start) & 127
        high, low = [], []
        for pair in range(3):
            value = speed[pair, pl.ds(4 * down, 6)]
            part = value[5]
            for i in range(5):
                part = jnp.where(group == i, value[i], part)
            part = jnp.where(lane < 48, pltpu.roll(part, back, 1), 0.0)
            rounded = part.astype(BF16).astype(F32)
            high.append(rounded + pltpu.roll(rounded, 64, 1))
            low.append(part - rounded)
        found = dot(jnp.concatenate(high + low, 0).astype(BF16), weights[b], NN)
        found = found[:24] + found[24:]
        wz, wz_moment = along_z(cell, frac[0])
        totals = [zero] * 4
        for pair in range(3):
            rows_of = slice(8 * pair, 8 * pair + 8)
            plain = found[rows_of, :128]
            totals[0] = totals[0] + wz[pair] * plain
            totals[1] = totals[1] + wz_moment[pair] * plain
            totals[2] = totals[2] + wz[pair] * found[rows_of, 128:256]
            totals[3] = totals[3] + wz[pair] * found[rows_of, 256:]
        totals = [(t + pltpu.roll(t, 7, 0)) * alive for t in totals]
        for i in range(3):
            here = 2 * i + 2
            moved = totals[0][here : here + 1]
            out_velocity[pl.ds(i, 1), lanes] = moved
            out_offsets[pl.ds(i, 1), lanes] = frac[i][:1] * alive + DT * moved
            for j in range(3):
                out_affine[pl.ds(3 * i + j, 1), lanes] = 4.0 * totals[j + 1][here : here + 1]

    def gather_some(step, carry):
        for u in range(UNROLL):
            gather(step * UNROLL + u)
        return carry

    lax.fori_loop(0, BLOCKS // UNROLL, gather_some, 0)

    inner = lane < 120
    for dz in (0, 1, -1):

        def wait(dz=dz):
            for dx in (-1, 0, 1):
                for dy in (-1, 1):
                    end_sends[dz, dx, dy].wait_recv()

        where_z(dz, wait)
    totals = [ends[0, 0], ends[1, 0]]
    marks = [zero, zero]
    for dz, dx in NINE:
        keep = inner
        if dx == -1:
            keep = keep & (place < 2)
        elif dx == 1:
            keep = keep & (place >= 16) & (place < 18)
        if dz == -1:
            keep = keep & (pair_of == 0) & below
        elif dz == 1:
            keep = keep & (pair_of == 2) & above
        shift = 16 * dx + 2 * STEP * dz

        def moved(value, second=False):
            shift_by = (shift - STEP * dz if second else shift) % 128
            return jnp.where(keep, pltpu.roll(value, shift_by, 1) if shift_by else value, 0.0)

        if dz:
            if dx == 0:
                came = got_z[(1 - dz) // 2, EDGE_A]
            else:
                came = got_zx[1 - dz + (1 - dx) // 2, 2 if dx == -1 else 1]
            totals[0] = totals[0] + moved(came)
            totals[1] = totals[1] + moved(came, True)
        elif dx:
            for side in range(2):
                totals[side] = totals[side] + moved(got_x[(1 - dx) // 2, 6 + side])
        for dy in (-1, 1):
            side = (1 + dy) // 2
            came = got_ends.at[1 - side, SLOT[-dz, -dx]]
            totals[side] = totals[side] + moved(came[0])
            marks[side] = marks[side] + (moved(came[0], True) if dz else moved(came[1]))
    kinds = [
        jnp.concatenate(
            [
                marks[0][kind : kind + 1],
                columns[2 * kind],
                columns[2 * kind + 1],
                marks[1][kind : kind + 1],
            ],
            0,
        )
        for kind in range(2)
    ]
    parts = [
        jnp.concatenate([totals[0][2 * c : 2 * c + 2], totals[1][2 * c : 2 * c + 2]], 0)
        for c in range(4)
    ]
    new = contact(parts[0], parts[1:], kinds[0], kinds[1], bvel)
    first_row, last_row = edge_row(0), edge_row(5)
    here = lane[:4]
    outside = ((here < first_row + STEP) & (iz == 0)) | ((here >= last_row) & (iz == nz - 1))
    new = [jnp.where(outside, 0.0, value) for value in new]
    for side in range(2):
        edge_speed[side] = jnp.concatenate(
            [jnp.zeros((2, 128), F32)] + [value[2 * side : 2 * side + 2] for value in new], 0
        )

    for dz in (-1, 0, 1):

        def finish(dz=dz):
            for dx in (-1, 0, 1):
                if (dz, dx) != (0, 0):
                    grid_sends[-dz, -dx].wait_send()
                for dy in (-1, 1):
                    end_sends[-dz, -dx, -dy].wait_send()

        where_z(dz, finish)


def finish(
    tile_ref,
    live_ref,
    cells_ref,
    offsets_ref,
    velocity_ref,
    affine_ref,
    moved_ref,
    edge_speed,
    listed,
    out_velocity,
    out_affine,
    out_offsets,
):
    out_velocity[...] = velocity_ref[...]
    out_affine[...] = affine_ref[...]
    out_offsets[...] = moved_ref[...]

    def one(k, carry):
        b = listed[k + 1]
        lanes, row, cell, frac, alive, down, across = particle(
            b, tile_ref, live_ref, cells_ref, offsets_ref
        )
        side = jnp.where(across == 0, 0, 1)
        value = edge_speed[side]
        left = jnp.concatenate(
            [pltpu.roll(value, (128 - edge_row(z) - 4 * down) & 127, 1) for z in range(6)], 0
        )
        left_high, left_low = split(left)
        right = jnp.concatenate(
            [along_x_rows(cell, frac[1]), jnp.zeros((120, 256), F32)], 0
        )
        right_high, right_low = split(right)
        found = dot(left_high, right_high, NN) + (
            dot(left_low, right_high, NN) + dot(left_high, right_low, NN)
        )
        we, we_moment = along_edge(cell, frac[2], across)
        wz, wz_moment = six(near_z(cell), *spline(frac[0]))
        sum_w = sum(wz[z] * found[8 * z : 8 * z + 8, :128] for z in range(6))
        sum_z = sum(wz_moment[z] * found[8 * z : 8 * z + 8, :128] for z in range(6))
        sum_x = sum(wz[z] * found[8 * z : 8 * z + 8, 128:] for z in range(6))
        totals = [we * sum_w, we * sum_z, we * sum_x, we_moment * sum_w]
        totals = [(t + pltpu.roll(t, 7, 0)) * alive for t in totals]
        for i in range(3):
            here = 2 * i + 2
            moved = totals[0][here : here + 1]
            out_velocity[pl.ds(i, 1), lanes] += moved
            out_offsets[pl.ds(i, 1), lanes] += DT * moved
            for j in range(3):
                out_affine[pl.ds(3 * i + j, 1), lanes] += (
                    4.0 * totals[j + 1][here : here + 1]
                )
        return carry

    lax.fori_loop(0, listed[0], one, 0)


def on_device(
    cells,
    offsets,
    velocity,
    affine,
    stress,
    mass,
    block_tile,
    live_blocks,
    bucket_mask,
    friction_class,
    bucket_velocity,
):
    hbm = pl.BlockSpec(memory_space=pltpu.HBM)
    vmem = pl.BlockSpec(memory_space=pltpu.VMEM)
    smem = pl.BlockSpec(memory_space=pltpu.SMEM)
    count = cells.shape[0]
    args = (
        block_tile,
        live_blocks,
        bucket_velocity,
        cells.reshape(BLOCKS, 128),
        offsets,
        velocity,
        affine,
        stress,
        mass.reshape(BLOCKS, 128),
        bucket_mask,
        friction_class,
    )
    kept = pl.pallas_call(
        spread,
        out_shape=(
            pltpu.SMEM((BLOCKS,), jnp.int32),
            pltpu.SMEM((1,), jnp.int32),
            pltpu.VMEM((BLOCKS, 128), jnp.int32),
            pltpu.VMEM((3, count), F32),
            pltpu.VMEM((3, count), F32),
            pltpu.VMEM((9, count), F32),
            pltpu.VMEM((3, count), F32),
            pltpu.VMEM((2, 8, 128), F32),
            pltpu.SMEM((BLOCKS + 1,), jnp.int32),
        ),
        in_specs=[hbm] * len(args),
        out_specs=(smem,) * 2 + (vmem,) * 6 + (smem,),
        scratch_shapes=[pltpu.SMEM((3,), F32)]
        + [pltpu.VMEM(arg.shape, arg.dtype) for arg in args[5:]]
        + [
            pltpu.VMEM((BLOCKS, 128, 384), BF16),
            pltpu.VMEM((STEP * BLOCKS + 12, 3, 8, 128), F32),
            pltpu.VMEM((3, TILES, 8, 128), F32),
            pltpu.VMEM((2, 9, 8, 128), F32),
            pltpu.VMEM((3, XN, 8, 128), F32),
            pltpu.VMEM((2, 2, 8, 128), F32),
            pltpu.VMEM((2, 2, 8, 128), F32),
            pltpu.VMEM((2, 128, 128), F32),
            pltpu.VMEM((2, 4, 16, 128), F32),
            pltpu.VMEM((2, EDGE_B, 8, 128), F32),
            pltpu.VMEM((2, 9, 8, 128), F32),
            pltpu.VMEM((4, 4, 8, 128), F32),
            pltpu.VMEM((2, len(NINE), 2, 8, 128), F32),
            pltpu.SemaphoreType.DMA((len(args),)),
            pltpu.SemaphoreType.DMA((26,)),
            pltpu.SemaphoreType.DMA((26,)),
        ],
        compiler_params=pltpu.CompilerParams(
            collective_id=0, has_side_effects=True, vmem_limit_bytes=VMEM_SPREAD
        ),
    )(*args)
    return pl.pallas_call(
        finish,
        out_shape=(
            jax.ShapeDtypeStruct((3, count), F32),
            jax.ShapeDtypeStruct((9, count), F32),
            jax.ShapeDtypeStruct((3, count), F32),
        ),
        in_specs=[smem] * 2 + [vmem] * 6 + [smem],
        out_specs=(vmem,) * 3,
        compiler_params=pltpu.CompilerParams(vmem_limit_bytes=VMEM_FINISH),
    )(*kept)


def solution(mesh):
    along = ("gx", "gy", "gz")
    return jax.shard_map(
        on_device,
        mesh=mesh,
        in_specs=(
            P(along),
            P(None, along),
            P(None, along),
            P(None, along),
            P(None, along),
            P(along),
            P(along),
            P(along),
            P("gz", "gx", "gy"),
            P("gz", "gx", "gy"),
            P(),
        ),
        out_specs=(P(None, along), P(None, along), P(None, along)),
        check_vma=False,
    )
```

```python
import jax
import jax.numpy as jnp
from jax import lax
from jax.experimental import pallas as pl
from jax.experimental.pallas import tpu as pltpu
from jax.sharding import PartitionSpec as P

DT = 0.1
GRAVITY = -9.8
MASS_FLOOR = 0.5
SLIP_FLOOR = 0.1
FRICTION = (0.1, 0.4, 0.8, 1.2)

BLOCKS = 16
VMEM_SPREAD = 58 * 1024 * 1024
VMEM_FINISH = 16 * 1024 * 1024
XN = 18
STEP = 20
F32 = jnp.float32
BF16 = jnp.bfloat16
MESH = pl.DeviceIdType.MESH

PLANE, LEFT, EDGE_A, FIRST, EDGE_B, RIGHT, TILES = 0, 4, 5, 6, 24, 25, 26

FACES = [(dz, dx) for dz in (-1, 0, 1) for dx in (-1, 0, 1) if (dz, dx) != (0, 0)]
NINE = [(dz, dx) for dz in (-1, 1, 0) for dx in (-1, 1, 0)]
SLOT = {side: index for index, side in enumerate(NINE)}
Z_PLANE = {-1: 0, 1: 3}
Z_PAIR = {-1: 0, 1: 2}


def spline(frac):
    weights = (
        0.5 * (1.5 - frac) * (1.5 - frac),
        0.75 - (frac - 1.0) * (frac - 1.0),
        0.5 * (frac - 0.5) * (frac - 0.5),
    )
    moments = tuple(w * (float(k) - frac) for k, w in enumerate(weights))
    return weights, moments


def pick(hits, values):
    out = jnp.where(hits[2], values[2], 0.0)
    out = jnp.where(hits[1], values[1], out)
    return jnp.where(hits[0], values[0], out)


def split(value):
    high = value.astype(BF16)
    return high, (value - high.astype(F32)).astype(BF16)


def along_z(cell, frac):
    low = lax.broadcasted_iota(jnp.int32, (8, 128), 0) & 1
    near = lax.shift_right_logical(cell, 4) - low
    weights, moments = spline(frac)
    plain, moment = [], []
    for pair in range(3):
        hits = [near == 2 * pair - k for k in range(3)]
        plain.append(pick(hits, weights))
        moment.append(pick(hits, moments))
    return plain, moment


def six(near, weights, moments):
    hits = [near == v for v in range(4)]
    plain, moment = [], []
    for i in range(6):
        outs = []
        for values in (weights, moments):
            out = jnp.zeros((8, 128), F32)
            for k in range(3):
                if 0 <= i - k < 4:
                    out = jnp.where(hits[i - k], values[k], out)
            outs.append(out)
        plain.append(outs[0])
        moment.append(outs[1])
    return plain, moment


def near_z(cell):
    return lax.shift_right_logical(cell, 4)


def near_x(cell):
    return lax.shift_right_logical(cell, 2) & 3


def along_x_rows(cell, frac):
    row = lax.broadcasted_iota(jnp.int32, (8, 128), 0)
    weights, moments = spline(frac)
    hits = [row - near_x(cell) == k for k in range(3)]
    return jnp.concatenate([pick(hits, weights), pick(hits, moments)], 1)


def along_edge(cell, frac, across):
    row = lax.broadcasted_iota(jnp.int32, (8, 128), 0)
    first = jnp.where(across == 0, 0, jnp.where(across == 31, 4, -999))
    place = (row & 1) - (cell & 3) + first
    weights, moments = spline(frac)
    hits = [place == k for k in range(3)]
    return pick(hits, weights), pick(hits, moments)


def along_y(cell, frac, across):
    row = lax.broadcasted_iota(jnp.int32, (8, 128), 0)
    first = jnp.where(across == 0, 2, 0)
    last = jnp.where(across == 31, 4, 6)
    place = jnp.where((row >= first) & (row < last), row - (cell & 3), -9)
    weights, moments = spline(frac)
    hits = [place == k for k in range(3)]
    return pick(hits, weights), pick(hits, moments)


def by_channel(parts):
    row = lax.broadcasted_iota(jnp.int32, (8, 128), 0)
    out = jnp.where(row < 6, parts[2], parts[3])
    out = jnp.where(row < 4, parts[1], out)
    return jnp.where(row < 2, parts[0], out)


def dot(left, right, dims):
    return lax.dot_general(left, right, (dims, ((), ())), preferred_element_type=F32)


NN = ((1,), (0,))
NT = ((1,), (1,))


def contact(mass, momentum, kind, friction, bvel):
    floor = jnp.maximum(mass, MASS_FLOOR)
    speed = [momentum[0] / floor + DT * GRAVITY, momentum[1] / floor, momentum[2] / floor]
    coeff = jnp.where(friction == 3.0, FRICTION[3], 0.0)
    for level in range(3):
        coeff = jnp.where(friction == float(level), FRICTION[level], coeff)
    rel = [speed[i] - bvel[i] for i in range(3)]
    normal = jnp.minimum(rel[0], 0.0)
    slide = jnp.sqrt(rel[1] * rel[1] + rel[2] * rel[2])
    factor = jnp.maximum(0.0, 1.0 + coeff * normal / jnp.maximum(slide, SLIP_FLOOR))
    hit = [bvel[0] + (rel[0] - normal), bvel[1] + factor * rel[1], bvel[2] + factor * rel[2]]
    return [
        jnp.where(kind == 2.0, bvel[i], jnp.where(kind == 1.0, hit[i], speed[i])) for i in range(3)
    ]


def particle(b, tile_ref, live_ref, cells_ref, offsets_ref):
    lanes = pl.ds(b * 128 if isinstance(b, int) else pl.multiple_of(b * 128, 128), 128)

    def row(ref, r):
        return jnp.broadcast_to(ref[pl.ds(r, 1), lanes], (8, 128))

    cell = jnp.broadcast_to(cells_ref[pl.ds(b, 1), :], (8, 128))
    frac = [row(offsets_ref, r) for r in range(3)]
    alive = jnp.where(b < live_ref[0], 1.0, 0.0)
    tile = tile_ref[b]
    return lanes, row, cell, frac, alive, lax.shift_right_logical(tile, 5) & 3, tile & 31


def place_of(down, across):
    return (32 * down + 4 * across + 127) & 127


def weights_xy(cell, frac, across):
    weights, moments = spline(frac[1])
    wx, wx_moment = six(near_x(cell), weights, moments)
    wy, wy_moment = along_y(cell, frac[2], across)
    value = jnp.concatenate(
        [
            jnp.concatenate([wx[i] * wy for i in range(6)], 0),
            jnp.concatenate([wx_moment[i] * wy for i in range(6)], 0),
            jnp.concatenate([wx[i] * wy_moment for i in range(6)], 0),
        ],
        1,
    )
    high, low = split(value)
    pad = jnp.zeros((16, 384), BF16)
    return jnp.concatenate([high, pad, low, pad], 0)


def edge_row(z):
    return 60 * (z % 2) + STEP * (z // 2)


def spread(
    tile_hbm,
    live_hbm,
    bvel_hbm,
    cells_hbm,
    offsets_hbm,
    velocity_hbm,
    affine_hbm,
    stress_hbm,
    mass_hbm,
    mask_hbm,
    friction_hbm,
    tile_ref,
    live_ref,
    cells_ref,
    offsets_ref,
    out_velocity,
    out_affine,
    out_offsets,
    edge_speed,
    listed,
    bvel_ref,
    velocity_ref,
    affine_ref,
    stress_ref,
    mass_ref,
    mask_ref,
    friction_ref,
    weights,
    patch,
    grid,
    across_x,
    speed,
    ends,
    ends_z,
    classes,
    planes,
    got_z,
    got_x,
    got_zx,
    got_ends,
    load_sem,
    send_sem,
    recv_sem,
):
    loads = [
        pltpu.make_async_copy(source, target, load_sem.at[index])
        for index, (source, target) in enumerate(
            (
                (cells_hbm, cells_ref),
                (offsets_hbm, offsets_ref),
                (tile_hbm, tile_ref),
                (live_hbm, live_ref),
                (mass_hbm, mass_ref),
                (velocity_hbm, velocity_ref),
                (affine_hbm, affine_ref),
                (stress_hbm, stress_ref),
                (mask_hbm, mask_ref),
                (friction_hbm, friction_ref),
                (bvel_hbm, bvel_ref),
            )
        )
    ]
    ix, iy, iz = lax.axis_index("gx"), lax.axis_index("gy"), lax.axis_index("gz")
    nx, ny, nz = lax.axis_size("gx"), lax.axis_size("gy"), lax.axis_size("gz")
    above, below = iz < nz - 1, iz > 0

    def beside_of(i, n):
        return {-1: jnp.where(i == 0, n - 1, i - 1), 0: i, 1: jnp.where(i == n - 1, 0, i + 1)}

    at_x, at_y, at_z = beside_of(ix, nx), beside_of(iy, ny), beside_of(iz, nz)

    def device(dz, dx, dy):
        return {"gx": at_x[dx], "gy": at_y[dy], "gz": at_z[dz]}

    def where_z(dz, action):
        if dz == 0:
            action()
        else:
            pl.when(above if dz == 1 else below)(action)

    barrier = pltpu.get_barrier_semaphore()

    def greet(dz, dys):
        for dy in dys:
            for dx in (-1, 1, 0):
                if (dz, dx, dy) != (0, 0, 0):
                    pl.semaphore_signal(
                        barrier, inc=1, device_id=device(dz, dx, dy), device_id_type=MESH
                    )

    for dz in (1, 0, -1):
        where_z(dz, lambda dz=dz: greet(dz, (1,)))
    for load in loads:
        load.start()
    for dz in (1, 0, -1):
        where_z(dz, lambda dz=dz: greet(dz, (-1, 0)))

    counter = iter(range(26))

    def sender(src, dst, dz, dx, dy):
        slot = next(counter)
        return pltpu.make_async_remote_copy(
            src_ref=src,
            dst_ref=dst,
            send_sem=send_sem.at[slot],
            recv_sem=recv_sem.at[slot],
            device_id=device(dz, dx, dy),
            device_id_type=MESH,
        )

    grid_sends, end_sends = {}, {}
    for dz, dx in FACES:
        if dz == 0:
            side = (1 + dx) // 2
            src, dst = across_x.at[side], got_x.at[side]
        elif dx == 0:
            src = grid.at[Z_PAIR[dz], pl.ds(PLANE, EDGE_B)]
            dst = got_z.at[(1 + dz) // 2]
        else:
            src = grid.at[Z_PAIR[dz], pl.ds(LEFT if dx == -1 else EDGE_B - 2, 4)]
            dst = got_zx.at[1 + dz + (1 + dx) // 2]
        grid_sends[-dz, -dx] = sender(src, dst, dz, dx, 0)
    for dz, dx in NINE:
        for dy in (-1, 1):
            side = (1 + dy) // 2
            if dz == 0:
                src, dst = ends.at[side], got_ends.at[side, SLOT[dz, dx]]
            else:
                src = ends_z.at[(1 + dz) // 2, side]
                dst = got_ends.at[side, SLOT[dz, dx], 0]
            end_sends[-dz, -dx, -dy] = sender(src, dst, dz, dx, dy)

    speed[...] = jnp.zeros((3, XN, 8, 128), F32)
    classes[...] = jnp.zeros((2, 128, 128), F32)
    patch[pl.ds(0, 12)] = jnp.zeros((12, 3, 8, 128), F32)

    def clear(b, carry):
        patch[pl.ds(STEP * b + 18, 14)] = jnp.zeros((14, 3, 8, 128), F32)
        return carry

    lax.fori_loop(0, BLOCKS, clear, 0)
    for load in loads:
        load.wait()

    zero = jnp.zeros((8, 128), F32)
    lane = lax.broadcasted_iota(jnp.int32, (8, 128), 1)

    flipped = []
    for kind, source in enumerate((mask_ref, friction_ref)):
        for z in range(4):
            value = source[z].astype(F32)
            classes[kind, pl.ds(edge_row(z + 1) + 1, 16), :] = value
            planes[kind, z] = pltpu.roll(value, 8, 1, stride=8, stride_axis=0)
        flipped.append(classes[kind].T)
        for z in range(4):
            classes[kind, pl.ds(edge_row(z + 1) + 1, 16), :] = planes[kind, z]
    flat = planes.reshape(128, 128)
    sides = [flat[pl.ds(0, 8, stride=16), :], flat[pl.ds(15, 8, stride=16), :]]

    def scatter(b, edges):
        lanes, row, cell, frac, alive, down, across = particle(
            b, tile_ref, live_ref, cells_ref, offsets_ref
        )
        right = weights_xy(cell, frac, across)
        weights[b] = right
        wz, wz_moment = along_z(cell, frac[0])
        mass = jnp.broadcast_to(mass_ref[pl.ds(b, 1), :], (8, 128)) * alive
        push = by_channel([mass] + [mass * row(velocity_ref, i) for i in range(3)])
        scale = 4.0 * DT * alive

        def twist(j):
            return mass * by_channel(
                [zero] + [row(affine_ref, 3 * i + j) for i in range(3)]
            ) - scale * by_channel([zero] + [row(stress_ref, 3 * i + j) for i in range(3)])

        twists = [twist(j) for j in range(3)]
        left = jnp.concatenate(
            [
                jnp.concatenate([wz[p] * push + wz_moment[p] * twists[0] for p in range(3)], 0),
                jnp.concatenate([wz[p] * twists[1] for p in range(3)], 0),
                jnp.concatenate([wz[p] * twists[2] for p in range(3)], 0),
            ],
            1,
        )
        found = dot(jnp.concatenate(split(left), 0), right, NT)
        found = found[:24] + found[24:]
        start = place_of(down, across)
        group = lax.shift_right_logical((lane - start) & 127, 3)
        for pair in range(3):
            part = found[8 * pair : 8 * pair + 8]
            part = jnp.where(lane < 48, part + pltpu.roll(part, 64, 1), 0.0)
            part = pltpu.roll(part, start, 1)
            for i in range(6):
                patch[STEP * b + 12 + i, pair] = jnp.where(group == i, part, 0.0)

        we, we_moment = along_edge(cell, frac[2], across)
        lead = we * push + we_moment * twists[2]
        second = we * twists[0]
        third = we * twists[1]
        wz, wz_moment = six(near_z(cell), *spline(frac[0]))
        plain = [wz[z] * lead + wz_moment[z] * second for z in range(6)]
        moment = [wz[z] * third for z in range(6)]
        left = jnp.concatenate([jnp.concatenate(plain, 0), jnp.concatenate(moment, 0)], 1)
        across_x = along_x_rows(cell, frac[1])
        across_high = across_x.astype(BF16).astype(F32)
        pad = jnp.zeros((56, 256), F32)
        right = jnp.concatenate([across_high, pad, across_x - across_high, pad], 0).astype(BF16)
        found = dot(jnp.concatenate(split(left), 0), right, NT)
        found = found[:48] + found[48:]
        low = jnp.where(across == 0, 1.0, 0.0)
        high = jnp.where(across == 31, 1.0, 0.0)
        out = []
        for z in range(6):
            part = pltpu.roll(found[8 * z : 8 * z + 8], 4 * down, 1)
            out.append(edges[2 * z] + low * part)
            out.append(edges[2 * z + 1] + high * part)
        return tuple(out)

    edges = (zero,) * 12
    for b in range(BLOCKS):
        edges = scatter(b, edges)

    half = jnp.where(lane >= 60, lane - 60, lane)
    pair_of = jnp.where(half >= 2 * STEP, 2, jnp.where(half >= STEP, 1, 0))
    place = half - STEP * pair_of

    for side in range(2):
        total = zero
        for z in range(6):
            part = edges[2 * z + side]
            part = jnp.where(lane < XN, part + pltpu.roll(part, 64, 1), 0.0)
            if edge_row(z):
                part = pltpu.roll(part, edge_row(z), 1)
            total = total + part
        ends[side, 0] = total

    tail = jnp.zeros((6, 128), F32)
    for side, y in ((0, 0), (1, 127)):
        ends[side, 1] = jnp.concatenate([flipped[0][y : y + 1], flipped[1][y : y + 1], tail], 0)

    for dz in (-1, 1):
        pair = Z_PAIR[dz]
        grid[pair, pl.ds(PLANE, 4)] = planes[:, Z_PLANE[dz]].reshape(4, 8, 128)
        grid[pair, LEFT] = sides[0]
        grid[pair, RIGHT] = sides[1]
        here = pair_of == pair
        shift = (-STEP * dz) % 128

        def beside(first, second):
            moved = pltpu.roll(jnp.where(here, second, 0.0), shift, 1)
            return jnp.where(here, first, 0.0) + moved

        both = beside(ends[0, 0], ends[1, 0])
        grid[pair, EDGE_A] = both
        grid[pair, EDGE_B] = both
        for side in range(2):
            ends_z[(1 + dz) // 2, side] = beside(ends[side, 0], ends[side, 1])
    for side in range(2):
        across_x[side, 6] = ends[0, 0]
        across_x[side, 7] = ends[1, 0]
        across_x[side, 8] = sides[side]

    for pair in range(3):
        total = jnp.zeros((XN, 8, 128), F32)
        for b in range(BLOCKS):
            down = lax.shift_right_logical(tile_ref[b], 5) & 3
            total = total + patch[pl.ds(STEP * b + 12 - 4 * down, XN), pair]
        grid[pair, pl.ds(FIRST, XN)] = total
        speed[pair] = total
        across_x[0, pl.ds(2 * pair, 2)] = total[:2]
        across_x[1, pl.ds(2 * pair, 2)] = total[16:]

    pl.semaphore_wait(
        barrier, 26 - 9 * (1 - above.astype(jnp.int32)) - 9 * (1 - below.astype(jnp.int32))
    )
    def send_ends(dy):
        for dz in (1, -1, 0):

            def start(dz=dz):
                for dx in (1, -1, 0):
                    end_sends[-dz, -dx, -dy].start()

            where_z(dz, start)

    send_ends(1)
    send_ends(-1)
    for dz in (1, -1, 0):

        def start(dz=dz):
            for dx in (1, -1, 0):
                if (dz, dx) != (0, 0):
                    grid_sends[-dz, -dx].start()

        where_z(dz, start)
    count = jnp.int32(0)
    order = []
    for b in range(BLOCKS):
        across = tile_ref[b] & 31
        touches = jnp.where((across == 0) | (across == 31), 1, 0)
        order.append((touches, count))
        count = count + touches
    listed[0] = count
    for k in range(BLOCKS):
        at = jnp.int32(0)
        for b in range(k, BLOCKS):
            touches, before = order[b]
            at = at + jnp.where(before == k, b * touches, 0)
        listed[k + 1] = at

    for dz in (0, 1, -1):

        def wait(dz=dz):
            for dx in (-1, 0, 1):
                if (dz, dx) != (0, 0):
                    grid_sends[dz, dx].wait_recv()

        where_z(dz, wait)
    there = {-1: below, 1: above}
    for dx in (-1, 1):
        came = got_x.at[(1 - dx) // 2]
        xs = pl.ds(8 + 8 * dx, 2)
        speed[:, xs] = speed[:, xs] + came[pl.ds(0, 6)].reshape(3, 2, 8, 128)
    for dz in (-1, 1):
        pair = Z_PAIR[dz]
        came = got_z[(1 - dz) // 2, pl.ds(FIRST, XN)]
        parts = [got_zx[1 - dz + (1 - dx) // 2, pl.ds(0 if dx == -1 else 2, 2)] for dx in (-1, 1)]
        came = jnp.concatenate(
            [came[:2] + parts[0], came[2:16], came[16:] + parts[1]], 0
        )
        speed[pair] = speed[pair] + jnp.where(there[dz], came, 0.0)
    for kind in range(2):
        for dx, x, mark in ((-1, 0, 3), (1, 17, 0)):
            for z in range(4):
                classes[kind, pl.ds(edge_row(z + 1) + x, 1), :] = got_x[
                    (1 - dx) // 2, 8, pl.ds(4 * kind + z, 1), :
                ]
            for dz in (-1, 1):
                classes[kind, pl.ds(edge_row(0 if dz == -1 else 5) + x, 1), :] = got_zx[
                    1 - dz + (1 - dx) // 2, mark, pl.ds(4 * kind + Z_PLANE[-dz], 1), :
                ]
        for dz in (-1, 1):
            classes[kind, pl.ds(edge_row(0 if dz == -1 else 5) + 1, 16), :] = got_z[
                (1 - dz) // 2, pl.ds(PLANE + 2 * kind, 2)
            ].reshape(16, 128)

    columns = []
    for kind in range(2):
        flipped = classes[kind].T
        for y in (0, 127):
            value = jnp.zeros((1, 128), F32)
            for x in range(16):
                at = (y + 8 * x) & 127
                value = jnp.where((place[:1] & 15) == x, flipped[at : at + 1], value)
            columns.append(value)
    bvel = [bvel_ref[i] for i in range(3)]
    rows = speed.reshape(3 * XN * 8, 128)
    for z in range(6):
        pair, low = z // 2, z % 2

        def at(c):
            return pl.ds(pair * XN * 8 + 2 * c + low, XN, stride=8)

        load = [rows[at(c), :] for c in range(4)]
        kinds = [classes[kind, pl.ds(edge_row(z), XN), :] for kind in range(2)]
        new = contact(load[0], load[1:], kinds[0], kinds[1], bvel)
        for i in range(3):
            value = new[i]
            if z == 0:
                value = jnp.where(below, value, 0.0)
            elif z == 5:
                value = jnp.where(above, value, 0.0)
            rows[at(i + 1), :] = value

    def gather(b):
        lanes, row, cell, frac, alive, down, across = particle(
            b, tile_ref, live_ref, cells_ref, offsets_ref
        )
        start = place_of(down, across)
        group = lax.shift_right_logical((lane - start) & 127, 3)
        back = (128 - start) & 127
        high, low = [], []
        for pair in range(3):
            value = speed[pair, pl.ds(4 * down, 6)]
            part = value[5]
            for i in range(5):
                part = jnp.where(group == i, value[i], part)
            part = jnp.where(lane < 48, pltpu.roll(part, back, 1), 0.0)
            rounded = part.astype(BF16).astype(F32)
            high.append(rounded + pltpu.roll(rounded, 64, 1))
            low.append(part - rounded)
        found = dot(jnp.concatenate(high + low, 0).astype(BF16), weights[b], NN)
        found = found[:24] + found[24:]
        wz, wz_moment = along_z(cell, frac[0])
        totals = [zero] * 4
        for pair in range(3):
            rows_of = slice(8 * pair, 8 * pair + 8)
            plain = found[rows_of, :128]
            totals[0] = totals[0] + wz[pair] * plain
            totals[1] = totals[1] + wz_moment[pair] * plain
            totals[2] = totals[2] + wz[pair] * found[rows_of, 128:256]
            totals[3] = totals[3] + wz[pair] * found[rows_of, 256:]
        totals = [(t + pltpu.roll(t, 7, 0)) * alive for t in totals]
        for i in range(3):
            here = 2 * i + 2
            moved = totals[0][here : here + 1]
            out_velocity[pl.ds(i, 1), lanes] = moved
            out_offsets[pl.ds(i, 1), lanes] = frac[i][:1] * alive + DT * moved
            for j in range(3):
                out_affine[pl.ds(3 * i + j, 1), lanes] = 4.0 * totals[j + 1][here : here + 1]

    for b in range(BLOCKS):
        gather(b)

    inner = lane < 120
    for dz in (0, 1, -1):

        def wait(dz=dz):
            for dx in (-1, 0, 1):
                for dy in (-1, 1):
                    end_sends[dz, dx, dy].wait_recv()

        where_z(dz, wait)
    totals = [ends[0, 0], ends[1, 0]]
    marks = [zero, zero]
    for dz, dx in NINE:
        keep = inner
        if dx == -1:
            keep = keep & (place < 2)
        elif dx == 1:
            keep = keep & (place >= 16) & (place < 18)
        if dz == -1:
            keep = keep & (pair_of == 0) & below
        elif dz == 1:
            keep = keep & (pair_of == 2) & above
        shift = 16 * dx + 2 * STEP * dz

        def moved(value, second=False):
            shift_by = (shift - STEP * dz if second else shift) % 128
            return jnp.where(keep, pltpu.roll(value, shift_by, 1) if shift_by else value, 0.0)

        if dz:
            if dx == 0:
                came = got_z[(1 - dz) // 2, EDGE_A]
            else:
                came = got_zx[1 - dz + (1 - dx) // 2, 2 if dx == -1 else 1]
            totals[0] = totals[0] + moved(came)
            totals[1] = totals[1] + moved(came, True)
        elif dx:
            for side in range(2):
                totals[side] = totals[side] + moved(got_x[(1 - dx) // 2, 6 + side])
        for dy in (-1, 1):
            side = (1 + dy) // 2
            came = got_ends.at[1 - side, SLOT[-dz, -dx]]
            totals[side] = totals[side] + moved(came[0])
            marks[side] = marks[side] + (moved(came[0], True) if dz else moved(came[1]))
    kinds = [
        jnp.concatenate(
            [
                marks[0][kind : kind + 1],
                columns[2 * kind],
                columns[2 * kind + 1],
                marks[1][kind : kind + 1],
            ],
            0,
        )
        for kind in range(2)
    ]
    parts = [
        jnp.concatenate([totals[0][2 * c : 2 * c + 2], totals[1][2 * c : 2 * c + 2]], 0)
        for c in range(4)
    ]
    new = contact(parts[0], parts[1:], kinds[0], kinds[1], bvel)
    first_row, last_row = edge_row(0), edge_row(5)
    here = lane[:4]
    outside = ((here < first_row + STEP) & (iz == 0)) | ((here >= last_row) & (iz == nz - 1))
    new = [jnp.where(outside, 0.0, value) for value in new]
    for side in range(2):
        edge_speed[side] = jnp.concatenate(
            [jnp.zeros((2, 128), F32)] + [value[2 * side : 2 * side + 2] for value in new], 0
        )

    for dz in (-1, 0, 1):

        def finish(dz=dz):
            for dx in (-1, 0, 1):
                if (dz, dx) != (0, 0):
                    grid_sends[-dz, -dx].wait_send()
                for dy in (-1, 1):
                    end_sends[-dz, -dx, -dy].wait_send()

        where_z(dz, finish)


def finish(
    tile_ref,
    live_ref,
    cells_ref,
    offsets_ref,
    velocity_ref,
    affine_ref,
    moved_ref,
    edge_speed,
    listed,
    out_velocity,
    out_affine,
    out_offsets,
):
    out_velocity[...] = velocity_ref[...]
    out_affine[...] = affine_ref[...]
    out_offsets[...] = moved_ref[...]

    def share(k):
        b = listed[k + 1]
        lanes, row, cell, frac, alive, down, across = particle(
            b, tile_ref, live_ref, cells_ref, offsets_ref
        )
        side = jnp.where(across == 0, 0, 1)
        value = edge_speed[side]
        left = jnp.concatenate(
            [pltpu.roll(value, (128 - edge_row(z) - 4 * down) & 127, 1) for z in range(6)], 0
        )
        left_high, left_low = split(left)
        right = jnp.concatenate(
            [along_x_rows(cell, frac[1]), jnp.zeros((120, 256), F32)], 0
        )
        right_high, right_low = split(right)
        found = dot(left_high, right_high, NN) + (
            dot(left_low, right_high, NN) + dot(left_high, right_low, NN)
        )
        we, we_moment = along_edge(cell, frac[2], across)
        wz, wz_moment = six(near_z(cell), *spline(frac[0]))
        sum_w = sum(wz[z] * found[8 * z : 8 * z + 8, :128] for z in range(6))
        sum_z = sum(wz_moment[z] * found[8 * z : 8 * z + 8, :128] for z in range(6))
        sum_x = sum(wz[z] * found[8 * z : 8 * z + 8, 128:] for z in range(6))
        totals = [we * sum_w, we * sum_z, we * sum_x, we_moment * sum_w]
        used = jnp.where(k < listed[0], alive, 0.0)
        return lanes, [(t + pltpu.roll(t, 7, 0)) * used for t in totals]

    def two(step, carry):
        for lanes, totals in [share(2 * step + u) for u in range(2)]:
            for i in range(3):
                here = 2 * i + 2
                moved = totals[0][here : here + 1]
                out_velocity[pl.ds(i, 1), lanes] += moved
                out_offsets[pl.ds(i, 1), lanes] += DT * moved
                for j in range(3):
                    out_affine[pl.ds(3 * i + j, 1), lanes] += (
                        4.0 * totals[j + 1][here : here + 1]
                    )
        return carry

    lax.fori_loop(0, lax.shift_right_logical(listed[0] + 1, 1), two, 0)


def on_device(
    cells,
    offsets,
    velocity,
    affine,
    stress,
    mass,
    block_tile,
    live_blocks,
    bucket_mask,
    friction_class,
    bucket_velocity,
):
    hbm = pl.BlockSpec(memory_space=pltpu.HBM)
    vmem = pl.BlockSpec(memory_space=pltpu.VMEM)
    smem = pl.BlockSpec(memory_space=pltpu.SMEM)
    count = cells.shape[0]
    args = (
        block_tile,
        live_blocks,
        bucket_velocity,
        cells.reshape(BLOCKS, 128),
        offsets,
        velocity,
        affine,
        stress,
        mass.reshape(BLOCKS, 128),
        bucket_mask,
        friction_class,
    )
    kept = pl.pallas_call(
        spread,
        out_shape=(
            pltpu.SMEM((BLOCKS,), jnp.int32),
            pltpu.SMEM((1,), jnp.int32),
            pltpu.VMEM((BLOCKS, 128), jnp.int32),
            pltpu.VMEM((3, count), F32),
            pltpu.VMEM((3, count), F32),
            pltpu.VMEM((9, count), F32),
            pltpu.VMEM((3, count), F32),
            pltpu.VMEM((2, 8, 128), F32),
            pltpu.SMEM((BLOCKS + 1,), jnp.int32),
        ),
        in_specs=[hbm] * len(args),
        out_specs=(smem,) * 2 + (vmem,) * 6 + (smem,),
        scratch_shapes=[pltpu.SMEM((3,), F32)]
        + [pltpu.VMEM(arg.shape, arg.dtype) for arg in args[5:]]
        + [
            pltpu.VMEM((BLOCKS, 128, 384), BF16),
            pltpu.VMEM((STEP * BLOCKS + 12, 3, 8, 128), F32),
            pltpu.VMEM((3, TILES, 8, 128), F32),
            pltpu.VMEM((2, 9, 8, 128), F32),
            pltpu.VMEM((3, XN, 8, 128), F32),
            pltpu.VMEM((2, 2, 8, 128), F32),
            pltpu.VMEM((2, 2, 8, 128), F32),
            pltpu.VMEM((2, 128, 128), F32),
            pltpu.VMEM((2, 4, 16, 128), F32),
            pltpu.VMEM((2, EDGE_B, 8, 128), F32),
            pltpu.VMEM((2, 9, 8, 128), F32),
            pltpu.VMEM((4, 4, 8, 128), F32),
            pltpu.VMEM((2, len(NINE), 2, 8, 128), F32),
            pltpu.SemaphoreType.DMA((len(args),)),
            pltpu.SemaphoreType.DMA((26,)),
            pltpu.SemaphoreType.DMA((26,)),
        ],
        compiler_params=pltpu.CompilerParams(
            collective_id=0, has_side_effects=True, vmem_limit_bytes=VMEM_SPREAD
        ),
    )(*args)
    return pl.pallas_call(
        finish,
        out_shape=(
            jax.ShapeDtypeStruct((3, count), F32),
            jax.ShapeDtypeStruct((9, count), F32),
            jax.ShapeDtypeStruct((3, count), F32),
        ),
        in_specs=[smem] * 2 + [vmem] * 6 + [smem],
        out_specs=(vmem,) * 3,
        compiler_params=pltpu.CompilerParams(vmem_limit_bytes=VMEM_FINISH),
    )(*kept)


def solution(mesh):
    along = ("gx", "gy", "gz")
    return jax.shard_map(
        on_device,
        mesh=mesh,
        in_specs=(
            P(along),
            P(None, along),
            P(None, along),
            P(None, along),
            P(None, along),
            P(along),
            P(along),
            P(along),
            P("gz", "gx", "gy"),
            P("gz", "gx", "gy"),
            P(),
        ),
        out_specs=(P(None, along), P(None, along), P(None, along)),
        check_vma=False,
    )
```

```python
import jax
import jax.numpy as jnp
from jax import lax
from jax.experimental import pallas as pl
from jax.experimental.pallas import tpu as pltpu
from jax.sharding import PartitionSpec as P

DT = 0.1
GRAVITY = -9.8
MASS_FLOOR = 0.5
SLIP_FLOOR = 0.1
FRICTION = (0.1, 0.4, 0.8, 1.2)

BLOCKS = 16
VMEM_SPREAD = 58 * 1024 * 1024
VMEM_FINISH = 16 * 1024 * 1024
XN = 18
STEP = 20
F32 = jnp.float32
BF16 = jnp.bfloat16
MESH = pl.DeviceIdType.MESH

PLANE, LEFT, EDGE_A, FIRST, EDGE_B, RIGHT, TILES = 0, 4, 5, 6, 24, 25, 26

FACES = [(dz, dx) for dz in (-1, 0, 1) for dx in (-1, 0, 1) if (dz, dx) != (0, 0)]
NINE = [(dz, dx) for dz in (-1, 1, 0) for dx in (-1, 1, 0)]
SLOT = {side: index for index, side in enumerate(NINE)}
Z_PLANE = {-1: 0, 1: 3}
Z_PAIR = {-1: 0, 1: 2}


def spline(frac):
    weights = (
        0.5 * (1.5 - frac) * (1.5 - frac),
        0.75 - (frac - 1.0) * (frac - 1.0),
        0.5 * (frac - 0.5) * (frac - 0.5),
    )
    moments = tuple(w * (float(k) - frac) for k, w in enumerate(weights))
    return weights, moments


def pick(hits, values):
    out = jnp.where(hits[2], values[2], 0.0)
    out = jnp.where(hits[1], values[1], out)
    return jnp.where(hits[0], values[0], out)


def split(value):
    high = value.astype(BF16)
    return high, (value - high.astype(F32)).astype(BF16)


def along_z(cell, frac):
    low = lax.broadcasted_iota(jnp.int32, (8, 128), 0) & 1
    near = lax.shift_right_logical(cell, 4) - low
    weights, moments = spline(frac)
    plain, moment = [], []
    for pair in range(3):
        hits = [near == 2 * pair - k for k in range(3)]
        plain.append(pick(hits, weights))
        moment.append(pick(hits, moments))
    return plain, moment


def six(near, weights, moments):
    hits = [near == v for v in range(4)]
    plain, moment = [], []
    for i in range(6):
        outs = []
        for values in (weights, moments):
            out = jnp.zeros((8, 128), F32)
            for k in range(3):
                if 0 <= i - k < 4:
                    out = jnp.where(hits[i - k], values[k], out)
            outs.append(out)
        plain.append(outs[0])
        moment.append(outs[1])
    return plain, moment


def near_z(cell):
    return lax.shift_right_logical(cell, 4)


def near_x(cell):
    return lax.shift_right_logical(cell, 2) & 3


def along_x_rows(cell, frac):
    row = lax.broadcasted_iota(jnp.int32, (8, 128), 0)
    weights, moments = spline(frac)
    hits = [row - near_x(cell) == k for k in range(3)]
    return jnp.concatenate([pick(hits, weights), pick(hits, moments)], 1)


def along_edge(cell, frac, across):
    row = lax.broadcasted_iota(jnp.int32, (8, 128), 0)
    first = jnp.where(across == 0, 0, jnp.where(across == 31, 4, -999))
    place = (row & 1) - (cell & 3) + first
    weights, moments = spline(frac)
    hits = [place == k for k in range(3)]
    return pick(hits, weights), pick(hits, moments)


def along_y(cell, frac, across):
    row = lax.broadcasted_iota(jnp.int32, (8, 128), 0)
    first = jnp.where(across == 0, 2, 0)
    last = jnp.where(across == 31, 4, 6)
    place = jnp.where((row >= first) & (row < last), row - (cell & 3), -9)
    weights, moments = spline(frac)
    hits = [place == k for k in range(3)]
    return pick(hits, weights), pick(hits, moments)


def by_channel(parts):
    row = lax.broadcasted_iota(jnp.int32, (8, 128), 0)
    out = jnp.where(row < 6, parts[2], parts[3])
    out = jnp.where(row < 4, parts[1], out)
    return jnp.where(row < 2, parts[0], out)


def dot(left, right, dims):
    return lax.dot_general(left, right, (dims, ((), ())), preferred_element_type=F32)


NN = ((1,), (0,))
NT = ((1,), (1,))


def contact(mass, momentum, kind, friction, bvel):
    floor = jnp.maximum(mass, MASS_FLOOR)
    speed = [momentum[0] / floor + DT * GRAVITY, momentum[1] / floor, momentum[2] / floor]
    coeff = jnp.where(friction == 3.0, FRICTION[3], 0.0)
    for level in range(3):
        coeff = jnp.where(friction == float(level), FRICTION[level], coeff)
    rel = [speed[i] - bvel[i] for i in range(3)]
    normal = jnp.minimum(rel[0], 0.0)
    slide = jnp.sqrt(rel[1] * rel[1] + rel[2] * rel[2])
    factor = jnp.maximum(0.0, 1.0 + coeff * normal / jnp.maximum(slide, SLIP_FLOOR))
    hit = [bvel[0] + (rel[0] - normal), bvel[1] + factor * rel[1], bvel[2] + factor * rel[2]]
    return [
        jnp.where(kind == 2.0, bvel[i], jnp.where(kind == 1.0, hit[i], speed[i])) for i in range(3)
    ]


def particle(b, tile_ref, live_ref, cells_ref, offsets_ref):
    lanes = pl.ds(b * 128 if isinstance(b, int) else pl.multiple_of(b * 128, 128), 128)

    def row(ref, r):
        return jnp.broadcast_to(ref[pl.ds(r, 1), lanes], (8, 128))

    cell = jnp.broadcast_to(cells_ref[pl.ds(b, 1), :], (8, 128))
    frac = [row(offsets_ref, r) for r in range(3)]
    alive = jnp.where(b < live_ref[0], 1.0, 0.0)
    tile = tile_ref[b]
    return lanes, row, cell, frac, alive, lax.shift_right_logical(tile, 5) & 3, tile & 31


def place_of(down, across):
    return (32 * down + 4 * across + 127) & 127


def weights_xy(cell, frac, across):
    weights, moments = spline(frac[1])
    wx, wx_moment = six(near_x(cell), weights, moments)
    wy, wy_moment = along_y(cell, frac[2], across)
    value = jnp.concatenate(
        [
            jnp.concatenate([wx[i] * wy for i in range(6)], 0),
            jnp.concatenate([wx_moment[i] * wy for i in range(6)], 0),
            jnp.concatenate([wx[i] * wy_moment for i in range(6)], 0),
        ],
        1,
    )
    high, low = split(value)
    pad = jnp.zeros((16, 384), BF16)
    return jnp.concatenate([high, pad, low, pad], 0)


def edge_row(z):
    return 60 * (z % 2) + STEP * (z // 2)


def spread(
    tile_hbm,
    live_hbm,
    bvel_hbm,
    cells_hbm,
    offsets_hbm,
    velocity_hbm,
    affine_hbm,
    stress_hbm,
    mass_hbm,
    mask_hbm,
    friction_hbm,
    tile_ref,
    live_ref,
    cells_ref,
    offsets_ref,
    out_velocity,
    out_affine,
    out_offsets,
    edge_speed,
    listed,
    bvel_ref,
    velocity_ref,
    affine_ref,
    stress_ref,
    mass_ref,
    mask_ref,
    friction_ref,
    weights,
    patch,
    grid,
    across_x,
    speed,
    ends,
    ends_z,
    classes,
    planes,
    got_z,
    got_x,
    got_zx,
    got_ends,
    load_sem,
    send_sem,
    recv_sem,
):
    loads = [
        pltpu.make_async_copy(source, target, load_sem.at[index])
        for index, (source, target) in enumerate(
            (
                (cells_hbm, cells_ref),
                (offsets_hbm, offsets_ref),
                (tile_hbm, tile_ref),
                (live_hbm, live_ref),
                (mass_hbm, mass_ref),
                (velocity_hbm, velocity_ref),
                (affine_hbm, affine_ref),
                (stress_hbm, stress_ref),
                (mask_hbm, mask_ref),
                (friction_hbm, friction_ref),
                (bvel_hbm, bvel_ref),
            )
        )
    ]
    ix, iy, iz = lax.axis_index("gx"), lax.axis_index("gy"), lax.axis_index("gz")
    nx, ny, nz = lax.axis_size("gx"), lax.axis_size("gy"), lax.axis_size("gz")
    above, below = iz < nz - 1, iz > 0

    def beside_of(i, n):
        return {-1: jnp.where(i == 0, n - 1, i - 1), 0: i, 1: jnp.where(i == n - 1, 0, i + 1)}

    at_x, at_y, at_z = beside_of(ix, nx), beside_of(iy, ny), beside_of(iz, nz)

    def device(dz, dx, dy):
        return {"gx": at_x[dx], "gy": at_y[dy], "gz": at_z[dz]}

    def where_z(dz, action):
        if dz == 0:
            action()
        else:
            pl.when(above if dz == 1 else below)(action)

    barrier = pltpu.get_barrier_semaphore()

    def greet(dz, dys):
        for dy in dys:
            for dx in (-1, 1, 0):
                if (dz, dx, dy) != (0, 0, 0):
                    pl.semaphore_signal(
                        barrier, inc=1, device_id=device(dz, dx, dy), device_id_type=MESH
                    )

    for dz in (1, 0, -1):
        where_z(dz, lambda dz=dz: greet(dz, (1,)))
    for load in loads:
        load.start()
    for dz in (1, 0, -1):
        where_z(dz, lambda dz=dz: greet(dz, (-1, 0)))

    counter = iter(range(26))

    def sender(src, dst, dz, dx, dy):
        slot = next(counter)
        return pltpu.make_async_remote_copy(
            src_ref=src,
            dst_ref=dst,
            send_sem=send_sem.at[slot],
            recv_sem=recv_sem.at[slot],
            device_id=device(dz, dx, dy),
            device_id_type=MESH,
        )

    grid_sends, end_sends = {}, {}
    for dz, dx in FACES:
        if dz == 0:
            side = (1 + dx) // 2
            src, dst = across_x.at[side], got_x.at[side]
        elif dx == 0:
            src = grid.at[Z_PAIR[dz], pl.ds(PLANE, EDGE_B)]
            dst = got_z.at[(1 + dz) // 2]
        else:
            src = grid.at[Z_PAIR[dz], pl.ds(LEFT if dx == -1 else EDGE_B - 2, 4)]
            dst = got_zx.at[1 + dz + (1 + dx) // 2]
        grid_sends[-dz, -dx] = sender(src, dst, dz, dx, 0)
    for dz, dx in NINE:
        for dy in (-1, 1):
            side = (1 + dy) // 2
            if dz == 0:
                src, dst = ends.at[side], got_ends.at[side, SLOT[dz, dx]]
            else:
                src = ends_z.at[(1 + dz) // 2, side]
                dst = got_ends.at[side, SLOT[dz, dx], 0]
            end_sends[-dz, -dx, -dy] = sender(src, dst, dz, dx, dy)

    speed[...] = jnp.zeros((4, XN, 8, 128), F32)
    classes[...] = jnp.zeros((2, 128, 128), F32)
    patch[pl.ds(0, 12)] = jnp.zeros((12, 3, 8, 128), F32)

    def clear(b, carry):
        patch[pl.ds(STEP * b + 18, 14)] = jnp.zeros((14, 3, 8, 128), F32)
        return carry

    lax.fori_loop(0, BLOCKS, clear, 0)
    for load in loads:
        load.wait()

    zero = jnp.zeros((8, 128), F32)
    lane = lax.broadcasted_iota(jnp.int32, (8, 128), 1)

    flipped = []
    for kind, source in enumerate((mask_ref, friction_ref)):
        for z in range(4):
            value = source[z].astype(F32)
            classes[kind, pl.ds(edge_row(z + 1) + 1, 16), :] = value
            planes[kind, z] = pltpu.roll(value, 8, 1, stride=8, stride_axis=0)
        flipped.append(classes[kind].T)
        for z in range(4):
            classes[kind, pl.ds(edge_row(z + 1) + 1, 16), :] = planes[kind, z]
    flat = planes.reshape(128, 128)
    sides = [flat[pl.ds(0, 8, stride=16), :], flat[pl.ds(15, 8, stride=16), :]]

    def scatter(b, edges):
        lanes, row, cell, frac, alive, down, across = particle(
            b, tile_ref, live_ref, cells_ref, offsets_ref
        )
        right = weights_xy(cell, frac, across)
        weights[b] = right
        wz, wz_moment = along_z(cell, frac[0])
        mass = jnp.broadcast_to(mass_ref[pl.ds(b, 1), :], (8, 128)) * alive
        push = by_channel([mass] + [mass * row(velocity_ref, i) for i in range(3)])
        scale = 4.0 * DT * alive

        def twist(j):
            return mass * by_channel(
                [zero] + [row(affine_ref, 3 * i + j) for i in range(3)]
            ) - scale * by_channel([zero] + [row(stress_ref, 3 * i + j) for i in range(3)])

        twists = [twist(j) for j in range(3)]
        left = jnp.concatenate(
            [
                jnp.concatenate([wz[p] * push + wz_moment[p] * twists[0] for p in range(3)], 0),
                jnp.concatenate([wz[p] * twists[1] for p in range(3)], 0),
                jnp.concatenate([wz[p] * twists[2] for p in range(3)], 0),
            ],
            1,
        )
        found = dot(jnp.concatenate(split(left), 0), right, NT)
        found = found[:24] + found[24:]
        start = place_of(down, across)
        group = lax.shift_right_logical((lane - start) & 127, 3)
        for pair in range(3):
            part = found[8 * pair : 8 * pair + 8]
            part = jnp.where(lane < 48, part + pltpu.roll(part, 64, 1), 0.0)
            part = pltpu.roll(part, start, 1)
            for i in range(6):
                patch[STEP * b + 12 + i, pair] = jnp.where(group == i, part, 0.0)

        we, we_moment = along_edge(cell, frac[2], across)
        lead = we * push + we_moment * twists[2]
        second = we * twists[0]
        third = we * twists[1]
        wz, wz_moment = six(near_z(cell), *spline(frac[0]))
        plain = [wz[z] * lead + wz_moment[z] * second for z in range(6)]
        moment = [wz[z] * third for z in range(6)]
        left = jnp.concatenate([jnp.concatenate(plain, 0), jnp.concatenate(moment, 0)], 1)
        across_x = along_x_rows(cell, frac[1])
        across_high = across_x.astype(BF16).astype(F32)
        pad = jnp.zeros((56, 256), F32)
        right = jnp.concatenate([across_high, pad, across_x - across_high, pad], 0).astype(BF16)
        found = dot(jnp.concatenate(split(left), 0), right, NT)
        found = found[:48] + found[48:]
        low = jnp.where(across == 0, 1.0, 0.0)
        high = jnp.where(across == 31, 1.0, 0.0)
        out = []
        for z in range(6):
            part = pltpu.roll(found[8 * z : 8 * z + 8], 4 * down, 1)
            out.append(edges[2 * z] + low * part)
            out.append(edges[2 * z + 1] + high * part)
        return tuple(out)

    edges = (zero,) * 12
    for b in range(BLOCKS):
        edges = scatter(b, edges)

    half = jnp.where(lane >= 60, lane - 60, lane)
    pair_of = jnp.where(half >= 2 * STEP, 2, jnp.where(half >= STEP, 1, 0))
    place = half - STEP * pair_of

    for side in range(2):
        total = zero
        for z in range(6):
            part = edges[2 * z + side]
            part = jnp.where(lane < XN, part + pltpu.roll(part, 64, 1), 0.0)
            if edge_row(z):
                part = pltpu.roll(part, edge_row(z), 1)
            total = total + part
        ends[side, 0] = total

    tail = jnp.zeros((6, 128), F32)
    for side, y in ((0, 0), (1, 127)):
        ends[side, 1] = jnp.concatenate([flipped[0][y : y + 1], flipped[1][y : y + 1], tail], 0)

    for dz in (-1, 1):
        pair = Z_PAIR[dz]
        grid[pair, pl.ds(PLANE, 4)] = planes[:, Z_PLANE[dz]].reshape(4, 8, 128)
        grid[pair, LEFT] = sides[0]
        grid[pair, RIGHT] = sides[1]
        here = pair_of == pair
        shift = (-STEP * dz) % 128

        def beside(first, second):
            moved = pltpu.roll(jnp.where(here, second, 0.0), shift, 1)
            return jnp.where(here, first, 0.0) + moved

        both = beside(ends[0, 0], ends[1, 0])
        grid[pair, EDGE_A] = both
        grid[pair, EDGE_B] = both
        for side in range(2):
            ends_z[(1 + dz) // 2, side] = beside(ends[side, 0], ends[side, 1])
    for side in range(2):
        across_x[side, 6] = ends[0, 0]
        across_x[side, 7] = ends[1, 0]
        across_x[side, 8] = sides[side]

    for pair in range(3):
        total = jnp.zeros((XN, 8, 128), F32)
        for b in range(BLOCKS):
            down = lax.shift_right_logical(tile_ref[b], 5) & 3
            total = total + patch[pl.ds(STEP * b + 12 - 4 * down, XN), pair]
        grid[pair, pl.ds(FIRST, XN)] = total
        speed[pair] = total
        across_x[0, pl.ds(2 * pair, 2)] = total[:2]
        across_x[1, pl.ds(2 * pair, 2)] = total[16:]

    pl.semaphore_wait(
        barrier, 26 - 9 * (1 - above.astype(jnp.int32)) - 9 * (1 - below.astype(jnp.int32))
    )
    def send_ends(dy):
        for dz in (1, -1, 0):

            def start(dz=dz):
                for dx in (1, -1, 0):
                    end_sends[-dz, -dx, -dy].start()

            where_z(dz, start)

    send_ends(1)
    send_ends(-1)
    for dz in (1, -1, 0):

        def start(dz=dz):
            for dx in (1, -1, 0):
                if (dz, dx) != (0, 0):
                    grid_sends[-dz, -dx].start()

        where_z(dz, start)
    count = jnp.int32(0)
    order = []
    for b in range(BLOCKS):
        across = tile_ref[b] & 31
        touches = jnp.where((across == 0) | (across == 31), 1, 0)
        order.append((touches, count))
        count = count + touches
    listed[0] = count
    for k in range(BLOCKS):
        at = jnp.int32(0)
        for b in range(k, BLOCKS):
            touches, before = order[b]
            at = at + jnp.where(before == k, b * touches, 0)
        listed[k + 1] = at

    for dz in (0, 1, -1):

        def wait(dz=dz):
            for dx in (-1, 0, 1):
                if (dz, dx) != (0, 0):
                    grid_sends[dz, dx].wait_recv()

        where_z(dz, wait)
    there = {-1: below, 1: above}
    for dx in (-1, 1):
        came = got_x.at[(1 - dx) // 2]
        xs = pl.ds(8 + 8 * dx, 2)
        speed[pl.ds(0, 3), xs] = speed[pl.ds(0, 3), xs] + came[pl.ds(0, 6)].reshape(3, 2, 8, 128)
    for dz in (-1, 1):
        pair = Z_PAIR[dz]
        came = got_z[(1 - dz) // 2, pl.ds(FIRST, XN)]
        parts = [got_zx[1 - dz + (1 - dx) // 2, pl.ds(0 if dx == -1 else 2, 2)] for dx in (-1, 1)]
        came = jnp.concatenate(
            [came[:2] + parts[0], came[2:16], came[16:] + parts[1]], 0
        )
        speed[pair] = speed[pair] + jnp.where(there[dz], came, 0.0)
    for kind in range(2):
        for dx, x, mark in ((-1, 0, 3), (1, 17, 0)):
            for z in range(4):
                classes[kind, pl.ds(edge_row(z + 1) + x, 1), :] = got_x[
                    (1 - dx) // 2, 8, pl.ds(4 * kind + z, 1), :
                ]
            for dz in (-1, 1):
                classes[kind, pl.ds(edge_row(0 if dz == -1 else 5) + x, 1), :] = got_zx[
                    1 - dz + (1 - dx) // 2, mark, pl.ds(4 * kind + Z_PLANE[-dz], 1), :
                ]
        for dz in (-1, 1):
            classes[kind, pl.ds(edge_row(0 if dz == -1 else 5) + 1, 16), :] = got_z[
                (1 - dz) // 2, pl.ds(PLANE + 2 * kind, 2)
            ].reshape(16, 128)

    columns = []
    for kind in range(2):
        flipped = classes[kind].T
        for y in (0, 127):
            value = jnp.zeros((1, 128), F32)
            for x in range(16):
                at = (y + 8 * x) & 127
                value = jnp.where((place[:1] & 15) == x, flipped[at : at + 1], value)
            columns.append(value)
    bvel = [bvel_ref[i] for i in range(3)]
    rows = speed.reshape(4 * XN * 8, 128)
    for z in range(6):
        pair, low = z // 2, z % 2

        def at(c):
            return pl.ds(pair * XN * 8 + 2 * c + low, XN, stride=8)

        load = [rows[at(c), :] for c in range(4)]
        kinds = [classes[kind, pl.ds(edge_row(z), XN), :] for kind in range(2)]
        new = contact(load[0], load[1:], kinds[0], kinds[1], bvel)
        for i in range(3):
            value = new[i]
            if z == 0:
                value = jnp.where(below, value, 0.0)
            elif z == 5:
                value = jnp.where(above, value, 0.0)
            rows[at(i + 1), :] = value

    def gather(b):
        lanes, row, cell, frac, alive, down, across = particle(
            b, tile_ref, live_ref, cells_ref, offsets_ref
        )
        start = place_of(down, across)
        group = lax.shift_right_logical((lane - start) & 127, 3)
        back = (128 - start) & 127
        high, low = [], []
        for pair in range(3):
            value = speed[pair, pl.ds(4 * down, 6)]
            part = value[5]
            for i in range(5):
                part = jnp.where(group == i, value[i], part)
            part = jnp.where(lane < 48, pltpu.roll(part, back, 1), 0.0)
            rounded = part.astype(BF16).astype(F32)
            high.append(rounded + pltpu.roll(rounded, 64, 1))
            low.append(part - rounded)
        found = dot(jnp.concatenate(high + low, 0).astype(BF16), weights[b], NN)
        found = found[:24] + found[24:]
        wz, wz_moment = along_z(cell, frac[0])
        totals = [zero] * 4
        for pair in range(3):
            rows_of = slice(8 * pair, 8 * pair + 8)
            plain = found[rows_of, :128]
            totals[0] = totals[0] + wz[pair] * plain
            totals[1] = totals[1] + wz_moment[pair] * plain
            totals[2] = totals[2] + wz[pair] * found[rows_of, 128:256]
            totals[3] = totals[3] + wz[pair] * found[rows_of, 256:]
        totals = [(t + pltpu.roll(t, 7, 0)) * alive for t in totals]
        for i in range(3):
            here = 2 * i + 2
            moved = totals[0][here : here + 1]
            out_velocity[pl.ds(i, 1), lanes] = moved
            out_offsets[pl.ds(i, 1), lanes] = frac[i][:1] * alive + DT * moved
            for j in range(3):
                out_affine[pl.ds(3 * i + j, 1), lanes] = 4.0 * totals[j + 1][here : here + 1]

    for b in range(BLOCKS):
        gather(b)

    inner = lane < 120
    for dz in (0, 1, -1):

        def wait(dz=dz):
            for dx in (-1, 0, 1):
                for dy in (-1, 1):
                    end_sends[dz, dx, dy].wait_recv()

        where_z(dz, wait)
    totals = [ends[0, 0], ends[1, 0]]
    marks = [zero, zero]
    for dz, dx in NINE:
        keep = inner
        if dx == -1:
            keep = keep & (place < 2)
        elif dx == 1:
            keep = keep & (place >= 16) & (place < 18)
        if dz == -1:
            keep = keep & (pair_of == 0) & below
        elif dz == 1:
            keep = keep & (pair_of == 2) & above
        shift = 16 * dx + 2 * STEP * dz

        def moved(value, second=False):
            shift_by = (shift - STEP * dz if second else shift) % 128
            return jnp.where(keep, pltpu.roll(value, shift_by, 1) if shift_by else value, 0.0)

        if dz:
            if dx == 0:
                came = got_z[(1 - dz) // 2, EDGE_A]
            else:
                came = got_zx[1 - dz + (1 - dx) // 2, 2 if dx == -1 else 1]
            totals[0] = totals[0] + moved(came)
            totals[1] = totals[1] + moved(came, True)
        elif dx:
            for side in range(2):
                totals[side] = totals[side] + moved(got_x[(1 - dx) // 2, 6 + side])
        for dy in (-1, 1):
            side = (1 + dy) // 2
            came = got_ends.at[1 - side, SLOT[-dz, -dx]]
            totals[side] = totals[side] + moved(came[0])
            marks[side] = marks[side] + (moved(came[0], True) if dz else moved(came[1]))
    kinds = [
        jnp.concatenate(
            [
                marks[0][kind : kind + 1],
                columns[2 * kind],
                columns[2 * kind + 1],
                marks[1][kind : kind + 1],
            ],
            0,
        )
        for kind in range(2)
    ]
    parts = [
        jnp.concatenate([totals[0][2 * c : 2 * c + 2], totals[1][2 * c : 2 * c + 2]], 0)
        for c in range(4)
    ]
    new = contact(parts[0], parts[1:], kinds[0], kinds[1], bvel)
    first_row, last_row = edge_row(0), edge_row(5)
    here = lane[:4]
    outside = ((here < first_row + STEP) & (iz == 0)) | ((here >= last_row) & (iz == nz - 1))
    new = [jnp.where(outside, 0.0, value) for value in new]
    for side in range(2):
        edge_speed[side] = jnp.concatenate(
            [jnp.zeros((2, 128), F32)] + [value[2 * side : 2 * side + 2] for value in new], 0
        )

    for dz in (-1, 0, 1):

        def finish(dz=dz):
            for dx in (-1, 0, 1):
                if (dz, dx) != (0, 0):
                    grid_sends[-dz, -dx].wait_send()
                for dy in (-1, 1):
                    end_sends[-dz, -dx, -dy].wait_send()

        where_z(dz, finish)


def finish(
    tile_ref,
    live_ref,
    cells_ref,
    offsets_ref,
    velocity_ref,
    affine_ref,
    moved_ref,
    edge_speed,
    listed,
    out_velocity,
    out_affine,
    out_offsets,
):
    out_velocity[...] = velocity_ref[...]
    out_affine[...] = affine_ref[...]
    out_offsets[...] = moved_ref[...]

    def share(k):
        b = listed[k + 1]
        lanes, row, cell, frac, alive, down, across = particle(
            b, tile_ref, live_ref, cells_ref, offsets_ref
        )
        side = jnp.where(across == 0, 0, 1)
        value = edge_speed[side]
        left = jnp.concatenate(
            [pltpu.roll(value, (128 - edge_row(z) - 4 * down) & 127, 1) for z in range(6)], 0
        )
        left_high, left_low = split(left)
        right = jnp.concatenate(
            [along_x_rows(cell, frac[1]), jnp.zeros((120, 256), F32)], 0
        )
        right_high, right_low = split(right)
        found = dot(left_high, right_high, NN) + (
            dot(left_low, right_high, NN) + dot(left_high, right_low, NN)
        )
        we, we_moment = along_edge(cell, frac[2], across)
        wz, wz_moment = six(near_z(cell), *spline(frac[0]))
        sum_w = sum(wz[z] * found[8 * z : 8 * z + 8, :128] for z in range(6))
        sum_z = sum(wz_moment[z] * found[8 * z : 8 * z + 8, :128] for z in range(6))
        sum_x = sum(wz[z] * found[8 * z : 8 * z + 8, 128:] for z in range(6))
        totals = [we * sum_w, we * sum_z, we * sum_x, we_moment * sum_w]
        used = jnp.where(k < listed[0], alive, 0.0)
        return lanes, [(t + pltpu.roll(t, 7, 0)) * used for t in totals]

    def two(step, carry):
        for lanes, totals in [share(2 * step + u) for u in range(2)]:
            for i in range(3):
                here = 2 * i + 2
                moved = totals[0][here : here + 1]
                out_velocity[pl.ds(i, 1), lanes] += moved
                out_offsets[pl.ds(i, 1), lanes] += DT * moved
                for j in range(3):
                    out_affine[pl.ds(3 * i + j, 1), lanes] += (
                        4.0 * totals[j + 1][here : here + 1]
                    )
        return carry

    lax.fori_loop(0, lax.shift_right_logical(listed[0] + 1, 1), two, 0)


def on_device(
    cells,
    offsets,
    velocity,
    affine,
    stress,
    mass,
    block_tile,
    live_blocks,
    bucket_mask,
    friction_class,
    bucket_velocity,
):
    hbm = pl.BlockSpec(memory_space=pltpu.HBM)
    vmem = pl.BlockSpec(memory_space=pltpu.VMEM)
    smem = pl.BlockSpec(memory_space=pltpu.SMEM)
    count = cells.shape[0]
    args = (
        block_tile,
        live_blocks,
        bucket_velocity,
        cells.reshape(BLOCKS, 128),
        offsets,
        velocity,
        affine,
        stress,
        mass.reshape(BLOCKS, 128),
        bucket_mask,
        friction_class,
    )
    kept = pl.pallas_call(
        spread,
        out_shape=(
            pltpu.SMEM((BLOCKS,), jnp.int32),
            pltpu.SMEM((1,), jnp.int32),
            pltpu.VMEM((BLOCKS, 128), jnp.int32),
            pltpu.VMEM((3, count), F32),
            pltpu.VMEM((3, count), F32),
            pltpu.VMEM((9, count), F32),
            pltpu.VMEM((3, count), F32),
            pltpu.VMEM((2, 8, 128), F32),
            pltpu.SMEM((BLOCKS + 1,), jnp.int32),
        ),
        in_specs=[hbm] * len(args),
        out_specs=(smem,) * 2 + (vmem,) * 6 + (smem,),
        scratch_shapes=[pltpu.SMEM((3,), F32)]
        + [pltpu.VMEM(arg.shape, arg.dtype) for arg in args[5:]]
        + [
            pltpu.VMEM((BLOCKS, 128, 384), BF16),
            pltpu.VMEM((STEP * BLOCKS + 12, 3, 8, 128), F32),
            pltpu.VMEM((3, TILES, 8, 128), F32),
            pltpu.VMEM((2, 9, 8, 128), F32),
            pltpu.VMEM((4, XN, 8, 128), F32),
            pltpu.VMEM((2, 2, 8, 128), F32),
            pltpu.VMEM((2, 2, 8, 128), F32),
            pltpu.VMEM((2, 128, 128), F32),
            pltpu.VMEM((2, 4, 16, 128), F32),
            pltpu.VMEM((2, EDGE_B, 8, 128), F32),
            pltpu.VMEM((2, 9, 8, 128), F32),
            pltpu.VMEM((4, 4, 8, 128), F32),
            pltpu.VMEM((2, len(NINE), 2, 8, 128), F32),
            pltpu.SemaphoreType.DMA((len(args),)),
            pltpu.SemaphoreType.DMA((26,)),
            pltpu.SemaphoreType.DMA((26,)),
        ],
        compiler_params=pltpu.CompilerParams(
            collective_id=0, has_side_effects=True, vmem_limit_bytes=VMEM_SPREAD
        ),
    )(*args)
    return pl.pallas_call(
        finish,
        out_shape=(
            jax.ShapeDtypeStruct((3, count), F32),
            jax.ShapeDtypeStruct((9, count), F32),
            jax.ShapeDtypeStruct((3, count), F32),
        ),
        in_specs=[smem] * 2 + [vmem] * 6 + [smem],
        out_specs=(vmem,) * 3,
        compiler_params=pltpu.CompilerParams(vmem_limit_bytes=VMEM_FINISH),
    )(*kept)


def solution(mesh):
    along = ("gx", "gy", "gz")
    return jax.shard_map(
        on_device,
        mesh=mesh,
        in_specs=(
            P(along),
            P(None, along),
            P(None, along),
            P(None, along),
            P(None, along),
            P(along),
            P(along),
            P(along),
            P("gz", "gx", "gy"),
            P("gz", "gx", "gy"),
            P(),
        ),
        out_specs=(P(None, along), P(None, along), P(None, along)),
        check_vma=False,
    )
```
